32 devices in a mesh: grp: 1, tm: 16 (over z, y, core), space: 2 (over x).
Axes of the slice: x: 2, y: 2, z: 4, core: 2. Of those that a mesh axis runs over, the one named last changes fastest.
Arguments:
- tokens: bfloat16 [256, 32, 1152], P('space', ('grp', 'tm')), may hold values from -6 to 6
- modulation: float32 [6, 1152], P('grp'), may hold values from -3 to 3
- qkv_spatial: bfloat16 [1152, 1728], P(None, 'space'), may hold values from -6 to 6
- bias_spatial: float32 [1728], P('space'), may hold values from -3 to 3
- out_spatial: bfloat16 [576, 1152], P('space'), may hold values from -0.25 to 0.25
- outbias_spatial: float32 [1152], replicated, may hold values from -3 to 3
- qkv_temporal: bfloat16 [1152, 1728], P(None, 'space'), may hold values from -6 to 6
- bias_temporal: float32 [1728], P('space'), may hold values from -3 to 3
- out_temporal: bfloat16 [576, 1152], replicated, may hold values from -0.25 to 0.25
- outbias_temporal: float32 [1152], replicated, may hold values from -3 to 3
Outputs:
- result: bfloat16 [256, 32, 1152], P('space', ('grp', 'tm'))
The draws below stay inside these ranges and needn't reach their ends.
All inputs are finite; a program needn't handle non-finite values.
Results may differ from the reference program's by a relative error of at most 0.025.
Values may be sent and summed in bfloat16 or wider, within the bound.
No kernel may reach another device: no remote copies, remote signals or barrier semaphores. Data moves between devices by JAX's collectives and lax.ppermute only.
A program may use at most 64 MiB of HBM per device.

```python
import jax
import jax.numpy as jnp
from jax import lax

D = 1152
HEADS = 8
HD = 72
WIN = 16
FRAMES = 32
PATCHES = 256
N_SPACE = 2


def drawn_projection(key):
    base = jnp.clip(jax.random.normal(jax.random.fold_in(key, 1), (D, HEADS, 3, HD), jnp.float32), -6.0, 6.0) * D ** (-0.5)
    return jnp.clip(base, -6.0, 6.0).reshape(D, 3 * HD * HEADS)


def draw_qkv_spatial(key, part):
    return drawn_projection(jax.random.fold_in(key, 101)).astype(jnp.bfloat16)


def draw_qkv_temporal(key, part):
    return drawn_projection(jax.random.fold_in(key, 202)).astype(jnp.bfloat16)


def draw_tokens(key, part):
    own_key = jax.random.fold_in(key, 303)
    shape = (PATCHES, FRAMES, D)
    base = jnp.clip(jax.random.normal(jax.random.fold_in(own_key, 1), shape, jnp.float32), -6.0, 6.0)
    return jnp.clip(base, -6.0, 6.0).astype(jnp.bfloat16)


def steps_of(stream_key, shape, split, low, largest):
    level, own = 1.0, jax.random.fold_in(stream_key, 6)
    for position, shards_of in split:
        draws = jnp.exp(jax.random.uniform(jax.random.fold_in(own, position), (shards_of,), jnp.float32, low / len(split), largest / len(split)))
        level = level * jnp.repeat(draws, shape[position] // shards_of).reshape([-1 if axis == position else 1 for axis in range(len(shape))])
    return level


def scatter_about(stream_key, extent, deviation, limit, split=(), kind=jnp.bfloat16):
    values = deviation * jax.random.normal(stream_key, extent, jnp.float32)
    if split:
        values = values * steps_of(stream_key, extent, split, -0.22, 0.18)
    return jnp.clip(values, -limit, limit).astype(kind)


def setup_inputs(seed: int = 0, part: int = 0) -> dict:
    streams_of = jax.random.split(jax.random.key(seed), 11)
    own_keys = jax.random.split(jax.random.fold_in(streams_of[10], part), 11)
    return {
        "tokens": draw_tokens(jax.random.fold_in(jax.random.fold_in(streams_of[10], part), 71), part),
        "modulation": scatter_about(own_keys[1], (6, D), 0.5, 3.0, (), jnp.float32),
        "qkv_spatial": draw_qkv_spatial(jax.random.fold_in(streams_of[10], 71), part),
        "bias_spatial": scatter_about(streams_of[3], (3 * HD * HEADS,), 0.5, 3.0, ((0, 2),), jnp.float32),
        "out_spatial": scatter_about(streams_of[4], (HEADS * HD, D), (HEADS * HD) ** -0.5, 0.25, ((0, 2),)),
        "outbias_spatial": scatter_about(streams_of[5], (D,), 0.5, 3.0, (), jnp.float32),
        "qkv_temporal": draw_qkv_temporal(jax.random.fold_in(streams_of[10], 71), part),
        "bias_temporal": scatter_about(streams_of[7], (3 * HD * HEADS,), 0.5, 3.0, ((0, 2),), jnp.float32),
        "out_temporal": scatter_about(streams_of[8], (HEADS * HD, D), (HEADS * HD) ** -0.5, 0.25),
        "outbias_temporal": scatter_about(streams_of[9], (D,), 0.5, 3.0, (), jnp.float32),
    }


def modulated(values, offset_vec, scaling):
    center = lax.optimization_barrier(jnp.mean(values, axis=-1, keepdims=True))
    spread = lax.optimization_barrier(jnp.mean((values - center) ** 2, axis=-1, keepdims=True))
    normed = (values - center) / jnp.sqrt(spread + 1e-06)
    return normed * (1.0 + scaling) + offset_vec

def project(rows, weights, biases):
    flat = rows.reshape(PATCHES * FRAMES, D)
    mixed = jnp.dot(flat, weights, preferred_element_type=jnp.float32) + biases
    return mixed.astype(jnp.bfloat16).reshape(PATCHES, FRAMES, HEADS, 3, HD)

def frame_attention(operands):
    queries, keys_in, values_in = operands
    scores = jnp.einsum('phe,qhe->hpq', queries.astype(jnp.float32), keys_in.astype(jnp.float32)) / jnp.sqrt(jnp.float32(HD))
    highest = lax.optimization_barrier(jnp.max(scores, axis=-1, keepdims=True))
    expon = jnp.exp(scores - highest)
    probs = (expon / lax.optimization_barrier(jnp.sum(expon, axis=-1, keepdims=True))).astype(jnp.bfloat16)
    return jnp.einsum('hpq,qhe->phe', probs.astype(jnp.float32), values_in.astype(jnp.float32)).astype(jnp.bfloat16)

def reference(tokens, modulation, qkv_spatial, bias_spatial, out_spatial, outbias_spatial, qkv_temporal, bias_temporal, out_temporal, outbias_temporal):
    tokens_f = tokens.astype(jnp.float32)
    h_spatial = modulated(tokens_f, modulation[0], modulation[1]).astype(jnp.bfloat16)
    grouped = project(h_spatial, qkv_spatial, bias_spatial)
    by_frame = jnp.transpose(grouped, (1, 0, 2, 3, 4))
    o_frames = lax.map(frame_attention, (by_frame[:, :, :, 0], by_frame[:, :, :, 1], by_frame[:, :, :, 2]))
    o_spatial = jnp.transpose(o_frames, (1, 0, 2, 3)).reshape(PATCHES * FRAMES, HEADS * HD)
    group_cols = HEADS // N_SPACE * HD
    total = jnp.zeros((PATCHES * FRAMES, D), jnp.float32)
    for group in range(N_SPACE):
        part = jnp.dot(o_spatial[:, group * group_cols:(group + 1) * group_cols], out_spatial[group * group_cols:(group + 1) * group_cols], preferred_element_type=jnp.float32)
        total = total + part.astype(jnp.bfloat16).astype(jnp.float32)
    total = total.reshape(PATCHES, FRAMES, D)
    mid_rows = (tokens_f + modulation[2] * (total + outbias_spatial)).astype(jnp.bfloat16)
    h_temporal = modulated(mid_rows.astype(jnp.float32), modulation[3], modulation[4]).astype(jnp.bfloat16)
    grouped_t = project(h_temporal, qkv_temporal, bias_temporal)
    queries = grouped_t[:, :, :, 0].astype(jnp.float32)
    padded_k = jnp.pad(grouped_t[:, :, :, 1].astype(jnp.float32), ((0, 0), (WIN - 1, 0), (0, 0), (0, 0)))
    padded_v = jnp.pad(grouped_t[:, :, :, 2].astype(jnp.float32), ((0, 0), (WIN - 1, 0), (0, 0), (0, 0)))
    frame_ids = jnp.arange(FRAMES, dtype=jnp.int32)
    score_list = []
    for offset in range(WIN):
        shifted = padded_k[:, WIN - 1 - offset:WIN - 1 - offset + FRAMES]
        raw = lax.optimization_barrier(jnp.sum(queries * shifted, axis=-1)) / jnp.sqrt(jnp.float32(HD))
        valid = (frame_ids >= offset)[None, :, None]
        score_list.append(jnp.where(valid, raw, jnp.float32(-1e+30)))
    scores = jnp.stack(score_list, axis=-1)
    highest = lax.optimization_barrier(jnp.max(scores, axis=-1, keepdims=True))
    expon = jnp.exp(scores - highest)
    probs = (expon / lax.optimization_barrier(jnp.sum(expon, axis=-1, keepdims=True))).astype(jnp.bfloat16).astype(jnp.float32)
    o_temporal = jnp.zeros((PATCHES, FRAMES, HEADS, HD), jnp.float32)
    for offset in range(WIN):
        shifted = padded_v[:, WIN - 1 - offset:WIN - 1 - offset + FRAMES]
        o_temporal = o_temporal + probs[..., offset][..., None] * shifted
    o_flat = o_temporal.astype(jnp.bfloat16).reshape(PATCHES * FRAMES, HEADS * HD)
    final = jnp.dot(o_flat, out_temporal, preferred_element_type=jnp.float32).reshape(PATCHES, FRAMES, D)
    return (mid_rows.astype(jnp.float32) + modulation[5] * (final + outbias_temporal)).astype(jnp.bfloat16)
```

```python
import functools
import math

import jax
import jax.numpy as jnp
from jax import lax
from jax.experimental import pallas as pl
from jax.experimental.pallas import tpu as pltpu
from jax.sharding import PartitionSpec as P

HD = 72
WIN = 16
BF = jnp.bfloat16
F32 = jnp.float32
EXP2_SCALE = 1.0 / (math.sqrt(HD) * math.log(2.0))

VMEM = pl.BlockSpec(memory_space=pltpu.VMEM)
SMEM = pl.BlockSpec(memory_space=pltpu.SMEM)
PARAMS = pltpu.CompilerParams(vmem_limit_bytes=48 * 1024 * 1024)

NT = (((1,), (1,)), ((), ()))
TN = (((0,), (0,)), ((), ()))


def mm(a, b, dims=(((1,), (0,)), ((), ()))):
    return lax.dot_general(a, b, dims, preferred_element_type=F32)


def modulated(values, offset_vec, scaling):
    center = jnp.mean(values, axis=-1, keepdims=True)
    moved = values - center
    spread = jnp.mean(moved * moved, axis=-1, keepdims=True)
    return moved * lax.rsqrt(spread + 1e-06) * (1.0 + scaling) + offset_vec


def attend(q_t, k_t, v_t, mask=None):
    scores = mm(k_t, q_t, TN)
    if mask is not None:
        scores = jnp.where(mask, scores, F32(-1e30))
    highest = jnp.max(scores, axis=0, keepdims=True)
    expon = jnp.exp2((scores - highest) * F32(EXP2_SCALE))
    total = jnp.sum(expon, axis=0, keepdims=True)
    return mm(v_t, expon.astype(BF)) * (1.0 / total)


def turned(values_t):
    return values_t.astype(BF).T


def kernel_qkv(x_ref, mod_ref, w_ref, b_ref, out_ref):
    frames, patches, width = x_ref.shape
    x = x_ref[...].reshape(frames * patches, width).astype(F32)
    h = modulated(x, mod_ref[0:1, :], mod_ref[1:2, :]).astype(BF)
    for i in range(w_ref.shape[0]):
        qkv = mm(w_ref[i], h, NT) + b_ref[i]
        for c in range(3):
            out_ref[i, c] = qkv[c * HD : (c + 1) * HD].astype(BF)


def kernel_spatial(ids_ref, x_ref, own_ref, mod_ref, w_ref, b_ref, out_ref, part_ref, *, chunked):
    others, frames, patches, width = x_ref.shape
    heads = w_ref.shape[0]
    spaces = others + 1
    for j in range(others):
        x = x_ref[j].reshape(frames * patches, width).astype(F32)
        h = modulated(x, mod_ref[0:1, :], mod_ref[1:2, :]).astype(BF)
        for i in range(heads):
            qkv = mm(w_ref[i], h, NT) + b_ref[i]
            for c in range(3):
                part_ref[j, i, c] = qkv[c * HD : (c + 1) * HD].astype(BF)
    for f in range(frames):
        cols = slice(f * patches, (f + 1) * patches)
        done = []
        for i in range(heads):
            q_t, k_t, v_t = (
                jnp.concatenate(
                    [own_ref[i, c, :, cols]] + [part_ref[j, i, c, :, cols] for j in range(others)],
                    axis=1,
                )
                for c in range(3)
            )
            done.append(attend(q_t, k_t, v_t))
        rows = jnp.concatenate(done, axis=0).T
        for j in range(spaces):
            place = lax.rem(ids_ref[0] - j + spaces, spaces)
            mine = rows[j * patches : (j + 1) * patches]
            if chunked:
                pieces, _, size, columns = out_ref.shape[1:]
                out_ref[place, :, f] = mine.reshape(pieces, size, columns).astype(BF)
            else:
                out_ref[place, f] = mine.astype(BF)


def middle(tokens, parts, outbias, gate):
    summed = parts[0].astype(BF).astype(F32)
    for part in parts[1:]:
        summed = summed + part.astype(BF).astype(F32)
    return (tokens.astype(F32) + gate * (summed + outbias)).astype(BF)


def kernel_temporal(ids_ref, o_ref, x_ref, out_w_ref, other_w_ref, outbias_ref, mod_ref, b_ref, *refs, size):
    w_refs, out_ref = refs[:-1], refs[-1]
    spaces, rows, _ = o_ref.shape
    space, core = ids_ref[0], ids_ref[1]
    parts = [mm(o_ref[space], out_w_ref[...])]
    for k in range(1, spaces):
        parts.append(mm(o_ref[lax.rem(space - k + spaces, spaces)], other_w_ref[k - 1]))
    y = middle(x_ref[...], parts, outbias_ref[...], mod_ref[2:3, :])
    h = modulated(y.astype(F32), mod_ref[3:4, :], mod_ref[4:5, :]).astype(BF)

    def place(axis):
        row = lax.broadcasted_iota(jnp.int32, (rows, rows), axis)
        frame = row // (2 * size) * 2 + row % (2 * size) // size
        return frame, row % size

    key_frame, key_patch = place(0)
    query_frame, query_patch = place(1)
    back = query_frame - key_frame
    mask = (key_patch == query_patch) & (back >= 0) & (back < WIN)

    heads = w_refs[0].shape[0]
    half = heads // 2
    done, order = [], []
    for n, w_ref in enumerate(w_refs):
        if n == 0:
            first = space * heads
        else:
            first = lax.rem(space - (n + 1) // 2 + spaces, spaces) * heads
            first = first + half * (core if n % 2 else 1 - core)
        for i in range(w_ref.shape[0]):
            qkv = (mm(w_ref[i], h, NT) + b_ref[first + i]).astype(BF)
            o_t = attend(qkv[0:HD], qkv[HD : 2 * HD], qkv[2 * HD : 3 * HD], mask)
            out_ref[first + i] = o_t.astype(BF)


def kernel_home(o_ref, x_ref, out_w_ref, other_w_ref, outbias_ref, mod_ref, out_ref):
    parts = [mm(o_ref[0], out_w_ref[...])]
    for k in range(1, o_ref.shape[0]):
        parts.append(mm(o_ref[k], other_w_ref[k - 1]))
    out_ref[...] = middle(x_ref[...], parts, outbias_ref[...], mod_ref[2:3, :])


def kernel_final(o_ref, y_ref, w_ref, outbias_ref, mod_ref, out_ref):
    final = mm(o_ref[...], w_ref[...]) + outbias_ref[...]
    out_ref[...] = (y_ref[...].astype(F32) + mod_ref[5:6, :] * final).astype(BF)


def call(kernel, out_shape, count, flops, nbytes, first_smem=False, scratch=()):
    return pl.pallas_call(
        kernel,
        out_shape=jax.ShapeDtypeStruct(out_shape, BF),
        in_specs=[SMEM if first_smem and i == 0 else VMEM for i in range(count)],
        out_specs=VMEM,
        scratch_shapes=list(scratch),
        compiler_params=PARAMS,
        cost_estimate=pl.CostEstimate(flops=int(flops), bytes_accessed=int(nbytes), transcendentals=0),
    )


def local(
    tokens,
    modulation,
    qkv_spatial,
    bias_spatial,
    out_spatial,
    outbias_spatial,
    qkv_temporal,
    bias_temporal,
    out_temporal,
    outbias_temporal,
):
    patches, frames, width = tokens.shape
    spaces, times = lax.axis_size("space"), lax.axis_size("tm")
    space, time = lax.axis_index("space"), lax.axis_index("tm")
    core = lax.rem(time, 2)
    heads = qkv_spatial.shape[1] // (3 * HD)
    cols = heads * HD
    half = heads // 2
    size = patches // times
    rows = patches * frames
    ids = jnp.stack([space, core]).astype(jnp.int32)

    def across(array, k):
        return lax.ppermute(array, "space", [(i, (i + k) % spaces) for i in range(spaces)])

    def beside(array):
        return lax.ppermute(array, "tm", [(i, i ^ 1) for i in range(times)])

    def frame_major(array):
        return jnp.swapaxes(array, -3, -2)

    arrived = [across(tokens, k) for k in range(1, spaces)]
    spread = lax.all_to_all(tokens.reshape(times, size, frames, width), "tm", 0, 0, tiled=True)

    w_spatial = qkv_spatial.T.reshape(heads, 3 * HD, width)
    b_spatial = bias_spatial.reshape(heads, 3 * HD, 1)
    own_tokens = frame_major(tokens)
    own = call(kernel_qkv, (heads, 3, HD, rows), 4, 2 * rows * width * cols * 3, 3e6)(
        own_tokens, modulation, w_spatial, b_spatial
    )

    w_temporal = qkv_temporal.T.reshape(heads, 3 * HD, width)
    my_heads = lax.dynamic_slice_in_dim(w_temporal, core * half, half, 0)
    my_out = lax.dynamic_slice_in_dim(out_spatial, core * half * HD, half * HD, 0)
    my_heads, my_out, *arrived = lax.optimization_barrier((my_heads, my_out, *arrived))
    other_out, other_heads = [], []
    for k in range(1, spaces):
        direct = across(my_out, k)
        passed = beside(direct)
        other_out.append(
            jnp.where(core == 0, jnp.concatenate([direct, passed]), jnp.concatenate([passed, direct]))
        )
    for k in range(1, spaces):
        direct = across(my_heads, k)
        other_heads += [direct, beside(direct)]
    other_out = jnp.stack(other_out)
    b_temporal = lax.all_gather(bias_temporal, "space", axis=0, tiled=True)
    b_temporal = b_temporal.reshape(spaces * heads, 3 * HD, 1)

    chunked = size % 8 == 0
    o_shape = (spaces, times, frames, size, cols) if chunked else (spaces, frames, patches, cols)
    o_all = call(
        functools.partial(kernel_spatial, chunked=chunked),
        o_shape,
        6,
        2 * rows * width * cols * 3 * (spaces - 1) + 4 * rows * cols * patches * spaces * spaces,
        4e6,
        True,
        [pltpu.VMEM((spaces - 1, heads, 3, HD, rows), BF)],
    )(ids, jnp.stack([frame_major(a) for a in arrived]), own, modulation, w_spatial, b_spatial)
    if not chunked:
        o_all = jnp.transpose(o_all.reshape(spaces, frames, times, size, cols), (0, 2, 1, 3, 4))

    o_here = lax.all_to_all(
        o_all.reshape(spaces * times, frames * size, cols), ("space", "tm"), 0, 0, tiled=True
    ).reshape(spaces, rows, cols)
    o_home = [lax.dynamic_index_in_dim(o_all, space, 0, keepdims=False)]
    for k in range(1, spaces):
        o_home.append(across(lax.dynamic_index_in_dim(o_all, (space + k) % spaces, 0, keepdims=False), k))
    o_home = jnp.stack(o_home).reshape(spaces, rows, cols)

    outbias_s = outbias_spatial.reshape(1, width)
    outbias_t = outbias_temporal.reshape(1, width)
    x_here = frame_major(spread).reshape(rows, width)
    o_t = call(
        functools.partial(kernel_temporal, size=size),
        (spaces * heads, HD, rows),
        8 + 1 + len(other_heads),
        2 * rows * width * cols * 4 * spaces + 4 * rows * rows * cols * spaces,
        8e6,
        True,
    )(ids, o_here, x_here, out_spatial, other_out, outbias_s, modulation, b_temporal, w_temporal, *other_heads)
    o_t = jnp.transpose(o_t, (2, 0, 1)).reshape(times, frames * size, spaces * cols)
    o_final = lax.all_to_all(o_t, "tm", 0, 0, tiled=True).reshape(rows, spaces * cols)

    x_home = jnp.swapaxes(tokens.reshape(times, size, frames, width), 1, 2).reshape(rows, width)
    y_home = call(kernel_home, (rows, width), 6, 2 * rows * width * cols * spaces, 3e6)(
        o_home, x_home, out_spatial, other_out, outbias_s, modulation
    )
    result = call(kernel_final, (rows, width), 5, 2 * rows * width * cols * spaces, 3e6)(
        o_final, y_home, out_temporal, outbias_t, modulation
    )
    return jnp.swapaxes(result.reshape(times, frames, size, width), 1, 2).reshape(patches, frames, width)


def solution(mesh):
    return jax.shard_map(
        local,
        mesh=mesh,
        in_specs=(
            P("space", ("grp", "tm"), None),
            P("grp", None),
            P(None, "space"),
            P("space"),
            P("space", None),
            P(),
            P(None, "space"),
            P("space"),
            P(),
            P(),
        ),
        out_specs=P("space", ("grp", "tm"), None),
        check_vma=False,
    )
```

```python
import functools
import math

import jax
import jax.numpy as jnp
from jax import lax
from jax.experimental import pallas as pl
from jax.experimental.pallas import tpu as pltpu
from jax.sharding import PartitionSpec as P

HD = 72
WIN = 16
BF = jnp.bfloat16
F32 = jnp.float32
EXP2_SCALE = 1.0 / (math.sqrt(HD) * math.log(2.0))

VMEM = pl.BlockSpec(memory_space=pltpu.VMEM)
SMEM = pl.BlockSpec(memory_space=pltpu.SMEM)
PARAMS = pltpu.CompilerParams(vmem_limit_bytes=48 * 1024 * 1024)

NT = (((1,), (1,)), ((), ()))
TN = (((0,), (0,)), ((), ()))


def mm(a, b, dims=(((1,), (0,)), ((), ()))):
    return lax.dot_general(a, b, dims, preferred_element_type=F32)


def modulated(values, offset_vec, scaling):
    center = jnp.mean(values, axis=-1, keepdims=True)
    moved = values - center
    spread = jnp.mean(moved * moved, axis=-1, keepdims=True)
    return moved * lax.rsqrt(spread + 1e-06) * (1.0 + scaling) + offset_vec


def attend(q_t, k_t, v_t, mask=None):
    scores = mm(k_t, q_t, TN)
    if mask is not None:
        scores = jnp.where(mask, scores, F32(-1e30))
    highest = jnp.max(scores, axis=0, keepdims=True)
    expon = jnp.exp2((scores - highest) * F32(EXP2_SCALE))
    total = jnp.sum(expon, axis=0, keepdims=True)
    return mm(v_t, expon.astype(BF)) * (1.0 / total)


def after(arrays, *others):
    return lax.optimization_barrier((*arrays, *others))[: len(arrays)]


def kernel_qkv(x_ref, mod_ref, w_ref, b_ref, out_ref):
    frames, patches, width = x_ref.shape
    x = x_ref[...].reshape(frames * patches, width).astype(F32)
    h = modulated(x, mod_ref[0:1, :], mod_ref[1:2, :]).astype(BF)
    for i in range(w_ref.shape[0]):
        qkv = mm(w_ref[i], h, NT) + b_ref[i]
        for c in range(3):
            out_ref[i, c] = qkv[c * HD : (c + 1) * HD].astype(BF)


def kernel_spatial(ids_ref, x_ref, own_ref, mod_ref, w_ref, b_ref, out_ref, part_ref, *, chunked):
    others, frames, patches, width = x_ref.shape
    heads = w_ref.shape[0]
    spaces = others + 1
    for j in range(others):
        x = x_ref[j].reshape(frames * patches, width).astype(F32)
        h = modulated(x, mod_ref[0:1, :], mod_ref[1:2, :]).astype(BF)
        for i in range(heads):
            qkv = mm(w_ref[i], h, NT) + b_ref[i]
            for c in range(3):
                part_ref[j, i, c] = qkv[c * HD : (c + 1) * HD].astype(BF)
    for f in range(frames):
        cols = slice(f * patches, (f + 1) * patches)
        done = []
        for i in range(heads):
            q_t, k_t, v_t = (
                jnp.concatenate(
                    [own_ref[i, c, :, cols]] + [part_ref[j, i, c, :, cols] for j in range(others)],
                    axis=1,
                )
                for c in range(3)
            )
            done.append(attend(q_t, k_t, v_t))
        rows = jnp.concatenate(done, axis=0).T
        for j in range(spaces):
            place = lax.rem(ids_ref[0] - j + spaces, spaces)
            mine = rows[j * patches : (j + 1) * patches]
            if chunked:
                pieces, _, size, columns = out_ref.shape[1:]
                out_ref[place, :, f] = mine.reshape(pieces, size, columns).astype(BF)
            else:
                out_ref[place, f] = mine.astype(BF)


def middle(tokens, parts, outbias, gate):
    summed = parts[0].astype(BF).astype(F32)
    for part in parts[1:]:
        summed = summed + part.astype(BF).astype(F32)
    return (tokens.astype(F32) + gate * (summed + outbias)).astype(BF)


def temporal_mask(rows, size):
    def place(axis):
        row = lax.broadcasted_iota(jnp.int32, (rows, rows), axis)
        frame = row // (2 * size) * 2 + row % (2 * size) // size
        return frame, row % size

    key_frame, key_patch = place(0)
    query_frame, query_patch = place(1)
    back = query_frame - key_frame
    return (key_patch == query_patch) & (back >= 0) & (back < WIN)


def temporal_head(w, b, h, mask):
    qkv = (mm(w, h, NT) + b).astype(BF)
    return attend(qkv[0:HD], qkv[HD : 2 * HD], qkv[2 * HD : 3 * HD], mask)


def kernel_temporal(o_ref, x_ref, out_w_ref, outbias_ref, mod_ref, b_ref, w_ref, h_ref, out_ref, *, size):
    spaces, rows, _ = o_ref.shape
    parts = [mm(o_ref[g], out_w_ref[g]) for g in range(spaces)]
    y = middle(x_ref[...], parts, outbias_ref[...], mod_ref[2:3, :])
    h = modulated(y.astype(F32), mod_ref[3:4, :], mod_ref[4:5, :]).astype(BF)
    h_ref[...] = h
    mask = temporal_mask(rows, size)
    for i in range(w_ref.shape[0]):
        out_ref[i] = temporal_head(w_ref[i], b_ref[i], h, mask)


def kernel_rest(ids_ref, h_ref, own_ref, b_ref, *refs, size):
    w_refs, (out_ref, turn_ref) = refs[:-2], refs[-2:]
    h = h_ref[...]
    rows = h.shape[0]
    mask = temporal_mask(rows, size)
    heads = own_ref.shape[0]
    half = heads // 2
    spaces = turn_ref.shape[0] // heads
    space, core = ids_ref[0], ids_ref[1]
    for i in range(heads):
        turn_ref[space * heads + i] = own_ref[i]
    for n, w_ref in enumerate(w_refs):
        shift = n // 2 + 1
        within = half * (1 - core if n % 2 else core)
        for i in range(half):
            o_t = temporal_head(w_ref[i], b_ref[shift * heads + within + i], h, mask)
            turn_ref[lax.rem(space - shift + spaces, spaces) * heads + within + i] = o_t
    out_ref[...] = turn_ref[...].reshape(-1, rows).T.astype(BF)


def kernel_home(ids_ref, o_ref, x_ref, out_w_ref, outbias_ref, mod_ref, out_ref):
    spaces = o_ref.shape[0]
    parts = [mm(o_ref[k], out_w_ref[lax.rem(ids_ref[0] - k + spaces, spaces)]) for k in range(spaces)]
    out_ref[...] = middle(x_ref[...], parts, outbias_ref[...], mod_ref[2:3, :])


def kernel_final(o_ref, y_ref, w_ref, outbias_ref, mod_ref, out_ref):
    final = mm(o_ref[...], w_ref[...]) + outbias_ref[...]
    out_ref[...] = (y_ref[...].astype(F32) + mod_ref[5:6, :] * final).astype(BF)


def call(kernel, out_shape, count, flops, nbytes, first_smem=False, scratch=()):
    return pl.pallas_call(
        kernel,
        out_shape=jax.ShapeDtypeStruct(out_shape, BF),
        in_specs=[SMEM if first_smem and i == 0 else VMEM for i in range(count)],
        out_specs=VMEM,
        scratch_shapes=list(scratch),
        compiler_params=PARAMS,
        cost_estimate=pl.CostEstimate(flops=int(flops), bytes_accessed=int(nbytes), transcendentals=0),
    )


def local(
    tokens,
    modulation,
    qkv_spatial,
    bias_spatial,
    out_spatial,
    outbias_spatial,
    qkv_temporal,
    bias_temporal,
    out_temporal,
    outbias_temporal,
):
    patches, frames, width = tokens.shape
    spaces, times = lax.axis_size("space"), lax.axis_size("tm")
    space, time = lax.axis_index("space"), lax.axis_index("tm")
    core = lax.rem(time, 2)
    heads = qkv_spatial.shape[1] // (3 * HD)
    cols = heads * HD
    half = heads // 2
    size = patches // times
    rows = patches * frames
    ids = jnp.stack([space, core]).astype(jnp.int32)

    def across(array, k):
        return lax.ppermute(array, "space", [(i, (i + k) % spaces) for i in range(spaces)])

    def beside(array):
        return lax.ppermute(array, "tm", [(i, i ^ 1) for i in range(times)])

    def frame_major(array):
        return jnp.swapaxes(array, -3, -2)

    share = math.gcd(times, 4)
    part = cols // share
    gathered = lax.all_gather(
        lax.dynamic_slice_in_dim(out_spatial, lax.rem(time, share) * part, part, 0),
        ("space", "tm"),
        axis=0,
        tiled=True,
        axis_index_groups=[
            [s * times + g * share + i for s in range(spaces) for i in range(share)] for g in range(times // share)
        ],
    ).reshape(spaces, cols, width)

    arrived = [across(tokens, k) for k in range(1, spaces)]

    w_spatial = qkv_spatial.T.reshape(heads, 3 * HD, width)
    b_spatial = bias_spatial.reshape(heads, 3 * HD, 1)
    own_tokens = frame_major(tokens)
    own = call(kernel_qkv, (heads, 3, HD, rows), 4, 2 * rows * width * cols * 3, 3e6)(
        own_tokens, modulation, w_spatial, b_spatial
    )

    (spread,) = after((tokens,), own)
    spread = lax.all_to_all(spread.reshape(times, size, frames, width), "tm", 0, 0, tiled=True)

    w_temporal = qkv_temporal.T.reshape(heads, 3 * HD, width)
    my_heads = lax.dynamic_slice_in_dim(w_temporal, core * half, half, 0)
    (my_heads,) = after((my_heads,), own, *arrived)
    arrived = [after((a,), own)[0] for a in arrived]
    direct_heads = [across(my_heads, k) for k in range(1, spaces)]
    b_temporal = jnp.stack([bias_temporal] + [across(bias_temporal, k) for k in range(1, spaces)])
    b_temporal = b_temporal.reshape(spaces * heads, 3 * HD, 1)

    chunked = size % 8 == 0
    o_shape = (spaces, times, frames, size, cols) if chunked else (spaces, frames, patches, cols)
    o_all = call(
        functools.partial(kernel_spatial, chunked=chunked),
        o_shape,
        6,
        1e10,
        4e6,
        True,
        [pltpu.VMEM((spaces - 1, heads, 3, HD, rows), BF)],
    )(ids, jnp.stack([frame_major(a) for a in arrived]), own, modulation, w_spatial, b_spatial)
    if not chunked:
        o_all = jnp.transpose(o_all.reshape(spaces, frames, times, size, cols), (0, 2, 1, 3, 4))

    o_here = lax.all_to_all(
        after((o_all,), spread, b_temporal)[0].reshape(spaces * times, frames * size, cols), ("space", "tm"), 0, 0, tiled=True
    ).reshape(spaces, rows, cols)
    other_heads = []
    for a in direct_heads:
        other_heads += [a, beside(after((a,), o_here)[0])]

    o_home = [lax.dynamic_index_in_dim(o_all, space, 0, keepdims=False)]
    for k in range(1, spaces):
        o_home.append(across(lax.dynamic_index_in_dim(o_all, (space + k) % spaces, 0, keepdims=False), k))
    o_home = jnp.stack(o_home).reshape(spaces, rows, cols)

    outbias_s = outbias_spatial.reshape(1, width)
    outbias_t = outbias_temporal.reshape(1, width)
    x_here = frame_major(spread).reshape(rows, width)
    h_here, o_own = pl.pallas_call(
        functools.partial(kernel_temporal, size=size),
        out_shape=(jax.ShapeDtypeStruct((rows, width), BF), jax.ShapeDtypeStruct((heads, HD, rows), F32)),
        in_specs=[VMEM] * 7,
        out_specs=(VMEM, VMEM),
        compiler_params=PARAMS,
        cost_estimate=pl.CostEstimate(
            flops=2 * rows * width * cols * (3 + spaces), bytes_accessed=5 * 10**6, transcendentals=0
        ),
    )(o_here, x_here, gathered, outbias_s, modulation, b_temporal, w_temporal)
    o_t = call(
        functools.partial(kernel_rest, size=size),
        (rows, spaces * cols),
        4 + len(other_heads),
        2 * rows * width * cols * 3 * (spaces - 1),
        5e6,
        True,
        [pltpu.VMEM((spaces * heads, HD, rows), F32)],
    )(ids, h_here, o_own, b_temporal, *other_heads)
    o_t = o_t.reshape(times, frames * size, spaces * cols)
    o_final = lax.all_to_all(o_t, "tm", 0, 0, tiled=True).reshape(rows, spaces * cols)

    x_home = jnp.swapaxes(tokens.reshape(times, size, frames, width), 1, 2).reshape(rows, width)
    y_home = call(kernel_home, (rows, width), 6, 2 * rows * width * cols * spaces, 3e6, True)(
        ids, o_home, x_home, gathered, outbias_s, modulation
    )
    result = call(kernel_final, (rows, width), 5, 2 * rows * width * cols * spaces, 3e6)(
        o_final, y_home, out_temporal, outbias_t, modulation
    )
    return jnp.swapaxes(result.reshape(times, frames, size, width), 1, 2).reshape(patches, frames, width)


def solution(mesh):
    return jax.shard_map(
        local,
        mesh=mesh,
        in_specs=(
            P("space", ("grp", "tm"), None),
            P("grp", None),
            P(None, "space"),
            P("space"),
            P("space", None),
            P(),
            P(None, "space"),
            P("space"),
            P(),
            P(),
        ),
        out_specs=P("space", ("grp", "tm"), None),
        check_vma=False,
    )
```

```python
import functools
import math

import jax
import jax.numpy as jnp
from jax import lax
from jax.experimental import pallas as pl
from jax.experimental.pallas import tpu as pltpu
from jax.sharding import PartitionSpec as P

HD = 72
WIN = 16
BF = jnp.bfloat16
F32 = jnp.float32
EXP2_SCALE = 1.0 / (math.sqrt(HD) * math.log(2.0))

VMEM = pl.BlockSpec(memory_space=pltpu.VMEM)
ANY = pl.BlockSpec(memory_space=pl.ANY)
SMEM = pl.BlockSpec(memory_space=pltpu.SMEM)
PARAMS = pltpu.CompilerParams(vmem_limit_bytes=63 * 1024 * 1024)

NT = (((1,), (1,)), ((), ()))
TN = (((0,), (0,)), ((), ()))


def mm(a, b, dims=(((1,), (0,)), ((), ()))):
    return lax.dot_general(a, b, dims, preferred_element_type=F32)


def modulated(values, offset_vec, scaling):
    center = jnp.mean(values, axis=-1, keepdims=True)
    moved = values - center
    spread = jnp.mean(moved * moved, axis=-1, keepdims=True)
    return moved * lax.rsqrt(spread + 1e-06) * (1.0 + scaling) + offset_vec


def attend(q_t, k_t, v_t, mask=None):
    scores = mm(k_t, q_t, TN)
    if mask is not None:
        scores = jnp.where(mask, scores, F32(-1e30))
    highest = jnp.max(scores, axis=0, keepdims=True)
    expon = jnp.exp2((scores - highest) * F32(EXP2_SCALE))
    total = jnp.sum(expon, axis=0, keepdims=True)
    return mm(v_t, expon.astype(BF)) * (1.0 / total)


def after(arrays, *others):
    return lax.optimization_barrier((*arrays, *others))[: len(arrays)]


def flat(ref, *index):
    block = ref[index] if index else ref[...]
    return block.reshape(-1, block.shape[-1])


def regroup(rows, frames):
    target = lax.broadcasted_iota(jnp.int32, (rows, rows), 0)
    source = lax.broadcasted_iota(jnp.int32, (rows, rows), 1)
    patches = rows // frames
    return (source == target % patches * frames + target // patches).astype(F32).astype(BF)


def spatial_rows(x, mod_ref, frames):
    h = modulated(x.astype(F32), mod_ref[0:1, :], mod_ref[1:2, :]).astype(BF)
    return mm(regroup(x.shape[0], frames), h).astype(BF)


def kernel_qkv(x_ref, mod_ref, w_ref, b_ref, out_ref):
    h = spatial_rows(flat(x_ref), mod_ref, x_ref.shape[1])
    bias = b_ref[...].T
    for i in range(w_ref.shape[0]):
        qkv = mm(w_ref[i], h, NT) + bias[:, i : i + 1]
        for c in range(3):
            out_ref[i, c] = qkv[c * HD : (c + 1) * HD].astype(BF)


def fetch(sources, targets, sems):
    copies = [pltpu.make_async_copy(a, b, sems.at[i]) for i, (a, b) in enumerate(zip(sources, targets))]
    for copy in copies:
        copy.start()
    return copies


def kernel_spatial(ids_ref, own_hbm, w_hbm, mod_ref, b_ref, *refs):
    x_refs, (out_ref, part_ref, own_ref, w_ref, sems) = refs[:-5], refs[-5:]
    copies = fetch((w_hbm, own_hbm), (w_ref, own_ref), sems)
    patches, frames, _ = x_refs[0].shape
    heads = w_ref.shape[0]
    spaces = len(x_refs) + 1
    bias = b_ref[...].T
    for j, x_ref in enumerate(x_refs):
        h = spatial_rows(flat(x_ref), mod_ref, frames)
        if j == 0:
            copies[0].wait()
        for i in range(heads):
            qkv = mm(w_ref[i], h, NT) + bias[:, i : i + 1]
            for c in range(3):
                part_ref[j, i, c] = qkv[c * HD : (c + 1) * HD].astype(BF)
    copies[1].wait()
    by_frame = []
    for f in range(frames):
        cols = slice(f * patches, (f + 1) * patches)
        done = []
        for i in range(heads):
            q_t, k_t, v_t = (
                jnp.concatenate(
                    [own_ref[i, c, :, cols]] + [part_ref[j, i, c, :, cols] for j in range(spaces - 1)],
                    axis=1,
                )
                for c in range(3)
            )
            done.append(attend(q_t, k_t, v_t))
        by_frame.append(jnp.concatenate(done, axis=0).astype(BF))
    back = regroup(patches * frames, frames)
    for j in range(spaces):
        mine = jnp.concatenate([o[:, j * patches : (j + 1) * patches] for o in by_frame], axis=1)
        out_ref[lax.rem(ids_ref[0] - j + spaces, spaces)] = lax.dot_general(
            back, mine, (((0,), (1,)), ((), ())), preferred_element_type=F32
        ).astype(BF)


def middle(tokens, parts, outbias, gate):
    summed = parts[0].astype(BF).astype(F32)
    for part in parts[1:]:
        summed = summed + part.astype(BF).astype(F32)
    return (tokens.astype(F32) + gate * (summed + outbias)).astype(BF)


def temporal_mask(rows, size, frames):
    def place(axis):
        row = lax.broadcasted_iota(jnp.int32, (rows, rows), axis)
        return row // (frames * size) * frames + row % frames, row // frames % size

    key_frame, key_patch = place(0)
    query_frame, query_patch = place(1)
    back = query_frame - key_frame
    return (key_patch == query_patch) & (back >= 0) & (back < WIN)


def temporal_head(w, b, h, mask):
    qkv = (mm(w, h, NT) + b).astype(BF)
    return attend(qkv[0:HD], qkv[HD : 2 * HD], qkv[2 * HD : 3 * HD], mask)


def out_places(pieces, out_w_ref, core):
    half = pieces[1].shape[0]
    places = [out_w_ref.at[0]]
    for n in range(1, len(pieces)):
        start = half * (core if n % 2 else 1 - core)
        places.append(out_w_ref.at[(n + 1) // 2, pl.ds(pl.multiple_of(start, half), half)])
    return places


def kernel_temporal(
    ids_ref, o_hbm, x_hbm, w_hbm, outbias_ref, mod_ref, b_ref, *refs, size, frames
):
    pieces, (h_ref, out_ref, o_ref, x_ref, out_w_ref, w_ref, sems) = refs[:-7], refs[-7:]
    copies = fetch(
        (*pieces, o_hbm, x_hbm, w_hbm),
        (*out_places(pieces, out_w_ref, ids_ref[1]), o_ref, x_ref, w_ref),
        sems,
    )
    spaces, rows, _ = o_ref.shape
    mask = temporal_mask(rows, size, frames)
    for copy in copies[:-1]:
        copy.wait()
    parts = [mm(o_ref[lax.rem(ids_ref[0] - k + spaces, spaces)], out_w_ref[k]) for k in range(spaces)]
    y = middle(flat(x_ref), parts, outbias_ref[...], mod_ref[2:3, :])
    h = modulated(y.astype(F32), mod_ref[3:4, :], mod_ref[4:5, :]).astype(BF)
    h_ref[...] = h
    bias = b_ref[...].T
    copies[-1].wait()
    for i in range(w_ref.shape[0]):
        out_ref[i] = temporal_head(w_ref[i], bias[:, i : i + 1], h, mask)


def kernel_rest(ids_ref, h_ref, own_ref, b_ref, *refs, size, frames):
    w_refs, (out_ref, turn_ref) = refs[:-2], refs[-2:]
    h = h_ref[...]
    rows = h.shape[0]
    mask = temporal_mask(rows, size, frames)
    heads = own_ref.shape[0]
    half = heads // 2
    spaces = turn_ref.shape[0] // heads
    space, core = ids_ref[0], ids_ref[1]
    bias = b_ref[...].T
    for i in range(heads):
        turn_ref[space * heads + i] = own_ref[i]
    for n, w_ref in enumerate(w_refs):
        shift = n // 2 + 1
        second = (core == 0) == (n % 2 == 1)
        within = jnp.where(second, half, 0)
        for i in range(half):
            first = shift * heads + i
            column = jnp.where(second, bias[:, first + half : first + half + 1], bias[:, first : first + 1])
            o_t = temporal_head(w_ref[i], column, h, mask)
            turn_ref[lax.rem(space - shift + spaces, spaces) * heads + within + i] = o_t
    out_ref[...] = turn_ref[...].reshape(-1, rows).T.astype(BF)


def kernel_home(ids_ref, o_own_ref, x_ref, outbias_ref, mod_ref, *refs):
    spaces = refs[-2].shape[0]
    o_refs, pieces, (out_ref, out_w_ref, sems) = refs[: spaces - 1], refs[spaces - 1 : -3], refs[-3:]
    copies = fetch(pieces, out_places(pieces, out_w_ref, ids_ref[1]), sems)
    for copy in copies:
        copy.wait()
    parts = [mm(o_own_ref[ids_ref[0]], out_w_ref[0])]
    for k in range(1, spaces):
        parts.append(mm(o_refs[k - 1][...], out_w_ref[k]))
    out_ref[...] = middle(flat(x_ref), parts, outbias_ref[...], mod_ref[2:3, :])


def kernel_final(o_ref, y_ref, w_ref, outbias_ref, mod_ref, out_ref):
    final = mm(o_ref[...], w_ref[...]) + outbias_ref[...]
    result = (y_ref[...].astype(F32) + mod_ref[5:6, :] * final).astype(BF)
    out_ref[...] = result.reshape(out_ref.shape)


def call(kernel, out_shape, count, flops, nbytes, first_smem=False, scratch=(), in_any=()):
    return pl.pallas_call(
        kernel,
        out_shape=jax.ShapeDtypeStruct(out_shape, BF),
        in_specs=[SMEM if first_smem and i == 0 else ANY if i in in_any else VMEM for i in range(count)],
        out_specs=VMEM,
        scratch_shapes=list(scratch),
        compiler_params=PARAMS,
        cost_estimate=pl.CostEstimate(flops=int(flops), bytes_accessed=int(nbytes), transcendentals=0),
    )


def local(
    tokens,
    modulation,
    qkv_spatial,
    bias_spatial,
    out_spatial,
    outbias_spatial,
    qkv_temporal,
    bias_temporal,
    out_temporal,
    outbias_temporal,
):
    patches, frames, width = tokens.shape
    spaces, times = lax.axis_size("space"), lax.axis_size("tm")
    space, time = lax.axis_index("space"), lax.axis_index("tm")
    core = lax.rem(time, 2)
    heads = qkv_spatial.shape[1] // (3 * HD)
    cols = heads * HD
    half = heads // 2
    size = patches // times
    rows = patches * frames
    ids = jnp.stack([space, core]).astype(jnp.int32)

    def across(array, k):
        return lax.ppermute(array, "space", [(i, (i + k) % spaces) for i in range(spaces)])

    def beside(array):
        return lax.ppermute(array, "tm", [(i, i ^ 1) for i in range(times)])

    arrived = [across(tokens, k) for k in range(1, spaces)]

    w_spatial = qkv_spatial.T.reshape(heads, 3 * HD, width)
    b_spatial = bias_spatial.reshape(heads, 3 * HD)
    own = call(kernel_qkv, (heads, 3, HD, rows), 4, 2 * rows * width * cols * 3, 3e6)(
        tokens, modulation, w_spatial, b_spatial
    )

    (spread,) = after((tokens,), own)
    spread = lax.all_to_all(spread.reshape(times, size, frames, width), "tm", 0, 0, tiled=True)

    w_temporal = qkv_temporal.T.reshape(heads, 3 * HD, width)
    my_heads = lax.dynamic_slice_in_dim(w_temporal, core * half, half, 0)
    b_temporal = jnp.stack([bias_temporal] + [across(bias_temporal, k) for k in range(1, spaces)])
    b_temporal = b_temporal.reshape(spaces * heads, 3 * HD)
    my_out = lax.dynamic_slice_in_dim(out_spatial, core * half * HD, half * HD, 0)
    (my_out,) = after((my_out,), own, b_temporal, *arrived)
    arrived = [after((a,), own)[0] for a in arrived]
    direct_out = [across(my_out, k) for k in range(1, spaces)]

    o_all = call(
        kernel_spatial,
        (spaces, rows, cols),
        5 + len(arrived),
        1e10,
        4e6,
        True,
        [
            pltpu.VMEM((spaces - 1, heads, 3, HD, rows), BF),
            pltpu.VMEM(own.shape, BF),
            pltpu.VMEM(w_spatial.shape, BF),
            pltpu.SemaphoreType.DMA((2,)),
        ],
        (1, 2),
    )(ids, own, w_spatial, modulation, b_spatial, *arrived)

    (my_heads,) = after((my_heads,), o_all, *direct_out)
    direct_heads = [across(my_heads, k) for k in range(1, spaces)]
    out_pieces = [out_spatial]
    for a in direct_out:
        out_pieces += [a, beside(after((a,), o_all)[0])]

    o_here = lax.all_to_all(
        after((o_all,), spread, *out_pieces)[0].reshape(spaces * times, frames * size, cols), ("space", "tm"), 0, 0, tiled=True
    ).reshape(spaces, rows, cols)
    other_heads = []
    for a in direct_heads:
        other_heads += [a, beside(after((a,), o_here)[0])]

    o_home = [
        across(lax.dynamic_index_in_dim(o_all, (space + k) % spaces, 0, keepdims=False), k)
        for k in range(1, spaces)
    ]

    outbias_s = outbias_spatial.reshape(1, width)
    outbias_t = outbias_temporal.reshape(1, width)
    x_here = spread.reshape(rows // frames, frames, width)
    h_here, o_own = pl.pallas_call(
        functools.partial(kernel_temporal, size=size, frames=frames),
        out_shape=(jax.ShapeDtypeStruct((rows, width), BF), jax.ShapeDtypeStruct((heads, HD, rows), F32)),
        in_specs=[SMEM] + [ANY] * 3 + [VMEM] * 3 + [ANY] * len(out_pieces),
        out_specs=(VMEM, VMEM),
        scratch_shapes=[
            pltpu.VMEM(o_here.shape, BF),
            pltpu.VMEM(x_here.shape, BF),
            pltpu.VMEM((spaces, cols, width), BF),
            pltpu.VMEM(w_temporal.shape, BF),
            pltpu.SemaphoreType.DMA((len(out_pieces) + 3,)),
        ],
        compiler_params=PARAMS,
        cost_estimate=pl.CostEstimate(
            flops=2 * rows * width * cols * (3 + spaces), bytes_accessed=5 * 10**6, transcendentals=0
        ),
    )(ids, o_here, x_here, w_temporal, outbias_s, modulation, b_temporal, *out_pieces)
    o_t = call(
        functools.partial(kernel_rest, size=size, frames=frames),
        (rows, spaces * cols),
        4 + len(other_heads),
        2 * rows * width * cols * 3 * (spaces - 1),
        5e6,
        True,
        [pltpu.VMEM((spaces * heads, HD, rows), F32)],
    )(ids, h_here, o_own, b_temporal, *other_heads)
    o_t = o_t.reshape(times, frames * size, spaces * cols)
    o_final = lax.all_to_all(o_t, "tm", 0, 0, tiled=True).reshape(rows, spaces * cols)

    y_home = call(
        kernel_home,
        (rows, width),
        5 + len(o_home) + len(out_pieces),
        2 * rows * width * cols * spaces,
        3e6,
        True,
        [pltpu.VMEM((spaces, cols, width), BF), pltpu.SemaphoreType.DMA((len(out_pieces),))],
        range(5 + len(o_home), 5 + len(o_home) + len(out_pieces)),
    )(ids, o_all, tokens, outbias_s, modulation, *o_home, *out_pieces)
    return call(kernel_final, (patches, frames, width), 5, 2 * rows * width * cols * spaces, 3e6)(
        o_final, y_home, out_temporal, outbias_t, modulation
    )


def solution(mesh):
    return jax.shard_map(
        local,
        mesh=mesh,
        in_specs=(
            P("space", ("grp", "tm"), None),
            P("grp", None),
            P(None, "space"),
            P("space"),
            P("space", None),
            P(),
            P(None, "space"),
            P("space"),
            P(),
            P(),
        ),
        out_specs=P("space", ("grp", "tm"), None),
        check_vma=False,
    )
```

```python
import functools
import math

import jax
import jax.numpy as jnp
from jax import lax
from jax.experimental import pallas as pl
from jax.experimental.pallas import tpu as pltpu
from jax.sharding import PartitionSpec as P

HD = 72
WIN = 16
BF = jnp.bfloat16
F32 = jnp.float32
EXP2_SCALE = 1.0 / (math.sqrt(HD) * math.log(2.0))

VMEM = pl.BlockSpec(memory_space=pltpu.VMEM)
ANY = pl.BlockSpec(memory_space=pl.ANY)
SMALL = pltpu.CompilerParams(vmem_limit_bytes=16 * 1024 * 1024)
PARAMS = pltpu.CompilerParams(vmem_limit_bytes=63 * 1024 * 1024)

NT = (((1,), (1,)), ((), ()))
TN = (((0,), (0,)), ((), ()))


def mm(a, b, dims=(((1,), (0,)), ((), ()))):
    return lax.dot_general(a, b, dims, preferred_element_type=F32)


def modulated(values, offset_vec, scaling):
    center = jnp.mean(values, axis=-1, keepdims=True)
    moved = values - center
    spread = jnp.mean(moved * moved, axis=-1, keepdims=True)
    return moved * lax.rsqrt(spread + 1e-06) * (1.0 + scaling) + offset_vec


def attend(q_t, k_t, v_t, mask=None):
    scores = mm(k_t, q_t, TN)
    if mask is not None:
        scores = jnp.where(mask, scores, F32(-1e30))
    highest = jnp.max(scores, axis=0, keepdims=True)
    expon = jnp.exp2((scores - highest) * F32(EXP2_SCALE))
    total = jnp.sum(expon, axis=0, keepdims=True)
    return mm(v_t, expon.astype(BF)) * (1.0 / total)


def after(arrays, *others):
    return lax.optimization_barrier((*arrays, *others))[: len(arrays)]


def flat(ref, *index):
    block = ref[index] if index else ref[...]
    return block.reshape(-1, block.shape[-1])


def column(rows):
    return lax.broadcasted_iota(jnp.int32, (rows, 1), 0)


def line(rows):
    return lax.broadcasted_iota(jnp.int32, (1, rows), 1)


def chosen(source, rows):
    return (source == line(rows)).astype(F32).astype(BF)


def by_frame_first(rows, frames):
    r = column(rows)
    return chosen(lax.rem(r, rows // frames) * frames + lax.div(r, rows // frames), rows)


def by_patch_first(rows, frames):
    r = column(rows)
    return chosen(lax.rem(r, frames) * (rows // frames) + lax.div(r, frames), rows)


def bias_column(b_ref):
    count = b_ref.shape[0]
    return jnp.broadcast_to(b_ref[...].reshape(1, count), (8, count)).T[:, 0:1]


def spatial_rows(x, mod_ref, frames):
    h = modulated(x.astype(F32), mod_ref[0:1, :], mod_ref[1:2, :]).astype(BF)
    return mm(by_frame_first(x.shape[0], frames), h).astype(BF)


def fetch(sources, targets, sems):
    copies = [pltpu.make_async_copy(a, b, sems.at[i]) for i, (a, b) in enumerate(zip(sources, targets))]
    for copy in copies:
        copy.start()
    return copies


def coordinates():
    return lax.axis_index("space"), lax.rem(lax.axis_index("tm"), 2)


def kernel_qkv(x_ref, w_hbm, w_other_hbm, out_w_hbm, mod_ref, b_ref, out_ref, heads_ref, half_ref, w_ref, sems):
    _, core = coordinates()
    half, rows = heads_ref.shape[0], half_ref.shape[0]
    copies = fetch(
        (
            w_hbm,
            out_w_hbm.at[pl.ds(pl.multiple_of(core * rows, rows), rows)],
            w_other_hbm.at[pl.ds(core * half, half)],
        ),
        (w_ref, half_ref, heads_ref),
        sems,
    )
    h = spatial_rows(flat(x_ref), mod_ref, x_ref.shape[1])
    bias = bias_column(b_ref)
    copies[0].wait()
    for i in range(w_ref.shape[0]):
        qkv = mm(w_ref[i], h, NT) + bias[i * 3 * HD : (i + 1) * 3 * HD]
        for c in range(3):
            out_ref[i, c] = qkv[c * HD : (c + 1) * HD].astype(BF)
    for copy in copies[1:]:
        copy.wait()


def kernel_spatial(own_hbm, w_hbm, mod_ref, b_ref, *refs):
    x_refs, (out_ref, part_ref, own_ref, w_ref, sems) = refs[:-5], refs[-5:]
    copies = fetch((w_hbm, own_hbm), (w_ref, own_ref), sems)
    space, _ = coordinates()
    patches, frames, _ = x_refs[0].shape
    heads = w_ref.shape[0]
    spaces = len(x_refs) + 1
    bias = bias_column(b_ref)
    for j, x_ref in enumerate(x_refs):
        h = spatial_rows(flat(x_ref), mod_ref, frames)
        if j == 0:
            copies[0].wait()
        for i in range(heads):
            qkv = mm(w_ref[i], h, NT) + bias[i * 3 * HD : (i + 1) * 3 * HD]
            for c in range(3):
                part_ref[j, i, c] = qkv[c * HD : (c + 1) * HD].astype(BF)
    copies[1].wait()
    by_frame = []
    for f in range(frames):
        cols = slice(f * patches, (f + 1) * patches)
        done = []
        for i in range(heads):
            q_t, k_t, v_t = (
                jnp.concatenate(
                    [own_ref[i, c, :, cols]] + [part_ref[j, i, c, :, cols] for j in range(spaces - 1)],
                    axis=1,
                )
                for c in range(3)
            )
            done.append(attend(q_t, k_t, v_t))
        by_frame.append(jnp.concatenate(done, axis=0).astype(BF))
    back = by_patch_first(patches * frames, frames)
    for j in range(spaces):
        mine = jnp.concatenate([o[:, j * patches : (j + 1) * patches] for o in by_frame], axis=1)
        out_ref[lax.rem(space - j + spaces, spaces)] = mm(back, mine, NT).astype(BF)


def middle(tokens, parts, outbias, gate):
    summed = parts[0].astype(BF).astype(F32)
    for part in parts[1:]:
        summed = summed + part.astype(BF).astype(F32)
    return (tokens.astype(F32) + gate * (summed + outbias)).astype(BF)


def temporal_mask(rows, size, frames):
    def place(row):
        device, within = lax.div(row, frames * size), lax.rem(row, frames * size)
        return device * frames + lax.rem(within, frames), lax.div(within, frames)

    key_frame, key_patch = place(column(rows))
    query_frame, query_patch = place(line(rows))
    code_key = key_patch * 4 * WIN * rows + key_frame
    code_query = query_patch * 4 * WIN * rows + query_frame
    back = code_query - code_key
    return (back >= 0) & (back < WIN)


def temporal_head(w, b, h, mask):
    qkv = (mm(w, h, NT) + b).astype(BF)
    return attend(qkv[0:HD], qkv[HD : 2 * HD], qkv[2 * HD : 3 * HD], mask)


def out_places(pieces, out_w_ref, core):
    half = pieces[1].shape[0]
    places = [out_w_ref.at[0]]
    for n in range(1, len(pieces)):
        start = half * (core if n % 2 else 1 - core)
        places.append(out_w_ref.at[(n + 1) // 2, pl.ds(pl.multiple_of(start, half), half)])
    return places


def kernel_temporal(
    o_hbm, x_hbm, w_hbm, outbias_ref, mod_ref, b_ref, *refs, size, frames
):
    space, core = coordinates()
    pieces, (h_ref, out_ref, o_ref, x_ref, out_w_ref, w_ref, sems) = refs[:-7], refs[-7:]
    copies = fetch(
        (*pieces, o_hbm, x_hbm, w_hbm),
        (*out_places(pieces, out_w_ref, core), o_ref, x_ref, w_ref),
        sems,
    )
    spaces, rows, _ = o_ref.shape
    mask = temporal_mask(rows, size, frames)
    for copy in copies[:-1]:
        copy.wait()
    parts = [mm(o_ref[lax.rem(space - k + spaces, spaces)], out_w_ref[k]) for k in range(spaces)]
    y = middle(flat(x_ref), parts, outbias_ref[...].reshape(1, -1), mod_ref[2:3, :])
    h = modulated(y.astype(F32), mod_ref[3:4, :], mod_ref[4:5, :]).astype(BF)
    h_ref[...] = h
    bias = bias_column(b_ref)
    copies[-1].wait()
    for i in range(w_ref.shape[0]):
        out_ref[i] = temporal_head(w_ref[i], bias[i * 3 * HD : (i + 1) * 3 * HD], h, mask)


def kernel_rest(h_ref, own_ref, *refs, size, frames, spaces):
    b_refs, w_hbms, (out_ref, turn_ref, w_ref, sems) = refs[: spaces - 1], refs[spaces - 1 : -4], refs[-4:]
    space, core = coordinates()
    copies = fetch(w_hbms, [w_ref.at[n] for n in range(len(w_hbms))], sems)
    h = h_ref[...]
    rows = h.shape[0]
    mask = temporal_mask(rows, size, frames)
    heads = own_ref.shape[0]
    half = heads // 2
    for i in range(heads):
        turn_ref[space * heads + i] = own_ref[i]
    for n in range(len(w_hbms)):
        shift = n // 2 + 1
        bias = bias_column(b_refs[shift - 1])
        second = (core == 0) == (n % 2 == 1)
        within = jnp.where(second, half, 0)
        group = lax.rem(space - shift + spaces, spaces)
        bias = jnp.where(second, bias[half * 3 * HD :], bias[: half * 3 * HD])
        copies[n].wait()
        for i in range(half):
            o_t = temporal_head(w_ref[n, i], bias[i * 3 * HD : (i + 1) * 3 * HD], h, mask)
            turn_ref[group * heads + within + i] = o_t
    out_ref[...] = turn_ref[...].reshape(-1, rows).T.astype(BF)


def kernel_home(o_own_ref, x_ref, outbias_ref, mod_ref, *refs):
    space, core = coordinates()
    spaces = refs[-2].shape[0]
    o_refs, pieces, (out_ref, out_w_ref, sems) = refs[: spaces - 1], refs[spaces - 1 : -3], refs[-3:]
    copies = fetch(pieces, out_places(pieces, out_w_ref, core), sems)
    for copy in copies:
        copy.wait()
    parts = [mm(o_own_ref[space], out_w_ref[0])]
    for k in range(1, spaces):
        parts.append(mm(o_refs[k - 1][...], out_w_ref[k]))
    out_ref[...] = middle(flat(x_ref), parts, outbias_ref[...].reshape(1, -1), mod_ref[2:3, :])


def kernel_final(o_ref, y_ref, w_ref, outbias_ref, mod_ref, out_ref):
    final = mm(o_ref[...], w_ref[...]) + outbias_ref[...].reshape(1, -1)
    result = (y_ref[...].astype(F32) + mod_ref[5:6, :] * final).astype(BF)
    out_ref[...] = result.reshape(out_ref.shape)


def call(kernel, out_shape, count, flops, nbytes, scratch=(), in_any=(), params=PARAMS):
    return pl.pallas_call(
        kernel,
        out_shape=jax.ShapeDtypeStruct(out_shape, BF),
        in_specs=[ANY if i in in_any else VMEM for i in range(count)],
        out_specs=VMEM,
        scratch_shapes=list(scratch),
        compiler_params=params,
        cost_estimate=pl.CostEstimate(flops=int(flops), bytes_accessed=int(nbytes), transcendentals=0),
    )


def local(
    tokens,
    modulation,
    qkv_spatial,
    bias_spatial,
    out_spatial,
    outbias_spatial,
    qkv_temporal,
    bias_temporal,
    out_temporal,
    outbias_temporal,
):
    patches, frames, width = tokens.shape
    spaces, times = lax.axis_size("space"), lax.axis_size("tm")
    space = lax.axis_index("space")
    heads = qkv_spatial.shape[1] // (3 * HD)
    cols = heads * HD
    half = heads // 2
    size = patches // times
    rows = patches * frames

    def across(array, k):
        return lax.ppermute(array, "space", [(i, (i + k) % spaces) for i in range(spaces)])

    def beside(array):
        return lax.ppermute(array, "tm", [(i, i ^ 1) for i in range(times)])

    arrived = [across(tokens, k) for k in range(1, spaces)]

    w_spatial = qkv_spatial.T.reshape(heads, 3 * HD, width)
    w_temporal = qkv_temporal.T.reshape(heads, 3 * HD, width)
    own, my_heads, my_out = pl.pallas_call(
        kernel_qkv,
        out_shape=tuple(
            jax.ShapeDtypeStruct(a, BF)
            for a in ((heads, 3, HD, rows), (half, 3 * HD, width), (half * HD, width))
        ),
        in_specs=[VMEM] + [ANY] * 3 + [VMEM] * 2,
        out_specs=(VMEM, ANY, ANY),
        scratch_shapes=[pltpu.VMEM(w_spatial.shape, BF), pltpu.SemaphoreType.DMA((3,))],
        compiler_params=PARAMS,
        cost_estimate=pl.CostEstimate(
            flops=2 * rows * width * cols * 3, bytes_accessed=3 * 10**6, transcendentals=0
        ),
    )(tokens, w_spatial, w_temporal, out_spatial, modulation, bias_spatial)

    (spread,) = after((tokens,), own)
    spread = lax.all_to_all(spread.reshape(times, size, frames, width), "tm", 0, 0, tiled=True)

    other_bias = [across(bias_temporal, k) for k in range(1, spaces)]
    (my_out,) = after((my_out,), *other_bias, *arrived)
    arrived = [after((a,), own)[0] for a in arrived]
    direct_out = [across(my_out, k) for k in range(1, spaces)]

    o_all = call(
        kernel_spatial,
        (spaces, rows, cols),
        4 + len(arrived),
        1e10,
        4e6,
        [
            pltpu.VMEM((spaces - 1, heads, 3, HD, rows), BF),
            pltpu.VMEM(own.shape, BF),
            pltpu.VMEM(w_spatial.shape, BF),
            pltpu.SemaphoreType.DMA((2,)),
        ],
        (0, 1),
    )(own, w_spatial, modulation, bias_spatial, *arrived)

    (my_heads,) = after((my_heads,), o_all, *direct_out)
    direct_heads = [across(my_heads, k) for k in range(1, spaces)]
    out_pieces = [out_spatial]
    for a in direct_out:
        out_pieces += [a, beside(after((a,), o_all)[0])]

    o_here = lax.all_to_all(
        after((o_all,), spread, *out_pieces)[0].reshape(spaces * times, frames * size, cols), ("space", "tm"), 0, 0, tiled=True
    ).reshape(spaces, rows, cols)
    other_heads = []
    for a in direct_heads:
        other_heads += [a, beside(after((a,), o_here)[0])]

    o_home = [
        across(lax.dynamic_index_in_dim(o_all, (space + k) % spaces, 0, keepdims=False), k)
        for k in range(1, spaces)
    ]

    y_home = call(
        kernel_home,
        (rows, width),
        4 + len(o_home) + len(out_pieces),
        2 * rows * width * cols * spaces,
        3e6,
        [pltpu.VMEM((spaces, cols, width), BF), pltpu.SemaphoreType.DMA((len(out_pieces),))],
        range(4 + len(o_home), 4 + len(o_home) + len(out_pieces)),
        SMALL,
    )(o_all, tokens, outbias_spatial, modulation, *o_home, *out_pieces)
    x_here = spread.reshape(rows // frames, frames, width)
    h_here, o_own = pl.pallas_call(
        functools.partial(kernel_temporal, size=size, frames=frames),
        out_shape=(jax.ShapeDtypeStruct((rows, width), BF), jax.ShapeDtypeStruct((heads, HD, rows), F32)),
        in_specs=[ANY] * 3 + [VMEM] * 3 + [ANY] * len(out_pieces),
        out_specs=(VMEM, VMEM),
        scratch_shapes=[
            pltpu.VMEM(o_here.shape, BF),
            pltpu.VMEM(x_here.shape, BF),
            pltpu.VMEM((spaces, cols, width), BF),
            pltpu.VMEM(w_temporal.shape, BF),
            pltpu.SemaphoreType.DMA((len(out_pieces) + 3,)),
        ],
        compiler_params=PARAMS,
        cost_estimate=pl.CostEstimate(
            flops=2 * rows * width * cols * (3 + spaces), bytes_accessed=5 * 10**6, transcendentals=0
        ),
    )(o_here, x_here, w_temporal, outbias_spatial, modulation, bias_temporal, *out_pieces)
    o_t = call(
        functools.partial(kernel_rest, size=size, frames=frames, spaces=spaces),
        (rows, spaces * cols),
        1 + spaces + len(other_heads),
        2 * rows * width * cols * 3 * (spaces - 1),
        5e6,
        [
            pltpu.VMEM((spaces * heads, HD, rows), F32),
            pltpu.VMEM((len(other_heads), half, 3 * HD, width), BF),
            pltpu.SemaphoreType.DMA((len(other_heads),)),
        ],
        range(1 + spaces, 1 + spaces + len(other_heads)),
    )(h_here, o_own, *other_bias, *other_heads)
    o_t = o_t.reshape(times, frames * size, spaces * cols)
    o_final = lax.all_to_all(o_t, "tm", 0, 0, tiled=True).reshape(rows, spaces * cols)

    return call(
        kernel_final, (patches, frames, width), 5, 2 * rows * width * cols * spaces, 3e6, params=SMALL
    )(o_final, y_home, out_temporal, outbias_temporal, modulation)


def solution(mesh):
    return jax.shard_map(
        local,
        mesh=mesh,
        in_specs=(
            P("space", ("grp", "tm"), None),
            P("grp", None),
            P(None, "space"),
            P("space"),
            P("space", None),
            P(),
            P(None, "space"),
            P("space"),
            P(),
            P(),
        ),
        out_specs=P("space", ("grp", "tm"), None),
        check_vma=False,
    )
```

```python
import functools
import math

import jax
import jax.numpy as jnp
from jax import lax
from jax.experimental import pallas as pl
from jax.experimental.pallas import tpu as pltpu
from jax.sharding import PartitionSpec as P

HD = 72
WIN = 16
BF = jnp.bfloat16
F32 = jnp.float32
EXP2_SCALE = 1.0 / (math.sqrt(HD) * math.log(2.0))

VMEM = pl.BlockSpec(memory_space=pltpu.VMEM)
ANY = pl.BlockSpec(memory_space=pl.ANY)
SMALL = pltpu.CompilerParams(vmem_limit_bytes=16 * 1024 * 1024)
PARAMS = pltpu.CompilerParams(vmem_limit_bytes=63 * 1024 * 1024)

NT = (((1,), (1,)), ((), ()))
TN = (((0,), (0,)), ((), ()))


def mm(a, b, dims=(((1,), (0,)), ((), ()))):
    return lax.dot_general(a, b, dims, preferred_element_type=F32)


def modulated(values, offset_vec, scaling):
    center = jnp.mean(values, axis=-1, keepdims=True)
    moved = values - center
    spread = jnp.mean(moved * moved, axis=-1, keepdims=True)
    return moved * lax.rsqrt(spread + 1e-06) * (1.0 + scaling) + offset_vec


def attend(q_t, k_t, v_t, mask=None):
    scores = mm(k_t, q_t, TN)
    if mask is not None:
        scores = jnp.where(mask, scores, F32(-1e30))
    highest = jnp.max(scores, axis=0, keepdims=True)
    expon = jnp.exp2((scores - highest) * F32(EXP2_SCALE))
    total = jnp.sum(expon, axis=0, keepdims=True)
    return mm(v_t, expon.astype(BF)) * (1.0 / total)


def after(arrays, *others):
    return lax.optimization_barrier((*arrays, *others))[: len(arrays)]


def flat(ref, *index):
    block = ref[index] if index else ref[...]
    return block.reshape(-1, block.shape[-1])


def column(rows):
    return lax.broadcasted_iota(jnp.int32, (rows, 1), 0)


def line(rows):
    return lax.broadcasted_iota(jnp.int32, (1, rows), 1)


def chosen(source, rows):
    return (source == line(rows)).astype(F32).astype(BF)


def by_frame_first(rows, frames):
    r = column(rows)
    return chosen(lax.rem(r, rows // frames) * frames + lax.div(r, rows // frames), rows)


def by_patch_first(rows, frames):
    r = column(rows)
    return chosen(lax.rem(r, frames) * (rows // frames) + lax.div(r, frames), rows)


def bias_column(b_ref):
    count = b_ref.shape[0]
    return jnp.broadcast_to(b_ref[...].reshape(1, count), (8, count)).T[:, 0:1]


def spatial_rows(x, mod_ref, frames):
    h = modulated(x.astype(F32), mod_ref[0:1, :], mod_ref[1:2, :]).astype(BF)
    return mm(by_frame_first(x.shape[0], frames), h).astype(BF)


def fetch(sources, targets, sems):
    copies = [pltpu.make_async_copy(a, b, sems.at[i]) for i, (a, b) in enumerate(zip(sources, targets))]
    for copy in copies:
        copy.start()
    return copies


def coordinates():
    return lax.axis_index("space"), lax.rem(lax.axis_index("tm"), 2)


def kernel_qkv(x_ref, w_hbm, w_other_hbm, out_w_hbm, mod_ref, b_ref, out_ref, heads_ref, half_ref, w_ref, sems):
    _, core = coordinates()
    half, rows = heads_ref.shape[0], half_ref.shape[0]
    copies = fetch(
        (
            w_hbm,
            out_w_hbm.at[pl.ds(pl.multiple_of(core * rows, rows), rows)],
            w_other_hbm.at[pl.ds(core * half, half)],
        ),
        (w_ref, half_ref, heads_ref),
        sems,
    )
    h = spatial_rows(flat(x_ref), mod_ref, x_ref.shape[1])
    bias = bias_column(b_ref)
    copies[0].wait()
    for i in range(w_ref.shape[0]):
        qkv = mm(w_ref[i], h, NT) + bias[i * 3 * HD : (i + 1) * 3 * HD]
        for c in range(3):
            out_ref[i, c] = qkv[c * HD : (c + 1) * HD].astype(BF)
    for copy in copies[1:]:
        copy.wait()


def kernel_spatial(own_hbm, w_hbm, mod_ref, b_ref, *refs):
    x_refs, (out_ref, part_ref, own_ref, w_ref, sems) = refs[:-5], refs[-5:]
    heads = w_ref.shape[0]
    copies = fetch(
        (*[w_hbm.at[i] for i in range(heads)], own_hbm),
        (*[w_ref.at[i] for i in range(heads)], own_ref),
        sems,
    )
    space, _ = coordinates()
    patches, frames, _ = x_refs[0].shape
    spaces = len(x_refs) + 1
    bias = bias_column(b_ref)
    rows = [spatial_rows(flat(x_ref), mod_ref, frames) for x_ref in x_refs]
    for i in range(heads):
        copies[i].wait()
        for j in range(spaces - 1):
            qkv = mm(w_ref[i], rows[j], NT) + bias[i * 3 * HD : (i + 1) * 3 * HD]
            for c in range(3):
                part_ref[j, i, c] = qkv[c * HD : (c + 1) * HD].astype(BF)
    copies[heads].wait()
    by_frame = []
    for f in range(frames):
        cols = slice(f * patches, (f + 1) * patches)
        done = []
        for i in range(heads):
            q_t, k_t, v_t = (
                jnp.concatenate(
                    [own_ref[i, c, :, cols]] + [part_ref[j, i, c, :, cols] for j in range(spaces - 1)],
                    axis=1,
                )
                for c in range(3)
            )
            done.append(attend(q_t, k_t, v_t))
        by_frame.append(jnp.concatenate(done, axis=0).astype(BF))
    back = by_patch_first(patches * frames, frames)
    for j in range(spaces):
        mine = jnp.concatenate([o[:, j * patches : (j + 1) * patches] for o in by_frame], axis=1)
        out_ref[lax.rem(space - j + spaces, spaces)] = mm(back, mine, NT).astype(BF)


def middle(tokens, parts, outbias, gate):
    summed = parts[0].astype(BF).astype(F32)
    for part in parts[1:]:
        summed = summed + part.astype(BF).astype(F32)
    return (tokens.astype(F32) + gate * (summed + outbias)).astype(BF)


def temporal_mask(rows, size, frames):
    def place(row):
        device, within = lax.div(row, frames * size), lax.rem(row, frames * size)
        return device * frames + lax.rem(within, frames), lax.div(within, frames)

    key_frame, key_patch = place(column(rows))
    query_frame, query_patch = place(line(rows))
    code_key = key_patch * 4 * WIN * rows + key_frame
    code_query = query_patch * 4 * WIN * rows + query_frame
    back = code_query - code_key
    return (back >= 0) & (back < WIN)


def temporal_head(w, b, h, mask):
    qkv = (mm(w, h, NT) + b).astype(BF)
    return attend(qkv[0:HD], qkv[HD : 2 * HD], qkv[2 * HD : 3 * HD], mask)


def parts_of(o, pieces, core):
    half = pieces[1].shape[0]
    parts = [mm(o(0), pieces[0][...])]
    for k in range(1, (len(pieces) + 1) // 2):
        first, second = pieces[2 * k - 1][...], pieces[2 * k][...]
        rows = jnp.concatenate([jnp.where(core == 0, first, second), jnp.where(core == 0, second, first)])
        parts.append(mm(o(k), rows))
    return parts


def kernel_temporal(o_ref, x_ref, w_ref, outbias_ref, mod_ref, b_ref, *refs, size, frames):
    space, core = coordinates()
    pieces, (h_ref, out_ref) = refs[:-2], refs[-2:]
    spaces, rows, _ = o_ref.shape
    mask = temporal_mask(rows, size, frames)
    parts = parts_of(lambda k: o_ref[lax.rem(space - k + spaces, spaces)], pieces, core)
    y = middle(flat(x_ref), parts, outbias_ref[...].reshape(1, -1), mod_ref[2:3, :])
    h = modulated(y.astype(F32), mod_ref[3:4, :], mod_ref[4:5, :]).astype(BF)
    h_ref[...] = h
    bias = bias_column(b_ref)
    for i in range(w_ref.shape[0]):
        out_ref[i] = temporal_head(w_ref[i], bias[i * 3 * HD : (i + 1) * 3 * HD], h, mask)


def kernel_rest(h_ref, own_ref, *refs, size, frames, spaces):
    b_refs, w_refs, (out_ref, turn_ref) = refs[: spaces - 1], refs[spaces - 1 : -2], refs[-2:]
    space, core = coordinates()
    h = h_ref[...]
    rows = h.shape[0]
    mask = temporal_mask(rows, size, frames)
    heads = own_ref.shape[0]
    half = heads // 2
    for i in range(heads):
        turn_ref[space * heads + i] = own_ref[i]
    for n, w_ref in enumerate(w_refs):
        shift = n // 2 + 1
        bias = bias_column(b_refs[shift - 1])
        second = (core == 0) == (n % 2 == 1)
        within = jnp.where(second, half, 0)
        group = lax.rem(space - shift + spaces, spaces)
        bias = jnp.where(second, bias[half * 3 * HD :], bias[: half * 3 * HD])
        for i in range(half):
            o_t = temporal_head(w_ref[i], bias[i * 3 * HD : (i + 1) * 3 * HD], h, mask)
            turn_ref[group * heads + within + i] = o_t
    out_ref[...] = turn_ref[...].reshape(-1, rows).T.astype(BF)


def kernel_home(o_own_ref, x_ref, outbias_ref, mod_ref, *refs):
    space, core = coordinates()
    spaces = o_own_ref.shape[0]
    o_refs, pieces, out_ref = refs[: spaces - 1], refs[spaces - 1 : -1], refs[-1]
    parts = parts_of(lambda k: o_refs[k - 1][...] if k else o_own_ref[space], pieces, core)
    out_ref[...] = middle(flat(x_ref), parts, outbias_ref[...].reshape(1, -1), mod_ref[2:3, :])


def kernel_final(o_ref, y_ref, w_ref, outbias_ref, mod_ref, out_ref):
    final = mm(o_ref[...], w_ref[...]) + outbias_ref[...].reshape(1, -1)
    result = (y_ref[...].astype(F32) + mod_ref[5:6, :] * final).astype(BF)
    out_ref[...] = result.reshape(out_ref.shape)


def call(kernel, out_shape, count, flops, nbytes, scratch=(), in_any=(), params=PARAMS):
    return pl.pallas_call(
        kernel,
        out_shape=jax.ShapeDtypeStruct(out_shape, BF),
        in_specs=[ANY if i in in_any else VMEM for i in range(count)],
        out_specs=VMEM,
        scratch_shapes=list(scratch),
        compiler_params=params,
        cost_estimate=pl.CostEstimate(flops=int(flops), bytes_accessed=int(nbytes), transcendentals=0),
    )


def local(
    tokens,
    modulation,
    qkv_spatial,
    bias_spatial,
    out_spatial,
    outbias_spatial,
    qkv_temporal,
    bias_temporal,
    out_temporal,
    outbias_temporal,
):
    patches, frames, width = tokens.shape
    spaces, times = lax.axis_size("space"), lax.axis_size("tm")
    space = lax.axis_index("space")
    heads = qkv_spatial.shape[1] // (3 * HD)
    cols = heads * HD
    half = heads // 2
    size = patches // times
    rows = patches * frames

    def across(array, k):
        return lax.ppermute(array, "space", [(i, (i + k) % spaces) for i in range(spaces)])

    def beside(array):
        return lax.ppermute(array, "tm", [(i, i ^ 1) for i in range(times)])

    arrived = [across(tokens, k) for k in range(1, spaces)]

    w_spatial = qkv_spatial.T.reshape(heads, 3 * HD, width)
    w_temporal = qkv_temporal.T.reshape(heads, 3 * HD, width)
    own, my_heads, my_out = pl.pallas_call(
        kernel_qkv,
        out_shape=tuple(
            jax.ShapeDtypeStruct(a, BF)
            for a in ((heads, 3, HD, rows), (half, 3 * HD, width), (half * HD, width))
        ),
        in_specs=[VMEM] + [ANY] * 3 + [VMEM] * 2,
        out_specs=(VMEM, VMEM, VMEM),
        scratch_shapes=[pltpu.VMEM(w_spatial.shape, BF), pltpu.SemaphoreType.DMA((3,))],
        compiler_params=PARAMS,
        cost_estimate=pl.CostEstimate(
            flops=2 * rows * width * cols * 3, bytes_accessed=3 * 10**6, transcendentals=0
        ),
    )(tokens, w_spatial, w_temporal, out_spatial, modulation, bias_spatial)

    (spread,) = after((tokens,), own)
    spread = lax.all_to_all(spread.reshape(times, size, frames, width), "tm", 0, 0, tiled=True)

    other_bias = [across(bias_temporal, k) for k in range(1, spaces)]
    (my_out,) = after((my_out,), *other_bias, *arrived)
    arrived = [after((a,), own)[0] for a in arrived]
    direct_out = [across(my_out, k) for k in range(1, spaces)]

    o_all = call(
        kernel_spatial,
        (spaces, rows, cols),
        4 + len(arrived),
        1e10,
        4e6,
        [
            pltpu.VMEM((spaces - 1, heads, 3, HD, rows), BF),
            pltpu.VMEM(own.shape, BF),
            pltpu.VMEM(w_spatial.shape, BF),
            pltpu.SemaphoreType.DMA((heads + 1,)),
        ],
        (0, 1),
    )(own, w_spatial, modulation, bias_spatial, *arrived)

    (my_heads,) = after((my_heads,), o_all, *direct_out)
    direct_heads = [across(my_heads, k) for k in range(1, spaces)]
    out_pieces = [out_spatial]
    for a in direct_out:
        out_pieces += [a, beside(after((a,), o_all)[0])]

    o_here = lax.all_to_all(
        after((o_all,), spread, *out_pieces)[0].reshape(spaces * times, frames * size, cols), ("space", "tm"), 0, 0, tiled=True
    ).reshape(spaces, rows, cols)
    other_heads = []
    for a in direct_heads:
        other_heads += [a, beside(after((a,), o_here)[0])]

    o_home = [
        across(lax.dynamic_index_in_dim(o_all, (space + k) % spaces, 0, keepdims=False), k)
        for k in range(1, spaces)
    ]

    y_home = call(
        kernel_home,
        (rows, width),
        4 + len(o_home) + len(out_pieces),
        2 * rows * width * cols * spaces,
        3e6,
        params=SMALL,
    )(o_all, tokens, outbias_spatial, modulation, *o_home, *out_pieces)
    x_here = spread.reshape(rows // frames, frames, width)
    h_here, o_own = pl.pallas_call(
        functools.partial(kernel_temporal, size=size, frames=frames),
        out_shape=(jax.ShapeDtypeStruct((rows, width), BF), jax.ShapeDtypeStruct((heads, HD, rows), F32)),
        in_specs=[VMEM] * (6 + len(out_pieces)),
        out_specs=(VMEM, VMEM),
        compiler_params=SMALL,
        cost_estimate=pl.CostEstimate(
            flops=2 * rows * width * cols * (3 + spaces), bytes_accessed=5 * 10**6, transcendentals=0
        ),
    )(o_here, x_here, w_temporal, outbias_spatial, modulation, bias_temporal, *out_pieces)
    o_t = call(
        functools.partial(kernel_rest, size=size, frames=frames, spaces=spaces),
        (rows, spaces * cols),
        1 + spaces + len(other_heads),
        2 * rows * width * cols * 3 * (spaces - 1),
        5e6,
        [
            pltpu.VMEM((spaces * heads, HD, rows), F32),
        ],
        params=SMALL,
    )(h_here, o_own, *other_bias, *other_heads)
    o_t = o_t.reshape(times, frames * size, spaces * cols)
    o_final = lax.all_to_all(o_t, "tm", 0, 0, tiled=True).reshape(rows, spaces * cols)

    return call(
        kernel_final, (patches, frames, width), 5, 2 * rows * width * cols * spaces, 3e6, params=SMALL
    )(o_final, y_home, out_temporal, outbias_temporal, modulation)


def solution(mesh):
    return jax.shard_map(
        local,
        mesh=mesh,
        in_specs=(
            P("space", ("grp", "tm"), None),
            P("grp", None),
            P(None, "space"),
            P("space"),
            P("space", None),
            P(),
            P(None, "space"),
            P("space"),
            P(),
            P(),
        ),
        out_specs=P("space", ("grp", "tm"), None),
        check_vma=False,
    )
```

```python
import functools
import math

import jax
import jax.numpy as jnp
from jax import lax
from jax.experimental import pallas as pl
from jax.experimental.pallas import tpu as pltpu
from jax.sharding import PartitionSpec as P

HD = 72
WIN = 16
BF = jnp.bfloat16
F32 = jnp.float32
EXP2_SCALE = 1.0 / (math.sqrt(HD) * math.log(2.0))

VMEM = pl.BlockSpec(memory_space=pltpu.VMEM)
ANY = pl.BlockSpec(memory_space=pl.ANY)
SMALL = pltpu.CompilerParams(vmem_limit_bytes=16 * 1024 * 1024)
PARAMS = pltpu.CompilerParams(vmem_limit_bytes=63 * 1024 * 1024)

NT = (((1,), (1,)), ((), ()))
TN = (((0,), (0,)), ((), ()))


def mm(a, b, dims=(((1,), (0,)), ((), ()))):
    return lax.dot_general(a, b, dims, preferred_element_type=F32)


def modulated(values, offset_vec, scaling):
    center = jnp.mean(values, axis=-1, keepdims=True)
    moved = values - center
    spread = jnp.mean(moved * moved, axis=-1, keepdims=True)
    return moved * lax.rsqrt(spread + 1e-06) * (1.0 + scaling) + offset_vec


def attend(q_t, k_t, v_t, mask=None):
    scores = mm(k_t, q_t, TN)
    if mask is not None:
        scores = jnp.where(mask, scores, F32(-1e30))
    highest = jnp.max(scores, axis=0, keepdims=True)
    expon = jnp.exp2((scores - highest) * F32(EXP2_SCALE))
    total = jnp.sum(expon, axis=0, keepdims=True)
    return mm(v_t, expon.astype(BF)) * (1.0 / total)


def after(arrays, *others):
    return lax.optimization_barrier((*arrays, *others))[: len(arrays)]


def flat(ref, *index):
    block = ref[index] if index else ref[...]
    return block.reshape(-1, block.shape[-1])


def column(rows):
    return lax.broadcasted_iota(jnp.int32, (rows, 1), 0)


def line(rows):
    return lax.broadcasted_iota(jnp.int32, (1, rows), 1)


def chosen(source, rows):
    return (source == line(rows)).astype(F32).astype(BF)


def by_frame_first(rows, frames):
    r = column(rows)
    return chosen(lax.rem(r, rows // frames) * frames + lax.div(r, rows // frames), rows)


def by_patch_first(rows, frames):
    r = column(rows)
    return chosen(lax.rem(r, frames) * (rows // frames) + lax.div(r, frames), rows)


def bias_column(b_ref):
    count = b_ref.shape[0]
    return jnp.broadcast_to(b_ref[...].reshape(1, count), (8, count)).T[:, 0:1]


def spatial_rows(x, mod_ref, frames):
    h = modulated(x.astype(F32), mod_ref[0:1, :], mod_ref[1:2, :]).astype(BF)
    return mm(by_frame_first(x.shape[0], frames), h).astype(BF)


def fetch(sources, targets, sems):
    copies = [pltpu.make_async_copy(a, b, sems.at[i]) for i, (a, b) in enumerate(zip(sources, targets))]
    for copy in copies:
        copy.start()
    return copies


def coordinates():
    return lax.axis_index("space"), lax.rem(lax.axis_index("tm"), 2)


def kernel_qkv(x_ref, w_ref, w_other_hbm, out_w_hbm, mod_ref, b_ref, out_ref, heads_ref, half_ref, sems):
    _, core = coordinates()
    half, rows = heads_ref.shape[0], half_ref.shape[0]
    copies = fetch(
        (
            out_w_hbm.at[pl.ds(pl.multiple_of(core * rows, rows), rows)],
            w_other_hbm.at[pl.ds(core * half, half)],
        ),
        (half_ref, heads_ref),
        sems,
    )
    h = spatial_rows(flat(x_ref), mod_ref, x_ref.shape[1])
    bias = bias_column(b_ref)
    for i in range(w_ref.shape[0]):
        qkv = mm(w_ref[i], h, NT) + bias[i * 3 * HD : (i + 1) * 3 * HD]
        for c in range(3):
            out_ref[i, c] = qkv[c * HD : (c + 1) * HD].astype(BF)
    for copy in copies:
        copy.wait()


def kernel_spatial(own_ref, w_ref, mod_ref, b_ref, *refs):
    x_refs, (out_ref, part_ref) = refs[:-2], refs[-2:]
    heads = w_ref.shape[0]
    space, _ = coordinates()
    patches, frames, _ = x_refs[0].shape
    spaces = len(x_refs) + 1
    bias = bias_column(b_ref)
    rows = [spatial_rows(flat(x_ref), mod_ref, frames) for x_ref in x_refs]
    for i in range(heads):
        for j in range(spaces - 1):
            qkv = mm(w_ref[i], rows[j], NT) + bias[i * 3 * HD : (i + 1) * 3 * HD]
            for c in range(3):
                part_ref[j, i, c] = qkv[c * HD : (c + 1) * HD].astype(BF)
    by_frame = []
    for f in range(frames):
        cols = slice(f * patches, (f + 1) * patches)
        done = []
        for i in range(heads):
            q_t, k_t, v_t = (
                jnp.concatenate(
                    [own_ref[i, c, :, cols]] + [part_ref[j, i, c, :, cols] for j in range(spaces - 1)],
                    axis=1,
                )
                for c in range(3)
            )
            done.append(attend(q_t, k_t, v_t))
        by_frame.append(jnp.concatenate(done, axis=0).astype(BF))
    back = by_patch_first(patches * frames, frames)
    for j in range(spaces):
        mine = jnp.concatenate([o[:, j * patches : (j + 1) * patches] for o in by_frame], axis=1)
        out_ref[lax.rem(space - j + spaces, spaces)] = mm(back, mine, NT).astype(BF)


def middle(tokens, parts, outbias, gate):
    summed = parts[0].astype(BF).astype(F32)
    for part in parts[1:]:
        summed = summed + part.astype(BF).astype(F32)
    return (tokens.astype(F32) + gate * (summed + outbias)).astype(BF)


def temporal_mask(rows, size, frames):
    def place(row):
        device, within = lax.div(row, frames * size), lax.rem(row, frames * size)
        return device * frames + lax.rem(within, frames), lax.div(within, frames)

    key_frame, key_patch = place(column(rows))
    query_frame, query_patch = place(line(rows))
    code_key = key_patch * 4 * WIN * rows + key_frame
    code_query = query_patch * 4 * WIN * rows + query_frame
    back = code_query - code_key
    return (back >= 0) & (back < WIN)


def temporal_head(w, b, h, mask):
    qkv = (mm(w, h, NT) + b).astype(BF)
    return attend(qkv[0:HD], qkv[HD : 2 * HD], qkv[2 * HD : 3 * HD], mask)


def parts_of(o, pieces, core):
    half = pieces[1].shape[0]
    parts = [mm(o(0), pieces[0][...])]
    for k in range(1, (len(pieces) + 1) // 2):
        first, second = pieces[2 * k - 1][...], pieces[2 * k][...]
        rows = jnp.concatenate([jnp.where(core == 0, first, second), jnp.where(core == 0, second, first)])
        parts.append(mm(o(k), rows))
    return parts


def kernel_temporal(o_ref, x_ref, w_ref, outbias_ref, mod_ref, b_ref, *refs, size, frames):
    space, core = coordinates()
    pieces, (h_ref, out_ref) = refs[:-2], refs[-2:]
    spaces, rows, _ = o_ref.shape
    mask = temporal_mask(rows, size, frames)
    parts = parts_of(lambda k: o_ref[lax.rem(space - k + spaces, spaces)], pieces, core)
    y = middle(flat(x_ref), parts, outbias_ref[...].reshape(1, -1), mod_ref[2:3, :])
    h = modulated(y.astype(F32), mod_ref[3:4, :], mod_ref[4:5, :]).astype(BF)
    h_ref[...] = h
    bias = bias_column(b_ref)
    for i in range(w_ref.shape[0]):
        out_ref[i] = temporal_head(w_ref[i], bias[i * 3 * HD : (i + 1) * 3 * HD], h, mask)


def kernel_rest(h_ref, own_ref, *refs, size, frames, spaces):
    b_refs, w_refs, (out_ref, turn_ref) = refs[: spaces - 1], refs[spaces - 1 : -2], refs[-2:]
    space, core = coordinates()
    h = h_ref[...]
    rows = h.shape[0]
    mask = temporal_mask(rows, size, frames)
    heads = own_ref.shape[0]
    half = heads // 2
    for i in range(heads):
        turn_ref[space * heads + i] = own_ref[i]
    for n, w_ref in enumerate(w_refs):
        shift = n // 2 + 1
        bias = bias_column(b_refs[shift - 1])
        second = (core == 0) == (n % 2 == 1)
        within = jnp.where(second, half, 0)
        group = lax.rem(space - shift + spaces, spaces)
        bias = jnp.where(second, bias[half * 3 * HD :], bias[: half * 3 * HD])
        for i in range(half):
            o_t = temporal_head(w_ref[i], bias[i * 3 * HD : (i + 1) * 3 * HD], h, mask)
            turn_ref[group * heads + within + i] = o_t
    out_ref[...] = turn_ref[...].reshape(-1, rows).T.astype(BF)


def kernel_home(o_own_ref, x_ref, outbias_ref, mod_ref, *refs):
    space, core = coordinates()
    spaces = o_own_ref.shape[0]
    o_refs, pieces, out_ref = refs[: spaces - 1], refs[spaces - 1 : -1], refs[-1]
    parts = parts_of(lambda k: o_refs[k - 1][...] if k else o_own_ref[space], pieces, core)
    out_ref[...] = middle(flat(x_ref), parts, outbias_ref[...].reshape(1, -1), mod_ref[2:3, :])


def kernel_final(o_ref, y_ref, w_ref, outbias_ref, mod_ref, out_ref):
    final = mm(o_ref[...], w_ref[...]) + outbias_ref[...].reshape(1, -1)
    result = (y_ref[...].astype(F32) + mod_ref[5:6, :] * final).astype(BF)
    out_ref[...] = result.reshape(out_ref.shape)


def call(kernel, out_shape, count, flops, nbytes, scratch=(), in_any=(), params=PARAMS):
    return pl.pallas_call(
        kernel,
        out_shape=jax.ShapeDtypeStruct(out_shape, BF),
        in_specs=[ANY if i in in_any else VMEM for i in range(count)],
        out_specs=VMEM,
        scratch_shapes=list(scratch),
        compiler_params=params,
        cost_estimate=pl.CostEstimate(flops=int(flops), bytes_accessed=int(nbytes), transcendentals=0),
    )


def local(
    tokens,
    modulation,
    qkv_spatial,
    bias_spatial,
    out_spatial,
    outbias_spatial,
    qkv_temporal,
    bias_temporal,
    out_temporal,
    outbias_temporal,
):
    patches, frames, width = tokens.shape
    spaces, times = lax.axis_size("space"), lax.axis_size("tm")
    space = lax.axis_index("space")
    heads = qkv_spatial.shape[1] // (3 * HD)
    cols = heads * HD
    half = heads // 2
    size = patches // times
    rows = patches * frames

    def across(array, k):
        return lax.ppermute(array, "space", [(i, (i + k) % spaces) for i in range(spaces)])

    def beside(array):
        return lax.ppermute(array, "tm", [(i, i ^ 1) for i in range(times)])

    arrived = [across(tokens, k) for k in range(1, spaces)]

    w_spatial = qkv_spatial.T.reshape(heads, 3 * HD, width)
    w_temporal = qkv_temporal.T.reshape(heads, 3 * HD, width)
    own, my_heads, my_out = pl.pallas_call(
        kernel_qkv,
        out_shape=tuple(
            jax.ShapeDtypeStruct(a, BF)
            for a in ((heads, 3, HD, rows), (half, 3 * HD, width), (half * HD, width))
        ),
        in_specs=[VMEM] * 2 + [ANY] * 2 + [VMEM] * 2,
        out_specs=(VMEM, VMEM, VMEM),
        scratch_shapes=[pltpu.SemaphoreType.DMA((2,))],
        compiler_params=SMALL,
        cost_estimate=pl.CostEstimate(
            flops=2 * rows * width * cols * 3, bytes_accessed=3 * 10**6, transcendentals=0
        ),
    )(tokens, w_spatial, w_temporal, out_spatial, modulation, bias_spatial)

    spread = lax.all_to_all(tokens.reshape(times, size, frames, width), "tm", 0, 0, tiled=True)

    other_bias = [across(bias_temporal, k) for k in range(1, spaces)]
    (my_out,) = after((my_out,), *other_bias, *arrived)
    arrived = [after((a,), own)[0] for a in arrived]
    direct_out = [across(my_out, k) for k in range(1, spaces)]

    o_all = call(
        kernel_spatial,
        (spaces, rows, cols),
        4 + len(arrived),
        1e10,
        4e6,
        [
            pltpu.VMEM((spaces - 1, heads, 3, HD, rows), BF),
        ],
        params=SMALL,
    )(own, w_spatial, modulation, bias_spatial, *arrived)

    (my_heads,) = after((my_heads,), o_all, *direct_out)
    direct_heads = [across(my_heads, k) for k in range(1, spaces)]
    out_pieces = [out_spatial]
    for a in direct_out:
        out_pieces += [a, beside(after((a,), o_all)[0])]

    o_here = lax.all_to_all(
        after((o_all,), spread, *out_pieces)[0].reshape(spaces * times, frames * size, cols), ("space", "tm"), 0, 0, tiled=True
    ).reshape(spaces, rows, cols)
    other_heads = []
    for a in direct_heads:
        other_heads += [a, beside(after((a,), o_here)[0])]

    o_home = [
        across(lax.dynamic_index_in_dim(o_all, (space + k) % spaces, 0, keepdims=False), k)
        for k in range(1, spaces)
    ]

    y_home = call(
        kernel_home,
        (rows, width),
        4 + len(o_home) + len(out_pieces),
        2 * rows * width * cols * spaces,
        3e6,
        params=SMALL,
    )(o_all, tokens, outbias_spatial, modulation, *o_home, *out_pieces)
    x_here = spread.reshape(rows // frames, frames, width)
    h_here, o_own = pl.pallas_call(
        functools.partial(kernel_temporal, size=size, frames=frames),
        out_shape=(jax.ShapeDtypeStruct((rows, width), BF), jax.ShapeDtypeStruct((heads, HD, rows), F32)),
        in_specs=[VMEM] * (6 + len(out_pieces)),
        out_specs=(VMEM, VMEM),
        compiler_params=SMALL,
        cost_estimate=pl.CostEstimate(
            flops=2 * rows * width * cols * (3 + spaces), bytes_accessed=5 * 10**6, transcendentals=0
        ),
    )(o_here, x_here, w_temporal, outbias_spatial, modulation, bias_temporal, *out_pieces)
    o_t = call(
        functools.partial(kernel_rest, size=size, frames=frames, spaces=spaces),
        (rows, spaces * cols),
        1 + spaces + len(other_heads),
        2 * rows * width * cols * 3 * (spaces - 1),
        5e6,
        [
            pltpu.VMEM((spaces * heads, HD, rows), F32),
        ],
        params=SMALL,
    )(h_here, o_own, *other_bias, *other_heads)
    o_t = o_t.reshape(times, frames * size, spaces * cols)
    o_final = lax.all_to_all(o_t, "tm", 0, 0, tiled=True).reshape(rows, spaces * cols)

    return call(
        kernel_final, (patches, frames, width), 5, 2 * rows * width * cols * spaces, 3e6, params=SMALL
    )(o_final, y_home, out_temporal, outbias_temporal, modulation)


def solution(mesh):
    return jax.shard_map(
        local,
        mesh=mesh,
        in_specs=(
            P("space", ("grp", "tm"), None),
            P("grp", None),
            P(None, "space"),
            P("space"),
            P("space", None),
            P(),
            P(None, "space"),
            P("space"),
            P(),
            P(),
        ),
        out_specs=P("space", ("grp", "tm"), None),
        check_vma=False,
    )
```

```python
import functools
import math

import jax
import jax.numpy as jnp
from jax import lax
from jax.experimental import pallas as pl
from jax.experimental.pallas import tpu as pltpu
from jax.sharding import PartitionSpec as P

HD = 72
WIN = 16
BF = jnp.bfloat16
F32 = jnp.float32
EXP2_SCALE = 1.0 / (math.sqrt(HD) * math.log(2.0))

VMEM = pl.BlockSpec(memory_space=pltpu.VMEM)
ANY = pl.BlockSpec(memory_space=pl.ANY)
SMALL = pltpu.CompilerParams(vmem_limit_bytes=16 * 1024 * 1024)
PARAMS = pltpu.CompilerParams(vmem_limit_bytes=63 * 1024 * 1024)

NT = (((1,), (1,)), ((), ()))
TN = (((0,), (0,)), ((), ()))


def mm(a, b, dims=(((1,), (0,)), ((), ()))):
    return lax.dot_general(a, b, dims, preferred_element_type=F32)


def modulated(values, offset_vec, scaling):
    center = jnp.mean(values, axis=-1, keepdims=True)
    moved = values - center
    spread = jnp.mean(moved * moved, axis=-1, keepdims=True)
    return moved * lax.rsqrt(spread + 1e-06) * (1.0 + scaling) + offset_vec


def attend(q_t, k_t, v_t, mask=None):
    scores = mm(k_t, q_t, TN)
    if mask is not None:
        scores = jnp.where(mask, scores, F32(-1e30))
    highest = jnp.max(scores, axis=0, keepdims=True)
    expon = jnp.exp2((scores - highest) * F32(EXP2_SCALE))
    total = jnp.sum(expon, axis=0, keepdims=True)
    return mm(v_t, expon.astype(BF)) * (1.0 / total)


def after(arrays, *others):
    return lax.optimization_barrier((*arrays, *others))[: len(arrays)]


def flat(ref, *index):
    block = ref[index] if index else ref[...]
    return block.reshape(-1, block.shape[-1])


def column(rows):
    return lax.broadcasted_iota(jnp.int32, (rows, 1), 0)


def line(rows):
    return lax.broadcasted_iota(jnp.int32, (1, rows), 1)


def chosen(source, rows):
    return (source == line(rows)).astype(F32).astype(BF)


def by_frame_first(rows, frames):
    r = column(rows)
    return chosen(lax.rem(r, rows // frames) * frames + lax.div(r, rows // frames), rows)


def by_patch_first(rows, frames):
    r = column(rows)
    return chosen(lax.rem(r, frames) * (rows // frames) + lax.div(r, frames), rows)


def bias_column(b_ref):
    count = b_ref.shape[0]
    return jnp.broadcast_to(b_ref[...].reshape(1, count), (8, count)).T[:, 0:1]


def spatial_rows(x, mod_ref, frames):
    h = modulated(x.astype(F32), mod_ref[0:1, :], mod_ref[1:2, :]).astype(BF)
    return mm(by_frame_first(x.shape[0], frames), h).astype(BF)


def fetch(sources, targets, sems):
    copies = [pltpu.make_async_copy(a, b, sems.at[i]) for i, (a, b) in enumerate(zip(sources, targets))]
    for copy in copies:
        copy.start()
    return copies


def coordinates():
    return lax.axis_index("space"), lax.rem(lax.axis_index("tm"), 2)


def kernel_qkv(x_ref, w_hbm, w_other_hbm, mod_ref, b_ref, out_ref, heads_ref, w_ref, sems):
    _, core = coordinates()
    half = heads_ref.shape[0]
    copies = fetch((w_hbm, w_other_hbm.at[pl.ds(core * half, half)]), (w_ref, heads_ref), sems)
    h = spatial_rows(flat(x_ref), mod_ref, x_ref.shape[1])
    bias = bias_column(b_ref)
    copies[0].wait()
    for i in range(w_ref.shape[0]):
        qkv = mm(w_ref[i], h, NT) + bias[i * 3 * HD : (i + 1) * 3 * HD]
        for c in range(3):
            out_ref[i, c] = qkv[c * HD : (c + 1) * HD].astype(BF)
    copies[1].wait()


def kernel_spatial(own_ref, w_ref, mod_ref, b_ref, *refs):
    x_refs, (out_ref, part_ref) = refs[:-2], refs[-2:]
    heads = w_ref.shape[0]
    space, _ = coordinates()
    patches, frames, _ = x_refs[0].shape
    spaces = len(x_refs) + 1
    bias = bias_column(b_ref)
    rows = [spatial_rows(flat(x_ref), mod_ref, frames) for x_ref in x_refs]
    for i in range(heads):
        for j in range(spaces - 1):
            qkv = mm(w_ref[i], rows[j], NT) + bias[i * 3 * HD : (i + 1) * 3 * HD]
            for c in range(3):
                part_ref[j, i, c] = qkv[c * HD : (c + 1) * HD].astype(BF)
    by_frame = []
    for f in range(frames):
        cols = slice(f * patches, (f + 1) * patches)
        done = []
        for i in range(heads):
            q_t, k_t, v_t = (
                jnp.concatenate(
                    [own_ref[i, c, :, cols]] + [part_ref[j, i, c, :, cols] for j in range(spaces - 1)],
                    axis=1,
                )
                for c in range(3)
            )
            done.append(attend(q_t, k_t, v_t))
        by_frame.append(jnp.concatenate(done, axis=0).astype(BF))
    back = by_patch_first(patches * frames, frames)
    for j in range(spaces):
        mine = jnp.concatenate([o[:, j * patches : (j + 1) * patches] for o in by_frame], axis=1)
        out_ref[lax.rem(space - j + spaces, spaces)] = mm(back, mine, NT).astype(BF)


def middle(tokens, parts, outbias, gate):
    summed = parts[0].astype(BF).astype(F32)
    for part in parts[1:]:
        summed = summed + part.astype(BF).astype(F32)
    return (tokens.astype(F32) + gate * (summed + outbias)).astype(BF)


def temporal_mask(rows, size, frames):
    def place(row):
        device, within = lax.div(row, frames * size), lax.rem(row, frames * size)
        return device * frames + lax.rem(within, frames), lax.div(within, frames)

    key_frame, key_patch = place(column(rows))
    query_frame, query_patch = place(line(rows))
    code_key = key_patch * 4 * WIN * rows + key_frame
    code_query = query_patch * 4 * WIN * rows + query_frame
    back = code_query - code_key
    return (back >= 0) & (back < WIN)


def temporal_head(w, b, h, mask):
    qkv = (mm(w, h, NT) + b).astype(BF)
    return attend(qkv[0:HD], qkv[HD : 2 * HD], qkv[2 * HD : 3 * HD], mask)


def parts_of(o, pieces, core):
    half = pieces[1].shape[0]
    parts = [mm(o(0), pieces[0][...])]
    for k in range(1, (len(pieces) + 1) // 2):
        first, second = pieces[2 * k - 1][...], pieces[2 * k][...]
        rows = jnp.concatenate([jnp.where(core == 0, first, second), jnp.where(core == 0, second, first)])
        parts.append(mm(o(k), rows))
    return parts


def kernel_temporal(o_ref, x_ref, w_ref, outbias_ref, mod_ref, b_ref, *refs, size, frames):
    space, core = coordinates()
    pieces, (h_ref, out_ref) = refs[:-2], refs[-2:]
    spaces, rows, _ = o_ref.shape
    mask = temporal_mask(rows, size, frames)
    parts = parts_of(lambda k: o_ref[lax.rem(space - k + spaces, spaces)], pieces, core)
    y = middle(flat(x_ref), parts, outbias_ref[...].reshape(1, -1), mod_ref[2:3, :])
    h = modulated(y.astype(F32), mod_ref[3:4, :], mod_ref[4:5, :]).astype(BF)
    h_ref[...] = h
    bias = bias_column(b_ref)
    for i in range(w_ref.shape[0]):
        out_ref[i] = temporal_head(w_ref[i], bias[i * 3 * HD : (i + 1) * 3 * HD], h, mask)


def kernel_rest(h_ref, own_ref, *refs, size, frames, spaces):
    b_refs, w_refs, (out_ref, turn_ref) = refs[: spaces - 1], refs[spaces - 1 : -2], refs[-2:]
    space, core = coordinates()
    h = h_ref[...]
    rows = h.shape[0]
    mask = temporal_mask(rows, size, frames)
    heads = own_ref.shape[0]
    half = heads // 2
    for i in range(heads):
        turn_ref[space * heads + i] = own_ref[i]
    for n, w_ref in enumerate(w_refs):
        shift = n // 2 + 1
        bias = bias_column(b_refs[shift - 1])
        second = (core == 0) == (n % 2 == 1)
        within = jnp.where(second, half, 0)
        group = lax.rem(space - shift + spaces, spaces)
        bias = jnp.where(second, bias[half * 3 * HD :], bias[: half * 3 * HD])
        for i in range(half):
            o_t = temporal_head(w_ref[i], bias[i * 3 * HD : (i + 1) * 3 * HD], h, mask)
            turn_ref[group * heads + within + i] = o_t
    out_ref[...] = turn_ref[...].reshape(-1, rows).T.astype(BF)


def kernel_home(o_own_ref, x_ref, outbias_ref, mod_ref, *refs):
    space, core = coordinates()
    spaces = o_own_ref.shape[0]
    o_refs, pieces, out_ref = refs[: spaces - 1], refs[spaces - 1 : -1], refs[-1]
    parts = parts_of(lambda k: o_refs[k - 1][...] if k else o_own_ref[space], pieces, core)
    out_ref[...] = middle(flat(x_ref), parts, outbias_ref[...].reshape(1, -1), mod_ref[2:3, :])


def kernel_final(o_ref, y_ref, w_ref, outbias_ref, mod_ref, out_ref):
    final = mm(o_ref[...], w_ref[...]) + outbias_ref[...].reshape(1, -1)
    result = (y_ref[...].astype(F32) + mod_ref[5:6, :] * final).astype(BF)
    out_ref[...] = result.reshape(out_ref.shape)


def call(kernel, out_shape, count, flops, nbytes, scratch=(), in_any=(), params=PARAMS):
    return pl.pallas_call(
        kernel,
        out_shape=jax.ShapeDtypeStruct(out_shape, BF),
        in_specs=[ANY if i in in_any else VMEM for i in range(count)],
        out_specs=VMEM,
        scratch_shapes=list(scratch),
        compiler_params=params,
        cost_estimate=pl.CostEstimate(flops=int(flops), bytes_accessed=int(nbytes), transcendentals=0),
    )


def local(
    tokens,
    modulation,
    qkv_spatial,
    bias_spatial,
    out_spatial,
    outbias_spatial,
    qkv_temporal,
    bias_temporal,
    out_temporal,
    outbias_temporal,
):
    patches, frames, width = tokens.shape
    spaces, times = lax.axis_size("space"), lax.axis_size("tm")
    space = lax.axis_index("space")
    heads = qkv_spatial.shape[1] // (3 * HD)
    cols = heads * HD
    half = heads // 2
    size = patches // times
    rows = patches * frames

    def across(array, k):
        return lax.ppermute(array, "space", [(i, (i + k) % spaces) for i in range(spaces)])

    def beside(array):
        return lax.ppermute(array, "tm", [(i, i ^ 1) for i in range(times)])

    arrived = [across(tokens, k) for k in range(1, spaces)]

    w_spatial = qkv_spatial.T.reshape(heads, 3 * HD, width)
    w_temporal = qkv_temporal.T.reshape(heads, 3 * HD, width)
    own, my_heads = pl.pallas_call(
        kernel_qkv,
        out_shape=tuple(
            jax.ShapeDtypeStruct(a, BF) for a in ((heads, 3, HD, rows), (half, 3 * HD, width))
        ),
        in_specs=[VMEM] + [ANY] * 2 + [VMEM] * 2,
        out_specs=(VMEM, VMEM),
        scratch_shapes=[pltpu.VMEM(w_spatial.shape, BF), pltpu.SemaphoreType.DMA((2,))],
        compiler_params=PARAMS,
        cost_estimate=pl.CostEstimate(
            flops=2 * rows * width * cols * 3, bytes_accessed=3 * 10**6, transcendentals=0
        ),
    )(tokens, w_spatial, w_temporal, modulation, bias_spatial)

    spread = lax.all_to_all(tokens.reshape(times, size, frames, width), "tm", 0, 0, tiled=True)

    other_bias = [across(bias_temporal, k) for k in range(1, spaces)]
    my_out = lax.dynamic_slice_in_dim(out_spatial, lax.rem(lax.axis_index("tm"), 2) * half * HD, half * HD, 0)
    arrived = [after((a,), own, *other_bias)[0] for a in arrived]
    direct_out = [across(my_out, k) for k in range(1, spaces)]

    o_all = call(
        kernel_spatial,
        (spaces, rows, cols),
        4 + len(arrived),
        1e10,
        4e6,
        [
            pltpu.VMEM((spaces - 1, heads, 3, HD, rows), BF),
        ],
        params=SMALL,
    )(own, w_spatial, modulation, bias_spatial, *arrived)

    (my_heads,) = after((my_heads,), *arrived)
    direct_heads = [across(my_heads, k) for k in range(1, spaces)]
    out_pieces = [out_spatial]
    for a in direct_out:
        out_pieces += [a, beside(a)]

    o_here = lax.all_to_all(
        after((o_all,), spread, *out_pieces)[0].reshape(spaces * times, frames * size, cols), ("space", "tm"), 0, 0, tiled=True
    ).reshape(spaces, rows, cols)
    other_heads = []
    for a in direct_heads:
        other_heads += [a, beside(after((a,), o_here)[0])]

    o_home = [
        across(lax.dynamic_index_in_dim(o_all, (space + k) % spaces, 0, keepdims=False), k)
        for k in range(1, spaces)
    ]

    y_home = call(
        kernel_home,
        (rows, width),
        4 + len(o_home) + len(out_pieces),
        2 * rows * width * cols * spaces,
        3e6,
        params=SMALL,
    )(o_all, tokens, outbias_spatial, modulation, *o_home, *out_pieces)
    x_here = spread.reshape(rows // frames, frames, width)
    h_here, o_own = pl.pallas_call(
        functools.partial(kernel_temporal, size=size, frames=frames),
        out_shape=(jax.ShapeDtypeStruct((rows, width), BF), jax.ShapeDtypeStruct((heads, HD, rows), F32)),
        in_specs=[VMEM] * (6 + len(out_pieces)),
        out_specs=(VMEM, VMEM),
        compiler_params=SMALL,
        cost_estimate=pl.CostEstimate(
            flops=2 * rows * width * cols * (3 + spaces), bytes_accessed=5 * 10**6, transcendentals=0
        ),
    )(o_here, x_here, w_temporal, outbias_spatial, modulation, bias_temporal, *out_pieces)
    o_t = call(
        functools.partial(kernel_rest, size=size, frames=frames, spaces=spaces),
        (rows, spaces * cols),
        1 + spaces + len(other_heads),
        2 * rows * width * cols * 3 * (spaces - 1),
        5e6,
        [
            pltpu.VMEM((spaces * heads, HD, rows), F32),
        ],
        params=SMALL,
    )(h_here, o_own, *other_bias, *other_heads)
    o_t = o_t.reshape(times, frames * size, spaces * cols)
    o_final = lax.all_to_all(o_t, "tm", 0, 0, tiled=True).reshape(rows, spaces * cols)

    return call(
        kernel_final, (patches, frames, width), 5, 2 * rows * width * cols * spaces, 3e6, params=SMALL
    )(o_final, y_home, out_temporal, outbias_temporal, modulation)


def solution(mesh):
    return jax.shard_map(
        local,
        mesh=mesh,
        in_specs=(
            P("space", ("grp", "tm"), None),
            P("grp", None),
            P(None, "space"),
            P("space"),
            P("space", None),
            P(),
            P(None, "space"),
            P("space"),
            P(),
            P(),
        ),
        out_specs=P("space", ("grp", "tm"), None),
        check_vma=False,
    )
```

```python
import functools
import math

import jax
import jax.numpy as jnp
from jax import lax
from jax.experimental import pallas as pl
from jax.experimental.pallas import tpu as pltpu
from jax.sharding import PartitionSpec as P

HD = 72
WIN = 16
BF = jnp.bfloat16
F32 = jnp.float32
EXP2_SCALE = 1.0 / (math.sqrt(HD) * math.log(2.0))

VMEM = pl.BlockSpec(memory_space=pltpu.VMEM)
ANY = pl.BlockSpec(memory_space=pl.ANY)
SMALL = pltpu.CompilerParams(vmem_limit_bytes=16 * 1024 * 1024)
PARAMS = pltpu.CompilerParams(vmem_limit_bytes=63 * 1024 * 1024)

NT = (((1,), (1,)), ((), ()))
TN = (((0,), (0,)), ((), ()))


def mm(a, b, dims=(((1,), (0,)), ((), ()))):
    return lax.dot_general(a, b, dims, preferred_element_type=F32)


def modulated(values, offset_vec, scaling):
    center = jnp.mean(values, axis=-1, keepdims=True)
    moved = values - center
    spread = jnp.mean(moved * moved, axis=-1, keepdims=True)
    return moved * lax.rsqrt(spread + 1e-06) * (1.0 + scaling) + offset_vec


def attend(q_t, k_t, v_t, mask=None):
    scores = mm(k_t, q_t, TN)
    if mask is not None:
        scores = jnp.where(mask, scores, F32(-1e30))
    highest = jnp.max(scores, axis=0, keepdims=True)
    expon = jnp.exp2((scores - highest) * F32(EXP2_SCALE))
    total = jnp.sum(expon, axis=0, keepdims=True)
    return mm(v_t, expon.astype(BF)) * (1.0 / total)


def after(arrays, *others):
    return lax.optimization_barrier((*arrays, *others))[: len(arrays)]


def flat(ref, *index):
    block = ref[index] if index else ref[...]
    return block.reshape(-1, block.shape[-1])


def column(rows):
    return lax.broadcasted_iota(jnp.int32, (rows, 1), 0)


def line(rows):
    return lax.broadcasted_iota(jnp.int32, (1, rows), 1)


def chosen(source, rows):
    return (source == line(rows)).astype(F32).astype(BF)


def by_frame_first(rows, frames):
    r = column(rows)
    return chosen(lax.rem(r, rows // frames) * frames + lax.div(r, rows // frames), rows)


def by_patch_first(rows, frames):
    r = column(rows)
    return chosen(lax.rem(r, frames) * (rows // frames) + lax.div(r, frames), rows)


def bias_column(b_ref):
    count = b_ref.shape[0]
    return jnp.broadcast_to(b_ref[...].reshape(1, count), (8, count)).T[:, 0:1]


def spatial_rows(x, mod_ref, frames):
    h = modulated(x.astype(F32), mod_ref[0:1, :], mod_ref[1:2, :]).astype(BF)
    return mm(by_frame_first(x.shape[0], frames), h).astype(BF)


def fetch(sources, targets, sems):
    copies = [pltpu.make_async_copy(a, b, sems.at[i]) for i, (a, b) in enumerate(zip(sources, targets))]
    for copy in copies:
        copy.start()
    return copies


def coordinates():
    return lax.axis_index("space"), lax.rem(lax.axis_index("tm"), 2)


def kernel_qkv(x_ref, w_ref, w_other_hbm, mod_ref, b_ref, out_ref, heads_ref, sems):
    _, core = coordinates()
    half = heads_ref.shape[0]
    copies = fetch((w_other_hbm.at[pl.ds(core * half, half)],), (heads_ref,), sems)
    h = spatial_rows(flat(x_ref), mod_ref, x_ref.shape[1])
    bias = bias_column(b_ref)
    for i in range(w_ref.shape[0]):
        qkv = mm(w_ref[i], h, NT) + bias[i * 3 * HD : (i + 1) * 3 * HD]
        for c in range(3):
            out_ref[i, c] = qkv[c * HD : (c + 1) * HD].astype(BF)
    copies[0].wait()


def kernel_spatial(own_ref, w_ref, mod_ref, b_ref, *refs):
    x_refs, (out_ref, part_ref) = refs[:-2], refs[-2:]
    heads = w_ref.shape[0]
    space, _ = coordinates()
    patches, frames, _ = x_refs[0].shape
    spaces = len(x_refs) + 1
    bias = bias_column(b_ref)
    rows = [spatial_rows(flat(x_ref), mod_ref, frames) for x_ref in x_refs]
    for i in range(heads):
        for j in range(spaces - 1):
            qkv = mm(w_ref[i], rows[j], NT) + bias[i * 3 * HD : (i + 1) * 3 * HD]
            for c in range(3):
                part_ref[j, i, c] = qkv[c * HD : (c + 1) * HD].astype(BF)
    by_frame = []
    for f in range(frames):
        cols = slice(f * patches, (f + 1) * patches)
        done = []
        for i in range(heads):
            q_t, k_t, v_t = (
                jnp.concatenate(
                    [own_ref[i, c, :, cols]] + [part_ref[j, i, c, :, cols] for j in range(spaces - 1)],
                    axis=1,
                )
                for c in range(3)
            )
            done.append(attend(q_t, k_t, v_t))
        by_frame.append(jnp.concatenate(done, axis=0).astype(BF))
    back = by_patch_first(patches * frames, frames)
    for j in range(spaces):
        mine = jnp.concatenate([o[:, j * patches : (j + 1) * patches] for o in by_frame], axis=1)
        out_ref[lax.rem(space - j + spaces, spaces)] = mm(back, mine, NT).astype(BF)


def middle(tokens, parts, outbias, gate):
    summed = parts[0].astype(BF).astype(F32)
    for part in parts[1:]:
        summed = summed + part.astype(BF).astype(F32)
    return (tokens.astype(F32) + gate * (summed + outbias)).astype(BF)


def temporal_mask(rows, size, frames):
    def place(row):
        device, within = lax.div(row, frames * size), lax.rem(row, frames * size)
        return device * frames + lax.rem(within, frames), lax.div(within, frames)

    key_frame, key_patch = place(column(rows))
    query_frame, query_patch = place(line(rows))
    code_key = key_patch * 4 * WIN * rows + key_frame
    code_query = query_patch * 4 * WIN * rows + query_frame
    back = code_query - code_key
    return (back >= 0) & (back < WIN)


def temporal_head(w, b, h, mask):
    qkv = (mm(w, h, NT) + b).astype(BF)
    return attend(qkv[0:HD], qkv[HD : 2 * HD], qkv[2 * HD : 3 * HD], mask)


def parts_of(o, pieces, core):
    half = pieces[1].shape[0]
    parts = [mm(o(0), pieces[0][...])]
    for k in range(1, (len(pieces) + 1) // 2):
        first, second = pieces[2 * k - 1][...], pieces[2 * k][...]
        rows = jnp.concatenate([jnp.where(core == 0, first, second), jnp.where(core == 0, second, first)])
        parts.append(mm(o(k), rows))
    return parts


def kernel_temporal(o_ref, x_ref, w_ref, outbias_ref, mod_ref, b_ref, *refs, size, frames):
    space, core = coordinates()
    pieces, (h_ref, out_ref) = refs[:-2], refs[-2:]
    spaces, rows, _ = o_ref.shape
    mask = temporal_mask(rows, size, frames)
    parts = parts_of(lambda k: o_ref[lax.rem(space - k + spaces, spaces)], pieces, core)
    y = middle(flat(x_ref), parts, outbias_ref[...].reshape(1, -1), mod_ref[2:3, :])
    h = modulated(y.astype(F32), mod_ref[3:4, :], mod_ref[4:5, :]).astype(BF)
    h_ref[...] = h
    bias = bias_column(b_ref)
    for i in range(w_ref.shape[0]):
        out_ref[i] = temporal_head(w_ref[i], bias[i * 3 * HD : (i + 1) * 3 * HD], h, mask)


def kernel_rest(h_ref, own_ref, *refs, size, frames, spaces):
    b_refs, w_refs, (out_ref, turn_ref) = refs[: spaces - 1], refs[spaces - 1 : -2], refs[-2:]
    space, core = coordinates()
    h = h_ref[...]
    rows = h.shape[0]
    mask = temporal_mask(rows, size, frames)
    heads = own_ref.shape[0]
    half = heads // 2
    for i in range(heads):
        turn_ref[space * heads + i] = own_ref[i]
    for n, w_ref in enumerate(w_refs):
        shift = n // 2 + 1
        bias = bias_column(b_refs[shift - 1])
        second = (core == 0) == (n % 2 == 1)
        within = jnp.where(second, half, 0)
        group = lax.rem(space - shift + spaces, spaces)
        bias = jnp.where(second, bias[half * 3 * HD :], bias[: half * 3 * HD])
        for i in range(half):
            o_t = temporal_head(w_ref[i], bias[i * 3 * HD : (i + 1) * 3 * HD], h, mask)
            turn_ref[group * heads + within + i] = o_t
    out_ref[...] = turn_ref[...].reshape(-1, rows).T.astype(BF)


def kernel_home(o_own_ref, x_ref, outbias_ref, mod_ref, *refs):
    space, core = coordinates()
    spaces = o_own_ref.shape[0]
    o_refs, pieces, out_ref = refs[: spaces - 1], refs[spaces - 1 : -1], refs[-1]
    parts = parts_of(lambda k: o_refs[k - 1][...] if k else o_own_ref[space], pieces, core)
    out_ref[...] = middle(flat(x_ref), parts, outbias_ref[...].reshape(1, -1), mod_ref[2:3, :])


def kernel_final(o_ref, y_ref, w_ref, outbias_ref, mod_ref, out_ref):
    final = mm(o_ref[...], w_ref[...]) + outbias_ref[...].reshape(1, -1)
    result = (y_ref[...].astype(F32) + mod_ref[5:6, :] * final).astype(BF)
    out_ref[...] = result.reshape(out_ref.shape)


def call(kernel, out_shape, count, flops, nbytes, scratch=(), in_any=(), params=PARAMS):
    return pl.pallas_call(
        kernel,
        out_shape=jax.ShapeDtypeStruct(out_shape, BF),
        in_specs=[ANY if i in in_any else VMEM for i in range(count)],
        out_specs=VMEM,
        scratch_shapes=list(scratch),
        compiler_params=params,
        cost_estimate=pl.CostEstimate(flops=int(flops), bytes_accessed=int(nbytes), transcendentals=0),
    )


def local(
    tokens,
    modulation,
    qkv_spatial,
    bias_spatial,
    out_spatial,
    outbias_spatial,
    qkv_temporal,
    bias_temporal,
    out_temporal,
    outbias_temporal,
):
    patches, frames, width = tokens.shape
    spaces, times = lax.axis_size("space"), lax.axis_size("tm")
    space = lax.axis_index("space")
    heads = qkv_spatial.shape[1] // (3 * HD)
    cols = heads * HD
    half = heads // 2
    size = patches // times
    rows = patches * frames

    def across(array, k):
        return lax.ppermute(array, "space", [(i, (i + k) % spaces) for i in range(spaces)])

    def beside(array):
        return lax.ppermute(array, "tm", [(i, i ^ 1) for i in range(times)])

    arrived = [across(tokens, k) for k in range(1, spaces)]

    w_spatial = qkv_spatial.T.reshape(heads, 3 * HD, width)
    w_temporal = qkv_temporal.T.reshape(heads, 3 * HD, width)
    own, my_heads = pl.pallas_call(
        kernel_qkv,
        out_shape=tuple(
            jax.ShapeDtypeStruct(a, BF) for a in ((heads, 3, HD, rows), (half, 3 * HD, width))
        ),
        in_specs=[VMEM] * 2 + [ANY] + [VMEM] * 2,
        out_specs=(VMEM, VMEM),
        scratch_shapes=[pltpu.SemaphoreType.DMA((1,))],
        compiler_params=SMALL,
        cost_estimate=pl.CostEstimate(
            flops=2 * rows * width * cols * 3, bytes_accessed=3 * 10**6, transcendentals=0
        ),
    )(tokens, w_spatial, w_temporal, modulation, bias_spatial)

    spread = lax.all_to_all(tokens.reshape(times, size, frames, width), "tm", 0, 0, tiled=True)

    other_bias = [across(bias_temporal, k) for k in range(1, spaces)]
    my_out = lax.dynamic_slice_in_dim(out_spatial, lax.rem(lax.axis_index("tm"), 2) * half * HD, half * HD, 0)
    arrived = [after((a,), own, *other_bias)[0] for a in arrived]
    direct_out = [across(my_out, k) for k in range(1, spaces)]

    o_all = call(
        kernel_spatial,
        (spaces, rows, cols),
        4 + len(arrived),
        1e10,
        4e6,
        [
            pltpu.VMEM((spaces - 1, heads, 3, HD, rows), BF),
        ],
        params=SMALL,
    )(own, w_spatial, modulation, bias_spatial, *arrived)

    (my_heads,) = after((my_heads,), *arrived)
    direct_heads = [across(my_heads, k) for k in range(1, spaces)]
    out_pieces = [out_spatial]
    for a in direct_out:
        out_pieces += [a, beside(a)]

    o_here = lax.all_to_all(
        after((o_all,), spread, *out_pieces)[0].reshape(spaces * times, frames * size, cols), ("space", "tm"), 0, 0, tiled=True
    ).reshape(spaces, rows, cols)
    other_heads = []
    for a in direct_heads:
        other_heads += [a, beside(after((a,), o_here)[0])]

    o_home = [
        across(lax.dynamic_index_in_dim(o_all, (space + k) % spaces, 0, keepdims=False), k)
        for k in range(1, spaces)
    ]

    y_home = call(
        kernel_home,
        (rows, width),
        4 + len(o_home) + len(out_pieces),
        2 * rows * width * cols * spaces,
        3e6,
        params=SMALL,
    )(o_all, tokens, outbias_spatial, modulation, *o_home, *out_pieces)
    x_here = spread.reshape(rows // frames, frames, width)
    h_here, o_own = pl.pallas_call(
        functools.partial(kernel_temporal, size=size, frames=frames),
        out_shape=(jax.ShapeDtypeStruct((rows, width), BF), jax.ShapeDtypeStruct((heads, HD, rows), F32)),
        in_specs=[VMEM] * (6 + len(out_pieces)),
        out_specs=(VMEM, VMEM),
        compiler_params=SMALL,
        cost_estimate=pl.CostEstimate(
            flops=2 * rows * width * cols * (3 + spaces), bytes_accessed=5 * 10**6, transcendentals=0
        ),
    )(o_here, x_here, w_temporal, outbias_spatial, modulation, bias_temporal, *out_pieces)
    o_t = call(
        functools.partial(kernel_rest, size=size, frames=frames, spaces=spaces),
        (rows, spaces * cols),
        1 + spaces + len(other_heads),
        2 * rows * width * cols * 3 * (spaces - 1),
        5e6,
        [
            pltpu.VMEM((spaces * heads, HD, rows), F32),
        ],
        params=SMALL,
    )(h_here, o_own, *other_bias, *other_heads)
    o_t = o_t.reshape(times, frames * size, spaces * cols)
    o_final = lax.all_to_all(o_t, "tm", 0, 0, tiled=True).reshape(rows, spaces * cols)

    return call(
        kernel_final, (patches, frames, width), 5, 2 * rows * width * cols * spaces, 3e6, params=SMALL
    )(o_final, y_home, out_temporal, outbias_temporal, modulation)


def solution(mesh):
    return jax.shard_map(
        local,
        mesh=mesh,
        in_specs=(
            P("space", ("grp", "tm"), None),
            P("grp", None),
            P(None, "space"),
            P("space"),
            P("space", None),
            P(),
            P(None, "space"),
            P("space"),
            P(),
            P(),
        ),
        out_specs=P("space", ("grp", "tm"), None),
        check_vma=False,
    )
```

```python
import functools
import math

import jax
import jax.numpy as jnp
from jax import lax
from jax.experimental import pallas as pl
from jax.experimental.pallas import tpu as pltpu
from jax.sharding import PartitionSpec as P

HD = 72
WIN = 16
BF = jnp.bfloat16
F32 = jnp.float32
EXP2_SCALE = 1.0 / (math.sqrt(HD) * math.log(2.0))

VMEM = pl.BlockSpec(memory_space=pltpu.VMEM)
ANY = pl.BlockSpec(memory_space=pl.ANY)
SMALL = pltpu.CompilerParams(vmem_limit_bytes=16 * 1024 * 1024)
PARAMS = pltpu.CompilerParams(vmem_limit_bytes=63 * 1024 * 1024)

NT = (((1,), (1,)), ((), ()))
TN = (((0,), (0,)), ((), ()))


def mm(a, b, dims=(((1,), (0,)), ((), ()))):
    return lax.dot_general(a, b, dims, preferred_element_type=F32)


def modulated(values, offset_vec, scaling):
    center = jnp.mean(values, axis=-1, keepdims=True)
    moved = values - center
    spread = jnp.mean(moved * moved, axis=-1, keepdims=True)
    return moved * lax.rsqrt(spread + 1e-06) * (1.0 + scaling) + offset_vec


def attend(q_t, k_t, v_t, mask=None):
    scores = mm(k_t, q_t, TN)
    if mask is not None:
        scores = jnp.where(mask, scores, F32(-1e30))
    highest = jnp.max(scores, axis=0, keepdims=True)
    expon = jnp.exp2((scores - highest) * F32(EXP2_SCALE))
    total = jnp.sum(expon, axis=0, keepdims=True)
    return mm(v_t, expon.astype(BF)) * (1.0 / total)


def after(arrays, *others):
    return lax.optimization_barrier((*arrays, *others))[: len(arrays)]


def flat(ref, *index):
    block = ref[index] if index else ref[...]
    return block.reshape(-1, block.shape[-1])


def column(rows):
    return lax.broadcasted_iota(jnp.int32, (rows, 1), 0)


def line(rows):
    return lax.broadcasted_iota(jnp.int32, (1, rows), 1)


def chosen(source, rows):
    return (source == line(rows)).astype(F32).astype(BF)


def by_frame_first(rows, frames):
    r = column(rows)
    return chosen(lax.rem(r, rows // frames) * frames + lax.div(r, rows // frames), rows)


def by_patch_first(rows, frames):
    r = column(rows)
    return chosen(lax.rem(r, frames) * (rows // frames) + lax.div(r, frames), rows)


def bias_column(b_ref):
    count = b_ref.shape[0]
    return jnp.broadcast_to(b_ref[...].reshape(1, count), (8, count)).T[:, 0:1]


def spatial_rows(x, mod_ref, frames):
    h = modulated(x.astype(F32), mod_ref[0:1, :], mod_ref[1:2, :]).astype(BF)
    return mm(by_frame_first(x.shape[0], frames), h).astype(BF)


def fetch(sources, targets, sems):
    copies = [pltpu.make_async_copy(a, b, sems.at[i]) for i, (a, b) in enumerate(zip(sources, targets))]
    for copy in copies:
        copy.start()
    return copies


def hops_of(heads, times):
    return [hop for hop in (2, 1) if heads % (2 * hop) == 0 and times % (2 * hop) == 0]


def masks_of(hops):
    masks = [0]
    for hop in hops:
        masks += [mask ^ hop for mask in masks]
    return masks


def coordinates(share):
    return lax.axis_index("space"), lax.rem(lax.axis_index("tm"), share)


def kernel_qkv(x_ref, w_hbm, w_other_hbm, mod_ref, b_ref, out_ref, heads_ref, w_ref, sems):
    part = heads_ref.shape[0]
    _, turn = coordinates(w_ref.shape[0] // part)
    copies = fetch((w_hbm, w_other_hbm.at[pl.ds(turn * part, part)]), (w_ref, heads_ref), sems)
    h = spatial_rows(flat(x_ref), mod_ref, x_ref.shape[1])
    bias = bias_column(b_ref)
    copies[0].wait()
    for i in range(w_ref.shape[0]):
        qkv = mm(w_ref[i], h, NT) + bias[i * 3 * HD : (i + 1) * 3 * HD]
        for c in range(3):
            out_ref[i, c] = qkv[c * HD : (c + 1) * HD].astype(BF)
    copies[1].wait()


def kernel_spatial(own_ref, w_ref, mod_ref, b_ref, *refs):
    x_refs, (out_ref, part_ref) = refs[:-2], refs[-2:]
    heads = w_ref.shape[0]
    space = lax.axis_index("space")
    patches, frames, _ = x_refs[0].shape
    spaces = len(x_refs) + 1
    bias = bias_column(b_ref)
    rows = [spatial_rows(flat(x_ref), mod_ref, frames) for x_ref in x_refs]
    for i in range(heads):
        for j in range(spaces - 1):
            qkv = mm(w_ref[i], rows[j], NT) + bias[i * 3 * HD : (i + 1) * 3 * HD]
            for c in range(3):
                part_ref[j, i, c] = qkv[c * HD : (c + 1) * HD].astype(BF)
    by_frame = []
    for f in range(frames):
        cols = slice(f * patches, (f + 1) * patches)
        done = []
        for i in range(heads):
            q_t, k_t, v_t = (
                jnp.concatenate(
                    [own_ref[i, c, :, cols]] + [part_ref[j, i, c, :, cols] for j in range(spaces - 1)],
                    axis=1,
                )
                for c in range(3)
            )
            done.append(attend(q_t, k_t, v_t))
        by_frame.append(jnp.concatenate(done, axis=0).astype(BF))
    back = by_patch_first(patches * frames, frames)
    for j in range(spaces):
        mine = jnp.concatenate([o[:, j * patches : (j + 1) * patches] for o in by_frame], axis=1)
        out_ref[lax.rem(space - j + spaces, spaces)] = mm(back, mine, NT).astype(BF)


def middle(tokens, parts, outbias, gate):
    summed = parts[0].astype(BF).astype(F32)
    for part in parts[1:]:
        summed = summed + part.astype(BF).astype(F32)
    return (tokens.astype(F32) + gate * (summed + outbias)).astype(BF)


def temporal_mask(rows, size, frames):
    def place(row):
        device, within = lax.div(row, frames * size), lax.rem(row, frames * size)
        return device * frames + lax.rem(within, frames), lax.div(within, frames)

    key_frame, key_patch = place(column(rows))
    query_frame, query_patch = place(line(rows))
    code_key = key_patch * 4 * WIN * rows + key_frame
    code_query = query_patch * 4 * WIN * rows + query_frame
    back = code_query - code_key
    return (back >= 0) & (back < WIN)


def temporal_head(w, b, h, mask):
    qkv = (mm(w, h, NT) + b).astype(BF)
    return attend(qkv[0:HD], qkv[HD : 2 * HD], qkv[2 * HD : 3 * HD], mask)


def parts_of(o, own_w_ref, pieces, w_ref, masks):
    share = len(masks)
    _, turn = coordinates(share)
    rows = pieces[0].shape[0]
    parts = [mm(o(0), own_w_ref[...])]
    for k in range(len(pieces) // share):
        for mask, piece in zip(masks, pieces[k * share : (k + 1) * share]):
            w_ref[turn ^ mask] = piece[...]
        columns = o(k + 1)
        parts.append(sum(mm(columns[:, q * rows : (q + 1) * rows], w_ref[q]) for q in range(share)))
    return parts


def kernel_temporal(o_ref, x_ref, w_ref, outbias_ref, mod_ref, b_ref, own_w_ref, *refs, size, frames, masks):
    space = lax.axis_index("space")
    pieces, (h_ref, out_ref, piece_ref) = refs[:-3], refs[-3:]
    spaces, rows, _ = o_ref.shape
    mask = temporal_mask(rows, size, frames)
    parts = parts_of(lambda k: o_ref[lax.rem(space - k + spaces, spaces)], own_w_ref, pieces, piece_ref, masks)
    y = middle(flat(x_ref), parts, outbias_ref[...].reshape(1, -1), mod_ref[2:3, :])
    h = modulated(y.astype(F32), mod_ref[3:4, :], mod_ref[4:5, :]).astype(BF)
    h_ref[...] = h
    bias = bias_column(b_ref)
    for i in range(w_ref.shape[0]):
        out_ref[i] = temporal_head(w_ref[i], bias[i * 3 * HD : (i + 1) * 3 * HD], h, mask)


def kernel_rest(h_ref, own_ref, *refs, size, frames, spaces, masks):
    b_refs, w_refs, (out_ref, turn_ref, bias_ref) = refs[: spaces - 1], refs[spaces - 1 : -3], refs[-3:]
    share = len(masks)
    space, turn = coordinates(share)
    h = h_ref[...]
    rows = h.shape[0]
    mask = temporal_mask(rows, size, frames)
    heads = own_ref.shape[0]
    part = heads // share
    for i in range(heads):
        turn_ref[space * heads + i] = own_ref[i]
    for k in range(spaces - 1):
        bias = bias_column(b_refs[k])
        for i in range(heads):
            bias_ref[i] = bias[i * 3 * HD : (i + 1) * 3 * HD]
        group = lax.rem(space - k - 1 + spaces, spaces)
        for n, w_ref in zip(masks, w_refs[k * share : (k + 1) * share]):
            for i in range(part):
                head = (turn ^ n) * part + i
                turn_ref[group * heads + head] = temporal_head(w_ref[i], bias_ref[head], h, mask)
    out_ref[...] = turn_ref[...].reshape(-1, rows).T.astype(BF)


def kernel_home(o_own_ref, x_ref, outbias_ref, mod_ref, own_w_ref, *refs, masks):
    space = lax.axis_index("space")
    spaces = o_own_ref.shape[0]
    o_refs, pieces, (out_ref, piece_ref) = refs[: spaces - 1], refs[spaces - 1 : -2], refs[-2:]
    parts = parts_of(
        lambda k: o_refs[k - 1][...] if k else o_own_ref[space], own_w_ref, pieces, piece_ref, masks
    )
    out_ref[...] = middle(flat(x_ref), parts, outbias_ref[...].reshape(1, -1), mod_ref[2:3, :])


def kernel_final(o_ref, y_ref, w_ref, outbias_ref, mod_ref, out_ref):
    final = mm(o_ref[...], w_ref[...]) + outbias_ref[...].reshape(1, -1)
    result = (y_ref[...].astype(F32) + mod_ref[5:6, :] * final).astype(BF)
    out_ref[...] = result.reshape(out_ref.shape)


def call(kernel, out_shape, count, flops, nbytes, scratch=(), in_any=(), params=PARAMS):
    return pl.pallas_call(
        kernel,
        out_shape=jax.ShapeDtypeStruct(out_shape, BF),
        in_specs=[ANY if i in in_any else VMEM for i in range(count)],
        out_specs=VMEM,
        scratch_shapes=list(scratch),
        compiler_params=params,
        cost_estimate=pl.CostEstimate(flops=int(flops), bytes_accessed=int(nbytes), transcendentals=0),
    )


def local(
    tokens,
    modulation,
    qkv_spatial,
    bias_spatial,
    out_spatial,
    outbias_spatial,
    qkv_temporal,
    bias_temporal,
    out_temporal,
    outbias_temporal,
):
    patches, frames, width = tokens.shape
    spaces, times = lax.axis_size("space"), lax.axis_size("tm")
    space = lax.axis_index("space")
    heads = qkv_spatial.shape[1] // (3 * HD)
    cols = heads * HD
    out_hops = hops_of(heads, times)
    out_masks = masks_of(out_hops)
    out_part = heads // len(out_masks) * HD
    hops = out_hops[-1:]
    masks = masks_of(hops)
    part = heads // len(masks)
    size = patches // times
    rows = patches * frames

    def across(array, k):
        return lax.ppermute(array, "space", [(i, (i + k) % spaces) for i in range(spaces)])

    def handed_on(array, hops):
        pieces = [array]
        for hop in hops:
            pieces += [lax.ppermute(a, "tm", [(i, i ^ hop) for i in range(times)]) for a in pieces]
        return pieces

    arrived = [across(tokens, k) for k in range(1, spaces)]

    w_spatial = qkv_spatial.T.reshape(heads, 3 * HD, width)
    w_temporal = qkv_temporal.T.reshape(heads, 3 * HD, width)
    own, my_heads = pl.pallas_call(
        kernel_qkv,
        out_shape=tuple(
            jax.ShapeDtypeStruct(a, BF) for a in ((heads, 3, HD, rows), (part, 3 * HD, width))
        ),
        in_specs=[VMEM] + [ANY] * 2 + [VMEM] * 2,
        out_specs=(VMEM, VMEM),
        scratch_shapes=[pltpu.VMEM(w_spatial.shape, BF), pltpu.SemaphoreType.DMA((2,))],
        compiler_params=PARAMS,
        cost_estimate=pl.CostEstimate(
            flops=2 * rows * width * cols * 3, bytes_accessed=3 * 10**6, transcendentals=0
        ),
    )(tokens, w_spatial, w_temporal, modulation, bias_spatial)

    spread = lax.all_to_all(tokens.reshape(times, size, frames, width), "tm", 0, 0, tiled=True)

    other_bias = [across(bias_temporal, k) for k in range(1, spaces)]
    my_out = lax.dynamic_slice_in_dim(
        out_spatial, lax.rem(lax.axis_index("tm"), len(out_masks)) * out_part, out_part, 0
    )
    out_pieces = []
    for k in range(1, spaces):
        out_pieces += handed_on(after((across(my_out, k),), own)[0], out_hops)
    arrived = [after((a,), own, *other_bias)[0] for a in arrived]

    o_all = call(
        kernel_spatial,
        (spaces, rows, cols),
        4 + len(arrived),
        1e10,
        4e6,
        [
            pltpu.VMEM((spaces - 1, heads, 3, HD, rows), BF),
        ],
        params=SMALL,
    )(own, w_spatial, modulation, bias_spatial, *arrived)

    (my_heads,) = after((my_heads,), *arrived)
    direct_heads = [across(my_heads, k) for k in range(1, spaces)]
    o_here = lax.all_to_all(
        after((o_all,), spread, *out_pieces)[0].reshape(spaces * times, frames * size, cols), ("space", "tm"), 0, 0, tiled=True
    ).reshape(spaces, rows, cols)
    other_heads = []
    for a in direct_heads:
        other_heads += handed_on(after((a,), o_here)[0], hops)

    o_home = [
        across(lax.dynamic_index_in_dim(o_all, (space + k) % spaces, 0, keepdims=False), k)
        for k in range(1, spaces)
    ]

    y_home = call(
        functools.partial(kernel_home, masks=out_masks),
        (rows, width),
        5 + len(o_home) + len(out_pieces),
        2 * rows * width * cols * spaces,
        3e6,
        [pltpu.VMEM((len(out_masks), out_part, width), BF)],
        params=SMALL,
    )(o_all, tokens, outbias_spatial, modulation, out_spatial, *o_home, *out_pieces)
    x_here = spread.reshape(rows // frames, frames, width)
    h_here, o_own = pl.pallas_call(
        functools.partial(kernel_temporal, size=size, frames=frames, masks=out_masks),
        out_shape=(jax.ShapeDtypeStruct((rows, width), BF), jax.ShapeDtypeStruct((heads, HD, rows), F32)),
        in_specs=[VMEM] * (7 + len(out_pieces)),
        out_specs=(VMEM, VMEM),
        scratch_shapes=[pltpu.VMEM((len(out_masks), out_part, width), BF)],
        compiler_params=SMALL,
        cost_estimate=pl.CostEstimate(
            flops=2 * rows * width * cols * (3 + spaces), bytes_accessed=5 * 10**6, transcendentals=0
        ),
    )(o_here, x_here, w_temporal, outbias_spatial, modulation, bias_temporal, out_spatial, *out_pieces)
    o_t = call(
        functools.partial(kernel_rest, size=size, frames=frames, spaces=spaces, masks=masks),
        (rows, spaces * cols),
        1 + spaces + len(other_heads),
        2 * rows * width * cols * 3 * (spaces - 1),
        5e6,
        [
            pltpu.VMEM((spaces * heads, HD, rows), F32),
            pltpu.VMEM((heads, 3 * HD, 1), F32),
        ],
        params=SMALL,
    )(h_here, o_own, *other_bias, *other_heads)
    o_t = o_t.reshape(times, frames * size, spaces * cols)
    o_final = lax.all_to_all(o_t, "tm", 0, 0, tiled=True).reshape(rows, spaces * cols)

    return call(
        kernel_final, (patches, frames, width), 5, 2 * rows * width * cols * spaces, 3e6
    )(o_final, y_home, out_temporal, outbias_temporal, modulation)


def solution(mesh):
    return jax.shard_map(
        local,
        mesh=mesh,
        in_specs=(
            P("space", ("grp", "tm"), None),
            P("grp", None),
            P(None, "space"),
            P("space"),
            P("space", None),
            P(),
            P(None, "space"),
            P("space"),
            P(),
            P(),
        ),
        out_specs=P("space", ("grp", "tm"), None),
        check_vma=False,
    )
```

```python
import functools
import math

import jax
import jax.numpy as jnp
from jax import lax
from jax.experimental import pallas as pl
from jax.experimental.pallas import tpu as pltpu
from jax.sharding import PartitionSpec as P

HD = 72
WIN = 16
BF = jnp.bfloat16
F32 = jnp.float32
EXP2_SCALE = 1.0 / (math.sqrt(HD) * math.log(2.0))

VMEM = pl.BlockSpec(memory_space=pltpu.VMEM)
ANY = pl.BlockSpec(memory_space=pl.ANY)
SMALL = pltpu.CompilerParams(vmem_limit_bytes=16 * 1024 * 1024)
PARAMS = pltpu.CompilerParams(vmem_limit_bytes=63 * 1024 * 1024)

NT = (((1,), (1,)), ((), ()))
TN = (((0,), (0,)), ((), ()))


def mm(a, b, dims=(((1,), (0,)), ((), ()))):
    return lax.dot_general(a, b, dims, preferred_element_type=F32)


def modulated(values, offset_vec, scaling):
    center = jnp.mean(values, axis=-1, keepdims=True)
    moved = values - center
    spread = jnp.mean(moved * moved, axis=-1, keepdims=True)
    return moved * lax.rsqrt(spread + 1e-06) * (1.0 + scaling) + offset_vec


def attend(q_t, k_t, v_t, mask=None):
    scores = mm(k_t, q_t, TN)
    if mask is not None:
        scores = jnp.where(mask, scores, F32(-1e30))
    highest = jnp.max(scores, axis=0, keepdims=True)
    expon = jnp.exp2((scores - highest) * F32(EXP2_SCALE))
    total = jnp.sum(expon, axis=0, keepdims=True)
    return mm(v_t, expon.astype(BF)) * (1.0 / total)


def after(arrays, *others):
    return lax.optimization_barrier((*arrays, *others))[: len(arrays)]


def flat(ref, *index):
    block = ref[index] if index else ref[...]
    return block.reshape(-1, block.shape[-1])


def column(rows):
    return lax.broadcasted_iota(jnp.int32, (rows, 1), 0)


def line(rows):
    return lax.broadcasted_iota(jnp.int32, (1, rows), 1)


def chosen(source, rows):
    return (source == line(rows)).astype(F32).astype(BF)


def by_frame_first(rows, frames):
    r = column(rows)
    return chosen(lax.rem(r, rows // frames) * frames + lax.div(r, rows // frames), rows)


def by_patch_first(rows, frames):
    r = column(rows)
    return chosen(lax.rem(r, frames) * (rows // frames) + lax.div(r, frames), rows)


def bias_column(b_ref):
    count = b_ref.shape[0]
    return jnp.broadcast_to(b_ref[...].reshape(1, count), (8, count)).T[:, 0:1]


def spatial_rows(x, mod_ref, frames):
    h = modulated(x.astype(F32), mod_ref[0:1, :], mod_ref[1:2, :]).astype(BF)
    return mm(by_frame_first(x.shape[0], frames), h).astype(BF)


def fetch(sources, targets, sems):
    copies = [pltpu.make_async_copy(a, b, sems.at[i]) for i, (a, b) in enumerate(zip(sources, targets))]
    for copy in copies:
        copy.start()
    return copies


def coordinates():
    return lax.axis_index("space"), lax.rem(lax.axis_index("tm"), 2)


def kernel_qkv(x_ref, w_hbm, w_other_hbm, out_w_hbm, mod_ref, b_ref, out_ref, heads_ref, half_ref, w_ref, sems):
    _, core = coordinates()
    half, rows = heads_ref.shape[0], half_ref.shape[0]
    copies = fetch(
        (
            w_hbm,
            out_w_hbm.at[pl.ds(pl.multiple_of(core * rows, rows), rows)],
            w_other_hbm.at[pl.ds(core * half, half)],
        ),
        (w_ref, half_ref, heads_ref),
        sems,
    )
    h = spatial_rows(flat(x_ref), mod_ref, x_ref.shape[1])
    bias = bias_column(b_ref)
    copies[0].wait()
    for i in range(w_ref.shape[0]):
        qkv = mm(w_ref[i], h, NT) + bias[i * 3 * HD : (i + 1) * 3 * HD]
        for c in range(3):
            out_ref[i, c] = qkv[c * HD : (c + 1) * HD].astype(BF)
    for copy in copies[1:]:
        copy.wait()


def kernel_spatial(own_hbm, w_hbm, mod_ref, b_ref, *refs):
    x_refs, (out_ref, part_ref, own_ref, w_ref, sems) = refs[:-5], refs[-5:]
    heads = w_ref.shape[0]
    copies = fetch(
        (*[w_hbm.at[i] for i in range(heads)], own_hbm),
        (*[w_ref.at[i] for i in range(heads)], own_ref),
        sems,
    )
    space, _ = coordinates()
    patches, frames, _ = x_refs[0].shape
    spaces = len(x_refs) + 1
    bias = bias_column(b_ref)
    rows = [spatial_rows(flat(x_ref), mod_ref, frames) for x_ref in x_refs]
    for i in range(heads):
        copies[i].wait()
        for j in range(spaces - 1):
            qkv = mm(w_ref[i], rows[j], NT) + bias[i * 3 * HD : (i + 1) * 3 * HD]
            for c in range(3):
                part_ref[j, i, c] = qkv[c * HD : (c + 1) * HD].astype(BF)
    copies[heads].wait()
    by_frame = []
    for f in range(frames):
        cols = slice(f * patches, (f + 1) * patches)
        done = []
        for i in range(heads):
            q_t, k_t, v_t = (
                jnp.concatenate(
                    [own_ref[i, c, :, cols]] + [part_ref[j, i, c, :, cols] for j in range(spaces - 1)],
                    axis=1,
                )
                for c in range(3)
            )
            done.append(attend(q_t, k_t, v_t))
        by_frame.append(jnp.concatenate(done, axis=0).astype(BF))
    back = by_patch_first(patches * frames, frames)
    for j in range(spaces):
        mine = jnp.concatenate([o[:, j * patches : (j + 1) * patches] for o in by_frame], axis=1)
        out_ref[lax.rem(space - j + spaces, spaces)] = mm(back, mine, NT).astype(BF)


def middle(tokens, parts, outbias, gate):
    summed = parts[0].astype(BF).astype(F32)
    for part in parts[1:]:
        summed = summed + part.astype(BF).astype(F32)
    return (tokens.astype(F32) + gate * (summed + outbias)).astype(BF)


def temporal_mask(rows, size, frames):
    def place(row):
        device, within = lax.div(row, frames * size), lax.rem(row, frames * size)
        return device * frames + lax.rem(within, frames), lax.div(within, frames)

    key_frame, key_patch = place(column(rows))
    query_frame, query_patch = place(line(rows))
    code_key = key_patch * 4 * WIN * rows + key_frame
    code_query = query_patch * 4 * WIN * rows + query_frame
    back = code_query - code_key
    return (back >= 0) & (back < WIN)


def temporal_head(w, b, h, mask):
    qkv = (mm(w, h, NT) + b).astype(BF)
    return attend(qkv[0:HD], qkv[HD : 2 * HD], qkv[2 * HD : 3 * HD], mask)


def parts_of(o, pieces, core):
    half = pieces[1].shape[0]
    parts = [mm(o(0), pieces[0][...])]
    for k in range(1, (len(pieces) + 1) // 2):
        first, second = pieces[2 * k - 1][...], pieces[2 * k][...]
        rows = jnp.concatenate([jnp.where(core == 0, first, second), jnp.where(core == 0, second, first)])
        parts.append(mm(o(k), rows))
    return parts


def kernel_between(o_ref, x_ref, outbias_ref, mod_ref, *refs):
    space, core = coordinates()
    pieces, h_ref = refs[:-1], refs[-1]
    spaces = o_ref.shape[0]
    parts = parts_of(lambda k: o_ref[lax.rem(space - k + spaces, spaces)], pieces, core)
    y = middle(flat(x_ref), parts, outbias_ref[...].reshape(1, -1), mod_ref[2:3, :])
    h_ref[...] = modulated(y.astype(F32), mod_ref[3:4, :], mod_ref[4:5, :]).astype(BF)


def kernel_own(h_ref, w_ref, b_ref, out_ref, *, size, frames):
    h = h_ref[...]
    mask = temporal_mask(h.shape[0], size, frames)
    bias = bias_column(b_ref)
    for i in range(w_ref.shape[0]):
        out_ref[i] = temporal_head(w_ref[i], bias[i * 3 * HD : (i + 1) * 3 * HD], h, mask)


def kernel_rest(h_ref, own_ref, *refs, size, frames, spaces):
    b_refs, w_refs, (out_ref, turn_ref) = refs[: spaces - 1], refs[spaces - 1 : -2], refs[-2:]
    space, core = coordinates()
    h = h_ref[...]
    rows = h.shape[0]
    mask = temporal_mask(rows, size, frames)
    heads = own_ref.shape[0]
    half = heads // 2
    for i in range(heads):
        turn_ref[space * heads + i] = own_ref[i]
    for n, w_ref in enumerate(w_refs):
        shift = n // 2 + 1
        bias = bias_column(b_refs[shift - 1])
        second = (core == 0) == (n % 2 == 1)
        within = jnp.where(second, half, 0)
        group = lax.rem(space - shift + spaces, spaces)
        bias = jnp.where(second, bias[half * 3 * HD :], bias[: half * 3 * HD])
        for i in range(half):
            o_t = temporal_head(w_ref[i], bias[i * 3 * HD : (i + 1) * 3 * HD], h, mask)
            turn_ref[group * heads + within + i] = o_t
    out_ref[...] = turn_ref[...].reshape(-1, rows).T.astype(BF)


def kernel_home(o_own_ref, x_ref, outbias_ref, mod_ref, *refs):
    space, core = coordinates()
    spaces = o_own_ref.shape[0]
    o_refs, pieces, out_ref = refs[: spaces - 1], refs[spaces - 1 : -1], refs[-1]
    parts = parts_of(lambda k: o_refs[k - 1][...] if k else o_own_ref[space], pieces, core)
    out_ref[...] = middle(flat(x_ref), parts, outbias_ref[...].reshape(1, -1), mod_ref[2:3, :])


def kernel_final(o_ref, y_ref, w_ref, outbias_ref, mod_ref, out_ref):
    final = mm(o_ref[...], w_ref[...]) + outbias_ref[...].reshape(1, -1)
    result = (y_ref[...].astype(F32) + mod_ref[5:6, :] * final).astype(BF)
    out_ref[...] = result.reshape(out_ref.shape)


def call(kernel, out_shape, count, flops, nbytes, scratch=(), in_any=(), params=PARAMS):
    return pl.pallas_call(
        kernel,
        out_shape=jax.ShapeDtypeStruct(out_shape, BF),
        in_specs=[ANY if i in in_any else VMEM for i in range(count)],
        out_specs=VMEM,
        scratch_shapes=list(scratch),
        compiler_params=params,
        cost_estimate=pl.CostEstimate(flops=int(flops), bytes_accessed=int(nbytes), transcendentals=0),
    )


def local(
    tokens,
    modulation,
    qkv_spatial,
    bias_spatial,
    out_spatial,
    outbias_spatial,
    qkv_temporal,
    bias_temporal,
    out_temporal,
    outbias_temporal,
):
    patches, frames, width = tokens.shape
    spaces, times = lax.axis_size("space"), lax.axis_size("tm")
    space = lax.axis_index("space")
    heads = qkv_spatial.shape[1] // (3 * HD)
    cols = heads * HD
    half = heads // 2
    size = patches // times
    rows = patches * frames

    def across(array, k):
        return lax.ppermute(array, "space", [(i, (i + k) % spaces) for i in range(spaces)])

    def beside(array):
        return lax.ppermute(array, "tm", [(i, i ^ 1) for i in range(times)])

    arrived = [across(tokens, k) for k in range(1, spaces)]

    w_spatial = qkv_spatial.T.reshape(heads, 3 * HD, width)
    w_temporal = qkv_temporal.T.reshape(heads, 3 * HD, width)
    own, my_heads, my_out = pl.pallas_call(
        kernel_qkv,
        out_shape=tuple(
            jax.ShapeDtypeStruct(a, BF)
            for a in ((heads, 3, HD, rows), (half, 3 * HD, width), (half * HD, width))
        ),
        in_specs=[VMEM] + [ANY] * 3 + [VMEM] * 2,
        out_specs=(VMEM, VMEM, VMEM),
        scratch_shapes=[pltpu.VMEM(w_spatial.shape, BF), pltpu.SemaphoreType.DMA((3,))],
        compiler_params=PARAMS,
        cost_estimate=pl.CostEstimate(
            flops=2 * rows * width * cols * 3, bytes_accessed=3 * 10**6, transcendentals=0
        ),
    )(tokens, w_spatial, w_temporal, out_spatial, modulation, bias_spatial)

    (spread,) = after((tokens,), own)
    spread = lax.all_to_all(spread.reshape(times, size, frames, width), "tm", 0, 0, tiled=True)

    other_bias = [across(bias_temporal, k) for k in range(1, spaces)]
    (my_out,) = after((my_out,), *other_bias, *arrived)
    arrived = [after((a,), own)[0] for a in arrived]
    direct_out = [across(my_out, k) for k in range(1, spaces)]

    o_all = call(
        kernel_spatial,
        (spaces, rows, cols),
        4 + len(arrived),
        1e10,
        4e6,
        [
            pltpu.VMEM((spaces - 1, heads, 3, HD, rows), BF),
            pltpu.VMEM(own.shape, BF),
            pltpu.VMEM(w_spatial.shape, BF),
            pltpu.SemaphoreType.DMA((heads + 1,)),
        ],
        (0, 1),
    )(own, w_spatial, modulation, bias_spatial, *arrived)

    (my_heads,) = after((my_heads,), o_all, *direct_out)
    direct_heads = [across(my_heads, k) for k in range(1, spaces)]
    out_pieces = [out_spatial]
    for a in direct_out:
        out_pieces += [a, beside(after((a,), o_all)[0])]

    o_here = lax.all_to_all(
        after((o_all,), spread, *out_pieces)[0].reshape(spaces * times, frames * size, cols), ("space", "tm"), 0, 0, tiled=True
    ).reshape(spaces, rows, cols)
    other_heads = []
    for a in direct_heads:
        other_heads += [a, beside(after((a,), o_here)[0])]

    o_home = [
        across(lax.dynamic_index_in_dim(o_all, (space + k) % spaces, 0, keepdims=False), k)
        for k in range(1, spaces)
    ]

    y_home = call(
        kernel_home,
        (rows, width),
        4 + len(o_home) + len(out_pieces),
        2 * rows * width * cols * spaces,
        3e6,
        params=SMALL,
    )(o_all, tokens, outbias_spatial, modulation, *o_home, *out_pieces)
    x_here = spread.reshape(rows // frames, frames, width)
    h_here = call(
        kernel_between, (rows, width), 4 + len(out_pieces), 2 * rows * width * cols * spaces, 3e6, params=SMALL
    )(o_here, x_here, outbias_spatial, modulation, *out_pieces)
    o_own = pl.pallas_call(
        functools.partial(kernel_own, size=size, frames=frames),
        out_shape=jax.ShapeDtypeStruct((heads, HD, rows), F32),
        in_specs=[VMEM] * 3,
        out_specs=VMEM,
        compiler_params=SMALL,
        cost_estimate=pl.CostEstimate(
            flops=2 * rows * width * cols * 3, bytes_accessed=3 * 10**6, transcendentals=0
        ),
    )(h_here, w_temporal, bias_temporal)
    o_t = call(
        functools.partial(kernel_rest, size=size, frames=frames, spaces=spaces),
        (rows, spaces * cols),
        1 + spaces + len(other_heads),
        2 * rows * width * cols * 3 * (spaces - 1),
        5e6,
        [
            pltpu.VMEM((spaces * heads, HD, rows), F32),
        ],
        params=SMALL,
    )(h_here, o_own, *other_bias, *other_heads)
    o_t = o_t.reshape(times, frames * size, spaces * cols)
    o_final = lax.all_to_all(o_t, "tm", 0, 0, tiled=True).reshape(rows, spaces * cols)

    return call(
        kernel_final, (patches, frames, width), 5, 2 * rows * width * cols * spaces, 3e6, params=SMALL
    )(o_final, y_home, out_temporal, outbias_temporal, modulation)


def solution(mesh):
    return jax.shard_map(
        local,
        mesh=mesh,
        in_specs=(
            P("space", ("grp", "tm"), None),
            P("grp", None),
            P(None, "space"),
            P("space"),
            P("space", None),
            P(),
            P(None, "space"),
            P("space"),
            P(),
            P(),
        ),
        out_specs=P("space", ("grp", "tm"), None),
        check_vma=False,
    )
```

```python
import functools
import math

import jax
import jax.numpy as jnp
from jax import lax
from jax.experimental import pallas as pl
from jax.experimental.pallas import tpu as pltpu
from jax.sharding import PartitionSpec as P

HD = 72
WIN = 16
BF = jnp.bfloat16
F32 = jnp.float32
EXP2_SCALE = 1.0 / (math.sqrt(HD) * math.log(2.0))

VMEM = pl.BlockSpec(memory_space=pltpu.VMEM)
ANY = pl.BlockSpec(memory_space=pl.ANY)
LARGE = pltpu.CompilerParams(vmem_limit_bytes=62 * 1024 * 1024)
SMALL = pltpu.CompilerParams(vmem_limit_bytes=16 * 1024 * 1024)
PARAMS = pltpu.CompilerParams(vmem_limit_bytes=63 * 1024 * 1024)

NT = (((1,), (1,)), ((), ()))
TN = (((0,), (0,)), ((), ()))


def mm(a, b, dims=(((1,), (0,)), ((), ()))):
    return lax.dot_general(a, b, dims, preferred_element_type=F32)


def modulated(values, offset_vec, scaling):
    center = jnp.mean(values, axis=-1, keepdims=True)
    moved = values - center
    spread = jnp.mean(moved * moved, axis=-1, keepdims=True)
    return moved * lax.rsqrt(spread + 1e-06) * (1.0 + scaling) + offset_vec


def attend(q_t, k_t, v_t, mask=None):
    scores = mm(k_t, q_t, TN)
    if mask is not None:
        scores = jnp.where(mask, scores, F32(-1e30))
    highest = jnp.max(scores, axis=0, keepdims=True)
    expon = jnp.exp2((scores - highest) * F32(EXP2_SCALE))
    total = jnp.sum(expon, axis=0, keepdims=True)
    return mm(v_t, expon.astype(BF)) * (1.0 / total)


def after(arrays, *others):
    return lax.optimization_barrier((*arrays, *others))[: len(arrays)]


def flat(ref, *index):
    block = ref[index] if index else ref[...]
    return block.reshape(-1, block.shape[-1])


def column(rows):
    return lax.broadcasted_iota(jnp.int32, (rows, 1), 0)


def line(rows):
    return lax.broadcasted_iota(jnp.int32, (1, rows), 1)


def chosen(source, rows):
    return (source == line(rows)).astype(F32).astype(BF)


def by_frame_first(rows, frames):
    r = column(rows)
    return chosen(lax.rem(r, rows // frames) * frames + lax.div(r, rows // frames), rows)


def by_patch_first(rows, frames):
    r = column(rows)
    return chosen(lax.rem(r, frames) * (rows // frames) + lax.div(r, frames), rows)


def bias_column(b_ref):
    count = b_ref.shape[0]
    return jnp.broadcast_to(b_ref[...].reshape(1, count), (8, count)).T[:, 0:1]


def spatial_rows(x, mod_ref, frames):
    h = modulated(x.astype(F32), mod_ref[0:1, :], mod_ref[1:2, :]).astype(BF)
    return mm(by_frame_first(x.shape[0], frames), h).astype(BF)


def fetch(sources, targets, sems):
    copies = [pltpu.make_async_copy(a, b, sems.at[i]) for i, (a, b) in enumerate(zip(sources, targets))]
    for copy in copies:
        copy.start()
    return copies


def coordinates():
    return lax.axis_index("space"), lax.rem(lax.axis_index("tm"), 2)


def kernel_qkv(x_ref, w_hbm, w_other_hbm, out_w_hbm, mod_ref, b_ref, out_ref, heads_ref, half_ref, w_ref, sems):
    _, core = coordinates()
    half, rows = heads_ref.shape[0], half_ref.shape[0]
    copies = fetch(
        (
            w_hbm,
            out_w_hbm.at[pl.ds(pl.multiple_of(core * rows, rows), rows)],
            w_other_hbm.at[pl.ds(core * half, half)],
        ),
        (w_ref, half_ref, heads_ref),
        sems,
    )
    h = spatial_rows(flat(x_ref), mod_ref, x_ref.shape[1])
    bias = bias_column(b_ref)
    copies[0].wait()
    for i in range(w_ref.shape[0]):
        qkv = mm(w_ref[i], h, NT) + bias[i * 3 * HD : (i + 1) * 3 * HD]
        for c in range(3):
            out_ref[i, c] = qkv[c * HD : (c + 1) * HD].astype(BF)
    for copy in copies[1:]:
        copy.wait()


def kernel_spatial(own_hbm, w_hbm, mod_ref, b_ref, *refs):
    x_refs, (out_ref, part_ref, own_ref, w_ref, sems) = refs[:-5], refs[-5:]
    heads = w_ref.shape[0]
    copies = fetch(
        (*[w_hbm.at[i] for i in range(heads)], own_hbm),
        (*[w_ref.at[i] for i in range(heads)], own_ref),
        sems,
    )
    space, _ = coordinates()
    patches, frames, _ = x_refs[0].shape
    spaces = len(x_refs) + 1
    bias = bias_column(b_ref)
    rows = [spatial_rows(flat(x_ref), mod_ref, frames) for x_ref in x_refs]
    for i in range(heads):
        copies[i].wait()
        for j in range(spaces - 1):
            qkv = mm(w_ref[i], rows[j], NT) + bias[i * 3 * HD : (i + 1) * 3 * HD]
            for c in range(3):
                part_ref[j, i, c] = qkv[c * HD : (c + 1) * HD].astype(BF)
    copies[heads].wait()
    by_frame = []
    for f in range(frames):
        cols = slice(f * patches, (f + 1) * patches)
        done = []
        for i in range(heads):
            q_t, k_t, v_t = (
                jnp.concatenate(
                    [own_ref[i, c, :, cols]] + [part_ref[j, i, c, :, cols] for j in range(spaces - 1)],
                    axis=1,
                )
                for c in range(3)
            )
            done.append(attend(q_t, k_t, v_t))
        by_frame.append(jnp.concatenate(done, axis=0).astype(BF))
    back = by_patch_first(patches * frames, frames)
    for j in range(spaces):
        mine = jnp.concatenate([o[:, j * patches : (j + 1) * patches] for o in by_frame], axis=1)
        out_ref[lax.rem(space - j + spaces, spaces)] = mm(back, mine, NT).astype(BF)


def middle(tokens, parts, outbias, gate):
    summed = parts[0].astype(BF).astype(F32)
    for part in parts[1:]:
        summed = summed + part.astype(BF).astype(F32)
    return (tokens.astype(F32) + gate * (summed + outbias)).astype(BF)


def temporal_mask(rows, size, frames):
    def place(row):
        device, within = lax.div(row, frames * size), lax.rem(row, frames * size)
        return device * frames + lax.rem(within, frames), lax.div(within, frames)

    key_frame, key_patch = place(column(rows))
    query_frame, query_patch = place(line(rows))
    code_key = key_patch * 4 * WIN * rows + key_frame
    code_query = query_patch * 4 * WIN * rows + query_frame
    back = code_query - code_key
    return (back >= 0) & (back < WIN)


def temporal_head(w, b, h, mask):
    qkv = (mm(w, h, NT) + b).astype(BF)
    return attend(qkv[0:HD], qkv[HD : 2 * HD], qkv[2 * HD : 3 * HD], mask)


def parts_of(o, pieces, core):
    half = pieces[1].shape[0]
    parts = [mm(o(0), pieces[0][...])]
    for k in range(1, (len(pieces) + 1) // 2):
        first, second = pieces[2 * k - 1][...], pieces[2 * k][...]
        rows = jnp.concatenate([jnp.where(core == 0, first, second), jnp.where(core == 0, second, first)])
        parts.append(mm(o(k), rows))
    return parts


def kernel_between(o_ref, x_ref, outbias_ref, mod_ref, *refs):
    space, core = coordinates()
    pieces, h_ref = refs[:-1], refs[-1]
    spaces = o_ref.shape[0]
    parts = parts_of(lambda k: o_ref[lax.rem(space - k + spaces, spaces)], pieces, core)
    y = middle(flat(x_ref), parts, outbias_ref[...].reshape(1, -1), mod_ref[2:3, :])
    h_ref[...] = modulated(y.astype(F32), mod_ref[3:4, :], mod_ref[4:5, :]).astype(BF)


def kernel_own(h_ref, w_ref, b_ref, out_ref, *, size, frames):
    h = h_ref[...]
    mask = temporal_mask(h.shape[0], size, frames)
    bias = bias_column(b_ref)
    for i in range(w_ref.shape[0]):
        out_ref[i] = temporal_head(w_ref[i], bias[i * 3 * HD : (i + 1) * 3 * HD], h, mask)


def kernel_rest(h_ref, own_ref, *refs, size, frames, spaces):
    b_refs, w_hbms, (out_ref, turn_ref, w_ref, sems) = refs[: spaces - 1], refs[spaces - 1 : -4], refs[-4:]
    copies = fetch(w_hbms, [w_ref.at[n] for n in range(len(w_hbms))], sems)
    space, core = coordinates()
    h = h_ref[...]
    rows = h.shape[0]
    mask = temporal_mask(rows, size, frames)
    heads = own_ref.shape[0]
    half = heads // 2
    for i in range(heads):
        turn_ref[space * heads + i] = own_ref[i]
    for n in range(len(w_hbms)):
        shift = n // 2 + 1
        bias = bias_column(b_refs[shift - 1])
        second = (core == 0) == (n % 2 == 1)
        within = jnp.where(second, half, 0)
        group = lax.rem(space - shift + spaces, spaces)
        bias = jnp.where(second, bias[half * 3 * HD :], bias[: half * 3 * HD])
        copies[n].wait()
        for i in range(half):
            o_t = temporal_head(w_ref[n, i], bias[i * 3 * HD : (i + 1) * 3 * HD], h, mask)
            turn_ref[group * heads + within + i] = o_t
    out_ref[...] = turn_ref[...].reshape(-1, rows).T.astype(BF)


def kernel_home(o_own_ref, x_ref, outbias_ref, mod_ref, *refs):
    space, core = coordinates()
    spaces = o_own_ref.shape[0]
    o_refs, pieces, out_ref = refs[: spaces - 1], refs[spaces - 1 : -1], refs[-1]
    parts = parts_of(lambda k: o_refs[k - 1][...] if k else o_own_ref[space], pieces, core)
    out_ref[...] = middle(flat(x_ref), parts, outbias_ref[...].reshape(1, -1), mod_ref[2:3, :])


def kernel_final(o_ref, y_ref, w_ref, outbias_ref, mod_ref, out_ref):
    final = mm(o_ref[...], w_ref[...]) + outbias_ref[...].reshape(1, -1)
    result = (y_ref[...].astype(F32) + mod_ref[5:6, :] * final).astype(BF)
    out_ref[...] = result.reshape(out_ref.shape)


def call(kernel, out_shape, count, flops, nbytes, scratch=(), in_any=(), params=PARAMS):
    return pl.pallas_call(
        kernel,
        out_shape=jax.ShapeDtypeStruct(out_shape, BF),
        in_specs=[ANY if i in in_any else VMEM for i in range(count)],
        out_specs=VMEM,
        scratch_shapes=list(scratch),
        compiler_params=params,
        cost_estimate=pl.CostEstimate(flops=int(flops), bytes_accessed=int(nbytes), transcendentals=0),
    )


def local(
    tokens,
    modulation,
    qkv_spatial,
    bias_spatial,
    out_spatial,
    outbias_spatial,
    qkv_temporal,
    bias_temporal,
    out_temporal,
    outbias_temporal,
):
    patches, frames, width = tokens.shape
    spaces, times = lax.axis_size("space"), lax.axis_size("tm")
    space = lax.axis_index("space")
    heads = qkv_spatial.shape[1] // (3 * HD)
    cols = heads * HD
    half = heads // 2
    size = patches // times
    rows = patches * frames

    def across(array, k):
        return lax.ppermute(array, "space", [(i, (i + k) % spaces) for i in range(spaces)])

    def beside(array):
        return lax.ppermute(array, "tm", [(i, i ^ 1) for i in range(times)])

    arrived = [across(tokens, k) for k in range(1, spaces)]

    w_spatial = qkv_spatial.T.reshape(heads, 3 * HD, width)
    w_temporal = qkv_temporal.T.reshape(heads, 3 * HD, width)
    own, my_heads, my_out = pl.pallas_call(
        kernel_qkv,
        out_shape=tuple(
            jax.ShapeDtypeStruct(a, BF)
            for a in ((heads, 3, HD, rows), (half, 3 * HD, width), (half * HD, width))
        ),
        in_specs=[VMEM] + [ANY] * 3 + [VMEM] * 2,
        out_specs=(VMEM, VMEM, VMEM),
        scratch_shapes=[pltpu.VMEM(w_spatial.shape, BF), pltpu.SemaphoreType.DMA((3,))],
        compiler_params=PARAMS,
        cost_estimate=pl.CostEstimate(
            flops=2 * rows * width * cols * 3, bytes_accessed=3 * 10**6, transcendentals=0
        ),
    )(tokens, w_spatial, w_temporal, out_spatial, modulation, bias_spatial)

    (spread,) = after((tokens,), own)
    spread = lax.all_to_all(spread.reshape(times, size, frames, width), "tm", 0, 0, tiled=True)

    other_bias = [across(bias_temporal, k) for k in range(1, spaces)]
    (my_out,) = after((my_out,), *other_bias, *arrived)
    arrived = [after((a,), own)[0] for a in arrived]
    direct_out = [across(my_out, k) for k in range(1, spaces)]

    o_all = call(
        kernel_spatial,
        (spaces, rows, cols),
        4 + len(arrived),
        1e10,
        4e6,
        [
            pltpu.VMEM((spaces - 1, heads, 3, HD, rows), BF),
            pltpu.VMEM(own.shape, BF),
            pltpu.VMEM(w_spatial.shape, BF),
            pltpu.SemaphoreType.DMA((heads + 1,)),
        ],
        (0, 1),
        params=LARGE,
    )(own, w_spatial, modulation, bias_spatial, *arrived)

    (my_heads,) = after((my_heads,), o_all, *direct_out)
    direct_heads = [across(my_heads, k) for k in range(1, spaces)]
    out_pieces = [out_spatial]
    for a in direct_out:
        out_pieces += [a, beside(after((a,), o_all)[0])]

    o_here = lax.all_to_all(
        after((o_all,), spread, *out_pieces)[0].reshape(spaces * times, frames * size, cols), ("space", "tm"), 0, 0, tiled=True
    ).reshape(spaces, rows, cols)
    other_heads = []
    for a in direct_heads:
        other_heads += [a, beside(after((a,), o_here)[0])]

    o_home = [
        across(lax.dynamic_index_in_dim(o_all, (space + k) % spaces, 0, keepdims=False), k)
        for k in range(1, spaces)
    ]

    y_home = call(
        kernel_home,
        (rows, width),
        4 + len(o_home) + len(out_pieces),
        2 * rows * width * cols * spaces,
        3e6,
        params=SMALL,
    )(o_all, tokens, outbias_spatial, modulation, *o_home, *out_pieces)
    x_here = spread.reshape(rows // frames, frames, width)
    h_here = call(
        kernel_between, (rows, width), 4 + len(out_pieces), 2 * rows * width * cols * spaces, 3e6, params=SMALL
    )(o_here, x_here, outbias_spatial, modulation, *out_pieces)
    o_own = pl.pallas_call(
        functools.partial(kernel_own, size=size, frames=frames),
        out_shape=jax.ShapeDtypeStruct((heads, HD, rows), F32),
        in_specs=[VMEM] * 3,
        out_specs=VMEM,
        compiler_params=SMALL,
        cost_estimate=pl.CostEstimate(
            flops=2 * rows * width * cols * 3, bytes_accessed=3 * 10**6, transcendentals=0
        ),
    )(h_here, w_temporal, bias_temporal)
    o_t = call(
        functools.partial(kernel_rest, size=size, frames=frames, spaces=spaces),
        (rows, spaces * cols),
        1 + spaces + len(other_heads),
        2 * rows * width * cols * 3 * (spaces - 1),
        5e6,
        [
            pltpu.VMEM((spaces * heads, HD, rows), F32),
            pltpu.VMEM((len(other_heads), half, 3 * HD, width), BF),
            pltpu.SemaphoreType.DMA((len(other_heads),)),
        ],
        range(1 + spaces, 1 + spaces + len(other_heads)),
        params=SMALL,
    )(h_here, o_own, *other_bias, *other_heads)
    o_t = o_t.reshape(times, frames * size, spaces * cols)
    o_final = lax.all_to_all(o_t, "tm", 0, 0, tiled=True).reshape(rows, spaces * cols)

    return call(
        kernel_final, (patches, frames, width), 5, 2 * rows * width * cols * spaces, 3e6, params=SMALL
    )(o_final, y_home, out_temporal, outbias_temporal, modulation)


def solution(mesh):
    return jax.shard_map(
        local,
        mesh=mesh,
        in_specs=(
            P("space", ("grp", "tm"), None),
            P("grp", None),
            P(None, "space"),
            P("space"),
            P("space", None),
            P(),
            P(None, "space"),
            P("space"),
            P(),
            P(),
        ),
        out_specs=P("space", ("grp", "tm"), None),
        check_vma=False,
    )
```

```python
import functools
import math

import jax
import jax.numpy as jnp
from jax import lax
from jax.experimental import pallas as pl
from jax.experimental.pallas import tpu as pltpu
from jax.sharding import PartitionSpec as P

HD = 72
WIN = 16
BF = jnp.bfloat16
F32 = jnp.float32
EXP2_SCALE = 1.0 / (math.sqrt(HD) * math.log(2.0))

VMEM = pl.BlockSpec(memory_space=pltpu.VMEM)
ANY = pl.BlockSpec(memory_space=pl.ANY)
LARGE = pltpu.CompilerParams(vmem_limit_bytes=62 * 1024 * 1024)
SMALL = pltpu.CompilerParams(vmem_limit_bytes=16 * 1024 * 1024)
PARAMS = pltpu.CompilerParams(vmem_limit_bytes=63 * 1024 * 1024)

NT = (((1,), (1,)), ((), ()))
TN = (((0,), (0,)), ((), ()))


def mm(a, b, dims=(((1,), (0,)), ((), ()))):
    return lax.dot_general(a, b, dims, preferred_element_type=F32)


def modulated(values, offset_vec, scaling):
    center = jnp.mean(values, axis=-1, keepdims=True)
    moved = values - center
    spread = jnp.mean(moved * moved, axis=-1, keepdims=True)
    return moved * lax.rsqrt(spread + 1e-06) * (1.0 + scaling) + offset_vec


def attend(q_t, k_t, v_t, mask=None):
    scores = mm(k_t, q_t, TN)
    if mask is not None:
        scores = jnp.where(mask, scores, F32(-1e30))
    highest = jnp.max(scores, axis=0, keepdims=True)
    expon = jnp.exp2((scores - highest) * F32(EXP2_SCALE))
    total = jnp.sum(expon, axis=0, keepdims=True)
    return mm(v_t, expon.astype(BF)) * (1.0 / total)


def after(arrays, *others):
    return lax.optimization_barrier((*arrays, *others))[: len(arrays)]


def flat(ref, *index):
    block = ref[index] if index else ref[...]
    return block.reshape(-1, block.shape[-1])


def column(rows):
    return lax.broadcasted_iota(jnp.int32, (rows, 1), 0)


def line(rows):
    return lax.broadcasted_iota(jnp.int32, (1, rows), 1)


def chosen(source, rows):
    return (source == line(rows)).astype(F32).astype(BF)


def by_frame_first(rows, frames):
    r = column(rows)
    return chosen(lax.rem(r, rows // frames) * frames + lax.div(r, rows // frames), rows)


def by_patch_first(rows, frames):
    r = column(rows)
    return chosen(lax.rem(r, frames) * (rows // frames) + lax.div(r, frames), rows)


def bias_column(b_ref):
    count = b_ref.shape[0]
    return jnp.broadcast_to(b_ref[...].reshape(1, count), (8, count)).T[:, 0:1]


def spatial_rows(x, mod_ref, frames):
    h = modulated(x.astype(F32), mod_ref[0:1, :], mod_ref[1:2, :]).astype(BF)
    return mm(by_frame_first(x.shape[0], frames), h).astype(BF)


def fetch(sources, targets, sems):
    copies = [pltpu.make_async_copy(a, b, sems.at[i]) for i, (a, b) in enumerate(zip(sources, targets))]
    for copy in copies:
        copy.start()
    return copies


def coordinates():
    return lax.axis_index("space"), lax.rem(lax.axis_index("tm"), 2)


def kernel_qkv(x_ref, w_hbm, w_other_hbm, out_w_hbm, mod_ref, b_ref, out_ref, heads_ref, half_ref, w_ref, sems):
    _, core = coordinates()
    half, rows = heads_ref.shape[0], half_ref.shape[0]
    copies = fetch(
        (
            w_hbm,
            out_w_hbm.at[pl.ds(pl.multiple_of(core * rows, rows), rows)],
            w_other_hbm.at[pl.ds(core * half, half)],
        ),
        (w_ref, half_ref, heads_ref),
        sems,
    )
    h = spatial_rows(flat(x_ref), mod_ref, x_ref.shape[1])
    bias = bias_column(b_ref)
    copies[0].wait()
    for i in range(w_ref.shape[0]):
        qkv = mm(w_ref[i], h, NT) + bias[i * 3 * HD : (i + 1) * 3 * HD]
        for c in range(3):
            out_ref[i, c] = qkv[c * HD : (c + 1) * HD].astype(BF)
    for copy in copies[1:]:
        copy.wait()


def kernel_spatial(own_hbm, w_hbm, mod_ref, b_ref, *refs):
    x_refs, (out_ref, part_ref, own_ref, w_ref, sems) = refs[:-5], refs[-5:]
    heads = w_ref.shape[0]
    copies = fetch(
        (*[w_hbm.at[i] for i in range(heads)], own_hbm),
        (*[w_ref.at[i] for i in range(heads)], own_ref),
        sems,
    )
    space, _ = coordinates()
    patches, frames, _ = x_refs[0].shape
    spaces = len(x_refs) + 1
    bias = bias_column(b_ref)
    rows = [spatial_rows(flat(x_ref), mod_ref, frames) for x_ref in x_refs]
    for i in range(heads):
        copies[i].wait()
        for j in range(spaces - 1):
            qkv = mm(w_ref[i], rows[j], NT) + bias[i * 3 * HD : (i + 1) * 3 * HD]
            for c in range(3):
                part_ref[j, i, c] = qkv[c * HD : (c + 1) * HD].astype(BF)
    copies[heads].wait()
    by_frame = []
    for f in range(frames):
        cols = slice(f * patches, (f + 1) * patches)
        done = []
        for i in range(heads):
            q_t, k_t, v_t = (
                jnp.concatenate(
                    [own_ref[i, c, :, cols]] + [part_ref[j, i, c, :, cols] for j in range(spaces - 1)],
                    axis=1,
                )
                for c in range(3)
            )
            done.append(attend(q_t, k_t, v_t))
        by_frame.append(jnp.concatenate(done, axis=0).astype(BF))
    back = by_patch_first(patches * frames, frames)
    for j in range(spaces):
        mine = jnp.concatenate([o[:, j * patches : (j + 1) * patches] for o in by_frame], axis=1)
        out_ref[lax.rem(space - j + spaces, spaces)] = mm(back, mine, NT).astype(BF)


def middle(tokens, parts, outbias, gate):
    summed = parts[0].astype(BF).astype(F32)
    for part in parts[1:]:
        summed = summed + part.astype(BF).astype(F32)
    return (tokens.astype(F32) + gate * (summed + outbias)).astype(BF)


def temporal_mask(rows, size, frames):
    def place(row):
        device, within = lax.div(row, frames * size), lax.rem(row, frames * size)
        return device * frames + lax.rem(within, frames), lax.div(within, frames)

    key_frame, key_patch = place(column(rows))
    query_frame, query_patch = place(line(rows))
    code_key = key_patch * 4 * WIN * rows + key_frame
    code_query = query_patch * 4 * WIN * rows + query_frame
    back = code_query - code_key
    return (back >= 0) & (back < WIN)


def temporal_head(w, b, h, mask):
    qkv = (mm(w, h, NT) + b).astype(BF)
    return attend(qkv[0:HD], qkv[HD : 2 * HD], qkv[2 * HD : 3 * HD], mask)


def parts_of(o, pieces, core):
    half = pieces[1].shape[0]
    parts = [mm(o(0), pieces[0][...])]
    for k in range(1, (len(pieces) + 1) // 2):
        first, second = pieces[2 * k - 1][...], pieces[2 * k][...]
        rows = jnp.concatenate([jnp.where(core == 0, first, second), jnp.where(core == 0, second, first)])
        parts.append(mm(o(k), rows))
    return parts


def kernel_between(o_ref, x_ref, outbias_ref, mod_ref, *refs):
    space, core = coordinates()
    pieces, h_ref = refs[:-1], refs[-1]
    spaces = o_ref.shape[0]
    parts = parts_of(lambda k: o_ref[lax.rem(space - k + spaces, spaces)], pieces, core)
    y = middle(flat(x_ref), parts, outbias_ref[...].reshape(1, -1), mod_ref[2:3, :])
    h_ref[...] = modulated(y.astype(F32), mod_ref[3:4, :], mod_ref[4:5, :]).astype(BF)


def kernel_own(h_ref, w_ref, b_ref, out_ref, *, size, frames):
    h = h_ref[...]
    mask = temporal_mask(h.shape[0], size, frames)
    bias = bias_column(b_ref)
    for i in range(w_ref.shape[0]):
        out_ref[i] = temporal_head(w_ref[i], bias[i * 3 * HD : (i + 1) * 3 * HD], h, mask)


def kernel_rest(h_ref, own_ref, *refs, size, frames, spaces):
    b_refs, w_refs, (out_ref, turn_ref) = refs[: spaces - 1], refs[spaces - 1 : -2], refs[-2:]
    space, core = coordinates()
    h = h_ref[...]
    rows = h.shape[0]
    mask = temporal_mask(rows, size, frames)
    heads = own_ref.shape[0]
    half = heads // 2
    for i in range(heads):
        turn_ref[space * heads + i] = own_ref[i]
    for n, w_ref in enumerate(w_refs):
        shift = n // 2 + 1
        bias = bias_column(b_refs[shift - 1])
        second = (core == 0) == (n % 2 == 1)
        within = jnp.where(second, half, 0)
        group = lax.rem(space - shift + spaces, spaces)
        bias = jnp.where(second, bias[half * 3 * HD :], bias[: half * 3 * HD])
        for i in range(half):
            o_t = temporal_head(w_ref[i], bias[i * 3 * HD : (i + 1) * 3 * HD], h, mask)
            turn_ref[group * heads + within + i] = o_t
    out_ref[...] = turn_ref[...].reshape(-1, rows).T.astype(BF)


def kernel_home(o_own_ref, x_ref, outbias_ref, mod_ref, *refs):
    space, core = coordinates()
    spaces = o_own_ref.shape[0]
    o_refs, pieces, out_ref = refs[: spaces - 1], refs[spaces - 1 : -1], refs[-1]
    parts = parts_of(lambda k: o_refs[k - 1][...] if k else o_own_ref[space], pieces, core)
    out_ref[...] = middle(flat(x_ref), parts, outbias_ref[...].reshape(1, -1), mod_ref[2:3, :])


def kernel_final(o_ref, y_ref, w_ref, outbias_ref, mod_ref, out_ref):
    final = mm(o_ref[...], w_ref[...]) + outbias_ref[...].reshape(1, -1)
    result = (y_ref[...].astype(F32) + mod_ref[5:6, :] * final).astype(BF)
    out_ref[...] = result.reshape(out_ref.shape)


def call(kernel, out_shape, count, flops, nbytes, scratch=(), in_any=(), params=PARAMS):
    return pl.pallas_call(
        kernel,
        out_shape=jax.ShapeDtypeStruct(out_shape, BF),
        in_specs=[ANY if i in in_any else VMEM for i in range(count)],
        out_specs=VMEM,
        scratch_shapes=list(scratch),
        compiler_params=params,
        cost_estimate=pl.CostEstimate(flops=int(flops), bytes_accessed=int(nbytes), transcendentals=0),
    )


def local(
    tokens,
    modulation,
    qkv_spatial,
    bias_spatial,
    out_spatial,
    outbias_spatial,
    qkv_temporal,
    bias_temporal,
    out_temporal,
    outbias_temporal,
):
    patches, frames, width = tokens.shape
    spaces, times = lax.axis_size("space"), lax.axis_size("tm")
    space = lax.axis_index("space")
    heads = qkv_spatial.shape[1] // (3 * HD)
    cols = heads * HD
    half = heads // 2
    size = patches // times
    rows = patches * frames

    def across(array, k):
        return lax.ppermute(array, "space", [(i, (i + k) % spaces) for i in range(spaces)])

    def beside(array):
        return lax.ppermute(array, "tm", [(i, i ^ 1) for i in range(times)])

    arrived = [across(tokens, k) for k in range(1, spaces)]

    w_spatial = qkv_spatial.T.reshape(heads, 3 * HD, width)
    w_temporal = qkv_temporal.T.reshape(heads, 3 * HD, width)
    own, my_heads, my_out = pl.pallas_call(
        kernel_qkv,
        out_shape=tuple(
            jax.ShapeDtypeStruct(a, BF)
            for a in ((heads, 3, HD, rows), (half, 3 * HD, width), (half * HD, width))
        ),
        in_specs=[VMEM] + [ANY] * 3 + [VMEM] * 2,
        out_specs=(VMEM, VMEM, VMEM),
        scratch_shapes=[pltpu.VMEM(w_spatial.shape, BF), pltpu.SemaphoreType.DMA((3,))],
        compiler_params=PARAMS,
        cost_estimate=pl.CostEstimate(
            flops=2 * rows * width * cols * 3, bytes_accessed=3 * 10**6, transcendentals=0
        ),
    )(tokens, w_spatial, w_temporal, out_spatial, modulation, bias_spatial)

    spread = lax.all_to_all(tokens.reshape(times, size, frames, width), "tm", 0, 0, tiled=True)

    other_bias = [across(bias_temporal, k) for k in range(1, spaces)]
    (my_out,) = after((my_out,), own)
    arrived = [after((a,), own)[0] for a in arrived]
    direct_out = [across(my_out, k) for k in range(1, spaces)]

    o_all = call(
        kernel_spatial,
        (spaces, rows, cols),
        4 + len(arrived),
        1e10,
        4e6,
        [
            pltpu.VMEM((spaces - 1, heads, 3, HD, rows), BF),
            pltpu.VMEM(own.shape, BF),
            pltpu.VMEM(w_spatial.shape, BF),
            pltpu.SemaphoreType.DMA((heads + 1,)),
        ],
        (0, 1),
        params=LARGE,
    )(own, w_spatial, modulation, bias_spatial, *arrived)

    (my_heads,) = after((my_heads,), o_all, *direct_out)
    direct_heads = [across(my_heads, k) for k in range(1, spaces)]
    out_pieces = [out_spatial]
    for a in direct_out:
        out_pieces += [a, beside(after((a,), o_all)[0])]

    o_here = lax.all_to_all(
        after((o_all,), spread, *out_pieces)[0].reshape(spaces * times, frames * size, cols), ("space", "tm"), 0, 0, tiled=True
    ).reshape(spaces, rows, cols)
    other_heads = []
    for a in direct_heads:
        other_heads += [a, beside(after((a,), o_here)[0])]

    o_home = [
        across(lax.dynamic_index_in_dim(o_all, (space + k) % spaces, 0, keepdims=False), k)
        for k in range(1, spaces)
    ]

    y_home = call(
        kernel_home,
        (rows, width),
        4 + len(o_home) + len(out_pieces),
        2 * rows * width * cols * spaces,
        3e6,
        params=SMALL,
    )(o_all, tokens, outbias_spatial, modulation, *o_home, *out_pieces)
    x_here = spread.reshape(rows // frames, frames, width)
    h_here = call(
        kernel_between, (rows, width), 4 + len(out_pieces), 2 * rows * width * cols * spaces, 3e6, params=SMALL
    )(o_here, x_here, outbias_spatial, modulation, *out_pieces)
    o_own = pl.pallas_call(
        functools.partial(kernel_own, size=size, frames=frames),
        out_shape=jax.ShapeDtypeStruct((heads, HD, rows), F32),
        in_specs=[VMEM] * 3,
        out_specs=VMEM,
        compiler_params=SMALL,
        cost_estimate=pl.CostEstimate(
            flops=2 * rows * width * cols * 3, bytes_accessed=3 * 10**6, transcendentals=0
        ),
    )(h_here, w_temporal, bias_temporal)
    o_t = call(
        functools.partial(kernel_rest, size=size, frames=frames, spaces=spaces),
        (rows, spaces * cols),
        1 + spaces + len(other_heads),
        2 * rows * width * cols * 3 * (spaces - 1),
        5e6,
        [
            pltpu.VMEM((spaces * heads, HD, rows), F32),
        ],
        params=SMALL,
    )(h_here, o_own, *other_bias, *other_heads)
    o_t = o_t.reshape(times, frames * size, spaces * cols)
    o_final = lax.all_to_all(o_t, "tm", 0, 0, tiled=True).reshape(rows, spaces * cols)

    return call(
        kernel_final, (patches, frames, width), 5, 2 * rows * width * cols * spaces, 3e6, params=SMALL
    )(o_final, y_home, out_temporal, outbias_temporal, modulation)


def solution(mesh):
    return jax.shard_map(
        local,
        mesh=mesh,
        in_specs=(
            P("space", ("grp", "tm"), None),
            P("grp", None),
            P(None, "space"),
            P("space"),
            P("space", None),
            P(),
            P(None, "space"),
            P("space"),
            P(),
            P(),
        ),
        out_specs=P("space", ("grp", "tm"), None),
        check_vma=False,
    )
```

```python
import functools
import math

import jax
import jax.numpy as jnp
from jax import lax
from jax.experimental import pallas as pl
from jax.experimental.pallas import tpu as pltpu
from jax.sharding import PartitionSpec as P

HD = 72
WIN = 16
BF = jnp.bfloat16
F32 = jnp.float32
EXP2_SCALE = 1.0 / (math.sqrt(HD) * math.log(2.0))

VMEM = pl.BlockSpec(memory_space=pltpu.VMEM)
ANY = pl.BlockSpec(memory_space=pl.ANY)
LARGE = pltpu.CompilerParams(vmem_limit_bytes=62 * 1024 * 1024)
SMALL = pltpu.CompilerParams(vmem_limit_bytes=16 * 1024 * 1024)
PARAMS = pltpu.CompilerParams(vmem_limit_bytes=63 * 1024 * 1024)

NT = (((1,), (1,)), ((), ()))
TN = (((0,), (0,)), ((), ()))


def mm(a, b, dims=(((1,), (0,)), ((), ()))):
    return lax.dot_general(a, b, dims, preferred_element_type=F32)


def modulated(values, offset_vec, scaling):
    center = jnp.mean(values, axis=-1, keepdims=True)
    moved = values - center
    spread = jnp.mean(moved * moved, axis=-1, keepdims=True)
    return moved * lax.rsqrt(spread + 1e-06) * (1.0 + scaling) + offset_vec


def attend(q_t, k_t, v_t, mask=None):
    scores = mm(k_t, q_t, TN)
    if mask is not None:
        scores = jnp.where(mask, scores, F32(-1e30))
    highest = jnp.max(scores, axis=0, keepdims=True)
    expon = jnp.exp2((scores - highest) * F32(EXP2_SCALE))
    total = jnp.sum(expon, axis=0, keepdims=True)
    return mm(v_t, expon.astype(BF)) * (1.0 / total)


def after(arrays, *others):
    return lax.optimization_barrier((*arrays, *others))[: len(arrays)]


def flat(ref, *index):
    block = ref[index] if index else ref[...]
    return block.reshape(-1, block.shape[-1])


def column(rows):
    return lax.broadcasted_iota(jnp.int32, (rows, 1), 0)


def line(rows):
    return lax.broadcasted_iota(jnp.int32, (1, rows), 1)


def chosen(source, rows):
    return (source == line(rows)).astype(F32).astype(BF)


def by_frame_first(rows, frames):
    r = column(rows)
    return chosen(lax.rem(r, rows // frames) * frames + lax.div(r, rows // frames), rows)


def by_patch_first(rows, frames):
    r = column(rows)
    return chosen(lax.rem(r, frames) * (rows // frames) + lax.div(r, frames), rows)


def bias_column(b_ref):
    count = b_ref.shape[0]
    return jnp.broadcast_to(b_ref[...].reshape(1, count), (8, count)).T[:, 0:1]


def spatial_rows(x, mod_ref, frames):
    h = modulated(x.astype(F32), mod_ref[0:1, :], mod_ref[1:2, :]).astype(BF)
    return mm(by_frame_first(x.shape[0], frames), h).astype(BF)


def fetch(sources, targets, sems):
    copies = [pltpu.make_async_copy(a, b, sems.at[i]) for i, (a, b) in enumerate(zip(sources, targets))]
    for copy in copies:
        copy.start()
    return copies


def coordinates():
    return lax.axis_index("space"), lax.rem(lax.axis_index("tm"), 2)


def kernel_qkv(x_ref, w_hbm, w_other_hbm, out_w_hbm, mod_ref, b_ref, out_ref, heads_ref, half_ref, w_ref, sems):
    _, core = coordinates()
    half, rows = heads_ref.shape[0], half_ref.shape[0]
    copies = fetch(
        (
            w_hbm,
            out_w_hbm.at[pl.ds(pl.multiple_of(core * rows, rows), rows)],
            w_other_hbm.at[pl.ds(core * half, half)],
        ),
        (w_ref, half_ref, heads_ref),
        sems,
    )
    h = spatial_rows(flat(x_ref), mod_ref, x_ref.shape[1])
    bias = bias_column(b_ref)
    copies[0].wait()
    for i in range(w_ref.shape[0]):
        qkv = mm(w_ref[i], h, NT) + bias[i * 3 * HD : (i + 1) * 3 * HD]
        for c in range(3):
            out_ref[i, c] = qkv[c * HD : (c + 1) * HD].astype(BF)
    for copy in copies[1:]:
        copy.wait()


def kernel_spatial(own_hbm, w_hbm, mod_ref, b_ref, *refs):
    x_refs, (out_ref, part_ref, own_ref, w_ref, sems) = refs[:-5], refs[-5:]
    heads = w_ref.shape[0]
    copies = fetch(
        (*[w_hbm.at[i] for i in range(heads)], own_hbm),
        (*[w_ref.at[i] for i in range(heads)], own_ref),
        sems,
    )
    space, _ = coordinates()
    patches, frames, _ = x_refs[0].shape
    spaces = len(x_refs) + 1
    bias = bias_column(b_ref)
    rows = [spatial_rows(flat(x_ref), mod_ref, frames) for x_ref in x_refs]
    for i in range(heads):
        copies[i].wait()
        for j in range(spaces - 1):
            qkv = mm(w_ref[i], rows[j], NT) + bias[i * 3 * HD : (i + 1) * 3 * HD]
            for c in range(3):
                part_ref[j, i, c] = qkv[c * HD : (c + 1) * HD].astype(BF)
    copies[heads].wait()
    by_frame = []
    for f in range(frames):
        cols = slice(f * patches, (f + 1) * patches)
        done = []
        for i in range(heads):
            q_t, k_t, v_t = (
                jnp.concatenate(
                    [own_ref[i, c, :, cols]] + [part_ref[j, i, c, :, cols] for j in range(spaces - 1)],
                    axis=1,
                )
                for c in range(3)
            )
            done.append(attend(q_t, k_t, v_t))
        by_frame.append(jnp.concatenate(done, axis=0).astype(BF))
    back = by_patch_first(patches * frames, frames)
    for j in range(spaces):
        mine = jnp.concatenate([o[:, j * patches : (j + 1) * patches] for o in by_frame], axis=1)
        out_ref[lax.rem(space - j + spaces, spaces)] = mm(back, mine, NT).astype(BF)


def middle(tokens, parts, outbias, gate):
    summed = parts[0].astype(BF).astype(F32)
    for part in parts[1:]:
        summed = summed + part.astype(BF).astype(F32)
    return (tokens.astype(F32) + gate * (summed + outbias)).astype(BF)


def temporal_mask(rows, size, frames):
    def place(row):
        device, within = lax.div(row, frames * size), lax.rem(row, frames * size)
        return device * frames + lax.rem(within, frames), lax.div(within, frames)

    key_frame, key_patch = place(column(rows))
    query_frame, query_patch = place(line(rows))
    code_key = key_patch * 4 * WIN * rows + key_frame
    code_query = query_patch * 4 * WIN * rows + query_frame
    back = code_query - code_key
    return (back >= 0) & (back < WIN)


def temporal_head(w, b, h, mask):
    qkv = (mm(w, h, NT) + b).astype(BF)
    return attend(qkv[0:HD], qkv[HD : 2 * HD], qkv[2 * HD : 3 * HD], mask)


def parts_of(o, pieces, core):
    half = pieces[1].shape[0]
    parts = [mm(o(0), pieces[0][...])]
    for k in range(1, (len(pieces) + 1) // 2):
        first, second = pieces[2 * k - 1][...], pieces[2 * k][...]
        rows = jnp.concatenate([jnp.where(core == 0, first, second), jnp.where(core == 0, second, first)])
        parts.append(mm(o(k), rows))
    return parts


def kernel_between(o_ref, x_ref, outbias_ref, mod_ref, *refs):
    space, core = coordinates()
    pieces, h_ref = refs[:-1], refs[-1]
    spaces = o_ref.shape[0]
    parts = parts_of(lambda k: o_ref[lax.rem(space - k + spaces, spaces)], pieces, core)
    y = middle(flat(x_ref), parts, outbias_ref[...].reshape(1, -1), mod_ref[2:3, :])
    h_ref[...] = modulated(y.astype(F32), mod_ref[3:4, :], mod_ref[4:5, :]).astype(BF)


def kernel_own(h_ref, w_ref, b_ref, out_ref, *, size, frames):
    h = h_ref[...]
    mask = temporal_mask(h.shape[0], size, frames)
    bias = bias_column(b_ref)
    for i in range(w_ref.shape[0]):
        out_ref[i] = temporal_head(w_ref[i], bias[i * 3 * HD : (i + 1) * 3 * HD], h, mask)


def kernel_rest(h_ref, own_ref, *refs, size, frames, spaces):
    b_refs, w_refs, (out_ref, turn_ref) = refs[: spaces - 1], refs[spaces - 1 : -2], refs[-2:]
    space, core = coordinates()
    h = h_ref[...]
    rows = h.shape[0]
    mask = temporal_mask(rows, size, frames)
    heads = own_ref.shape[0]
    half = heads // 2
    for i in range(heads):
        turn_ref[space * heads + i] = own_ref[i]
    for n, w_ref in enumerate(w_refs):
        shift = n // 2 + 1
        bias = bias_column(b_refs[shift - 1])
        second = (core == 0) == (n % 2 == 1)
        within = jnp.where(second, half, 0)
        group = lax.rem(space - shift + spaces, spaces)
        bias = jnp.where(second, bias[half * 3 * HD :], bias[: half * 3 * HD])
        for i in range(half):
            o_t = temporal_head(w_ref[i], bias[i * 3 * HD : (i + 1) * 3 * HD], h, mask)
            turn_ref[group * heads + within + i] = o_t
    out_ref[...] = turn_ref[...].reshape(-1, rows).T.astype(BF)


def kernel_home(o_own_ref, x_ref, outbias_ref, mod_ref, *refs):
    space, core = coordinates()
    spaces = o_own_ref.shape[0]
    o_refs, pieces, out_ref = refs[: spaces - 1], refs[spaces - 1 : -1], refs[-1]
    parts = parts_of(lambda k: o_refs[k - 1][...] if k else o_own_ref[space], pieces, core)
    out_ref[...] = middle(flat(x_ref), parts, outbias_ref[...].reshape(1, -1), mod_ref[2:3, :])


def kernel_final(o_ref, y_ref, w_ref, outbias_ref, mod_ref, out_ref):
    final = mm(o_ref[...], w_ref[...]) + outbias_ref[...].reshape(1, -1)
    result = (y_ref[...].astype(F32) + mod_ref[5:6, :] * final).astype(BF)
    out_ref[...] = result.reshape(out_ref.shape)


def call(kernel, out_shape, count, flops, nbytes, scratch=(), in_any=(), params=PARAMS):
    return pl.pallas_call(
        kernel,
        out_shape=jax.ShapeDtypeStruct(out_shape, BF),
        in_specs=[ANY if i in in_any else VMEM for i in range(count)],
        out_specs=VMEM,
        scratch_shapes=list(scratch),
        compiler_params=params,
        cost_estimate=pl.CostEstimate(flops=int(flops), bytes_accessed=int(nbytes), transcendentals=0),
    )


def local(
    tokens,
    modulation,
    qkv_spatial,
    bias_spatial,
    out_spatial,
    outbias_spatial,
    qkv_temporal,
    bias_temporal,
    out_temporal,
    outbias_temporal,
):
    patches, frames, width = tokens.shape
    spaces, times = lax.axis_size("space"), lax.axis_size("tm")
    space = lax.axis_index("space")
    heads = qkv_spatial.shape[1] // (3 * HD)
    cols = heads * HD
    half = heads // 2
    size = patches // times
    rows = patches * frames

    def across(array, k):
        return lax.ppermute(array, "space", [(i, (i + k) % spaces) for i in range(spaces)])

    def beside(array):
        return lax.ppermute(array, "tm", [(i, i ^ 1) for i in range(times)])

    arrived = [across(tokens, k) for k in range(1, spaces)]

    w_spatial = qkv_spatial.T.reshape(heads, 3 * HD, width)
    w_temporal = qkv_temporal.T.reshape(heads, 3 * HD, width)
    own, my_heads, my_out = pl.pallas_call(
        kernel_qkv,
        out_shape=tuple(
            jax.ShapeDtypeStruct(a, BF)
            for a in ((heads, 3, HD, rows), (half, 3 * HD, width), (half * HD, width))
        ),
        in_specs=[VMEM] + [ANY] * 3 + [VMEM] * 2,
        out_specs=(VMEM, VMEM, VMEM),
        scratch_shapes=[pltpu.VMEM(w_spatial.shape, BF), pltpu.SemaphoreType.DMA((3,))],
        compiler_params=PARAMS,
        cost_estimate=pl.CostEstimate(
            flops=2 * rows * width * cols * 3, bytes_accessed=3 * 10**6, transcendentals=0
        ),
    )(tokens, w_spatial, w_temporal, out_spatial, modulation, bias_spatial)

    spread = lax.all_to_all(tokens.reshape(times, size, frames, width), "tm", 0, 0, tiled=True)

    other_bias = [across(bias_temporal, k) for k in range(1, spaces)]
    (my_out,) = after((my_out,), own)
    arrived = [after((a,), own, *other_bias)[0] for a in arrived]
    direct_out = [across(my_out, k) for k in range(1, spaces)]

    o_all = call(
        kernel_spatial,
        (spaces, rows, cols),
        4 + len(arrived),
        1e10,
        4e6,
        [
            pltpu.VMEM((spaces - 1, heads, 3, HD, rows), BF),
            pltpu.VMEM(own.shape, BF),
            pltpu.VMEM(w_spatial.shape, BF),
            pltpu.SemaphoreType.DMA((heads + 1,)),
        ],
        (0, 1),
        params=LARGE,
    )(own, w_spatial, modulation, bias_spatial, *arrived)

    (my_heads,) = after((my_heads,), o_all, *direct_out)
    direct_heads = [across(my_heads, k) for k in range(1, spaces)]
    out_pieces = [out_spatial]
    for a in direct_out:
        out_pieces += [a, beside(after((a,), o_all)[0])]

    o_here = lax.all_to_all(
        after((o_all,), spread, *out_pieces)[0].reshape(spaces * times, frames * size, cols), ("space", "tm"), 0, 0, tiled=True
    ).reshape(spaces, rows, cols)
    other_heads = []
    for a in direct_heads:
        other_heads += [a, beside(after((a,), o_here)[0])]

    o_home = [
        across(lax.dynamic_index_in_dim(o_all, (space + k) % spaces, 0, keepdims=False), k)
        for k in range(1, spaces)
    ]

    y_home = call(
        kernel_home,
        (rows, width),
        4 + len(o_home) + len(out_pieces),
        2 * rows * width * cols * spaces,
        3e6,
        params=SMALL,
    )(o_all, tokens, outbias_spatial, modulation, *o_home, *out_pieces)
    x_here = spread.reshape(rows // frames, frames, width)
    h_here = call(
        kernel_between, (rows, width), 4 + len(out_pieces), 2 * rows * width * cols * spaces, 3e6, params=SMALL
    )(o_here, x_here, outbias_spatial, modulation, *out_pieces)
    o_own = pl.pallas_call(
        functools.partial(kernel_own, size=size, frames=frames),
        out_shape=jax.ShapeDtypeStruct((heads, HD, rows), F32),
        in_specs=[VMEM] * 3,
        out_specs=VMEM,
        compiler_params=SMALL,
        cost_estimate=pl.CostEstimate(
            flops=2 * rows * width * cols * 3, bytes_accessed=3 * 10**6, transcendentals=0
        ),
    )(h_here, w_temporal, bias_temporal)
    o_t = call(
        functools.partial(kernel_rest, size=size, frames=frames, spaces=spaces),
        (rows, spaces * cols),
        1 + spaces + len(other_heads),
        2 * rows * width * cols * 3 * (spaces - 1),
        5e6,
        [
            pltpu.VMEM((spaces * heads, HD, rows), F32),
        ],
        params=SMALL,
    )(h_here, o_own, *other_bias, *other_heads)
    o_t = o_t.reshape(times, frames * size, spaces * cols)
    o_final = lax.all_to_all(o_t, "tm", 0, 0, tiled=True).reshape(rows, spaces * cols)

    return call(
        kernel_final, (patches, frames, width), 5, 2 * rows * width * cols * spaces, 3e6, params=SMALL
    )(o_final, y_home, out_temporal, outbias_temporal, modulation)


def solution(mesh):
    return jax.shard_map(
        local,
        mesh=mesh,
        in_specs=(
            P("space", ("grp", "tm"), None),
            P("grp", None),
            P(None, "space"),
            P("space"),
            P("space", None),
            P(),
            P(None, "space"),
            P("space"),
            P(),
            P(),
        ),
        out_specs=P("space", ("grp", "tm"), None),
        check_vma=False,
    )
```

```python
import functools
import math

import jax
import jax.numpy as jnp
from jax import lax
from jax.experimental import pallas as pl
from jax.experimental.pallas import tpu as pltpu
from jax.sharding import PartitionSpec as P

HD = 72
WIN = 16
BF = jnp.bfloat16
F32 = jnp.float32
EXP2_SCALE = 1.0 / (math.sqrt(HD) * math.log(2.0))

VMEM = pl.BlockSpec(memory_space=pltpu.VMEM)
ANY = pl.BlockSpec(memory_space=pl.ANY)
LARGE = pltpu.CompilerParams(vmem_limit_bytes=62 * 1024 * 1024)
SMALL = pltpu.CompilerParams(vmem_limit_bytes=16 * 1024 * 1024)
PARAMS = pltpu.CompilerParams(vmem_limit_bytes=63 * 1024 * 1024)

NT = (((1,), (1,)), ((), ()))
TN = (((0,), (0,)), ((), ()))


def mm(a, b, dims=(((1,), (0,)), ((), ()))):
    return lax.dot_general(a, b, dims, preferred_element_type=F32)


def modulated(values, offset_vec, scaling):
    center = jnp.mean(values, axis=-1, keepdims=True)
    moved = values - center
    spread = jnp.mean(moved * moved, axis=-1, keepdims=True)
    return moved * lax.rsqrt(spread + 1e-06) * (1.0 + scaling) + offset_vec


def attend(q_t, k_t, v_t, mask=None):
    scores = mm(k_t, q_t, TN)
    if mask is not None:
        scores = jnp.where(mask, scores, F32(-1e30))
    highest = jnp.max(scores, axis=0, keepdims=True)
    expon = jnp.exp2((scores - highest) * F32(EXP2_SCALE))
    total = jnp.sum(expon, axis=0, keepdims=True)
    return mm(v_t, expon.astype(BF)) * (1.0 / total)


def after(arrays, *others):
    return lax.optimization_barrier((*arrays, *others))[: len(arrays)]


def flat(ref, *index):
    block = ref[index] if index else ref[...]
    return block.reshape(-1, block.shape[-1])


def column(rows):
    return lax.broadcasted_iota(jnp.int32, (rows, 1), 0)


def line(rows):
    return lax.broadcasted_iota(jnp.int32, (1, rows), 1)


def chosen(source, rows):
    return (source == line(rows)).astype(F32).astype(BF)


def by_frame_first(rows, frames):
    r = column(rows)
    return chosen(lax.rem(r, rows // frames) * frames + lax.div(r, rows // frames), rows)


def by_patch_first(rows, frames):
    r = column(rows)
    return chosen(lax.rem(r, frames) * (rows // frames) + lax.div(r, frames), rows)


def bias_column(b_ref):
    count = b_ref.shape[0]
    return jnp.broadcast_to(b_ref[...].reshape(1, count), (8, count)).T[:, 0:1]


def spatial_rows(x, mod_ref, frames):
    h = modulated(x.astype(F32), mod_ref[0:1, :], mod_ref[1:2, :]).astype(BF)
    return mm(by_frame_first(x.shape[0], frames), h).astype(BF)


def fetch(sources, targets, sems):
    copies = [pltpu.make_async_copy(a, b, sems.at[i]) for i, (a, b) in enumerate(zip(sources, targets))]
    for copy in copies:
        copy.start()
    return copies


def coordinates():
    return lax.axis_index("space"), lax.rem(lax.axis_index("tm"), 2)


def kernel_qkv(x_ref, w_hbm, w_other_hbm, out_w_hbm, mod_ref, b_ref, out_ref, heads_ref, half_ref, w_ref, sems):
    _, core = coordinates()
    half, rows = heads_ref.shape[0], half_ref.shape[0]
    copies = fetch(
        (
            w_hbm,
            out_w_hbm.at[pl.ds(pl.multiple_of(core * rows, rows), rows)],
            w_other_hbm.at[pl.ds(core * half, half)],
        ),
        (w_ref, half_ref, heads_ref),
        sems,
    )
    h = spatial_rows(flat(x_ref), mod_ref, x_ref.shape[1])
    bias = bias_column(b_ref)
    copies[0].wait()
    for i in range(w_ref.shape[0]):
        qkv = mm(w_ref[i], h, NT) + bias[i * 3 * HD : (i + 1) * 3 * HD]
        for c in range(3):
            out_ref[i, c] = qkv[c * HD : (c + 1) * HD].astype(BF)
    for copy in copies[1:]:
        copy.wait()


def kernel_spatial(own_hbm, w_hbm, mod_ref, b_ref, *refs):
    x_refs, (out_ref, part_ref, own_ref, w_ref, sems) = refs[:-5], refs[-5:]
    heads = w_ref.shape[0]
    copies = fetch(
        (*[w_hbm.at[i] for i in range(heads)], own_hbm),
        (*[w_ref.at[i] for i in range(heads)], own_ref),
        sems,
    )
    space, _ = coordinates()
    patches, frames, _ = x_refs[0].shape
    spaces = len(x_refs) + 1
    bias = bias_column(b_ref)
    rows = [spatial_rows(flat(x_ref), mod_ref, frames) for x_ref in x_refs]
    for i in range(heads):
        copies[i].wait()
        for j in range(spaces - 1):
            qkv = mm(w_ref[i], rows[j], NT) + bias[i * 3 * HD : (i + 1) * 3 * HD]
            for c in range(3):
                part_ref[j, i, c] = qkv[c * HD : (c + 1) * HD].astype(BF)
    copies[heads].wait()
    by_frame = []
    for f in range(frames):
        cols = slice(f * patches, (f + 1) * patches)
        done = []
        for i in range(heads):
            q_t, k_t, v_t = (
                jnp.concatenate(
                    [own_ref[i, c, :, cols]] + [part_ref[j, i, c, :, cols] for j in range(spaces - 1)],
                    axis=1,
                )
                for c in range(3)
            )
            done.append(attend(q_t, k_t, v_t))
        by_frame.append(jnp.concatenate(done, axis=0).astype(BF))
    back = by_patch_first(patches * frames, frames)
    for j in range(spaces):
        mine = jnp.concatenate([o[:, j * patches : (j + 1) * patches] for o in by_frame], axis=1)
        out_ref[lax.rem(space - j + spaces, spaces)] = mm(back, mine, NT).astype(BF)


def middle(tokens, parts, outbias, gate):
    summed = parts[0].astype(BF).astype(F32)
    for part in parts[1:]:
        summed = summed + part.astype(BF).astype(F32)
    return (tokens.astype(F32) + gate * (summed + outbias)).astype(BF)


def temporal_mask(rows, size, frames):
    def place(row):
        device, within = lax.div(row, frames * size), lax.rem(row, frames * size)
        return device * frames + lax.rem(within, frames), lax.div(within, frames)

    key_frame, key_patch = place(column(rows))
    query_frame, query_patch = place(line(rows))
    code_key = key_patch * 4 * WIN * rows + key_frame
    code_query = query_patch * 4 * WIN * rows + query_frame
    back = code_query - code_key
    return (back >= 0) & (back < WIN)


def temporal_head(w, b, h, mask):
    qkv = (mm(w, h, NT) + b).astype(BF)
    return attend(qkv[0:HD], qkv[HD : 2 * HD], qkv[2 * HD : 3 * HD], mask)


def parts_of(o, pieces, core):
    half = pieces[1].shape[0]
    parts = [mm(o(0), pieces[0][...])]
    for k in range(1, (len(pieces) + 1) // 2):
        first, second = pieces[2 * k - 1][...], pieces[2 * k][...]
        rows = jnp.concatenate([jnp.where(core == 0, first, second), jnp.where(core == 0, second, first)])
        parts.append(mm(o(k), rows))
    return parts


def kernel_between(o_ref, x_ref, outbias_ref, mod_ref, *refs):
    space, core = coordinates()
    pieces, h_ref = refs[:-1], refs[-1]
    spaces = o_ref.shape[0]
    parts = parts_of(lambda k: o_ref[lax.rem(space - k + spaces, spaces)], pieces, core)
    y = middle(flat(x_ref), parts, outbias_ref[...].reshape(1, -1), mod_ref[2:3, :])
    h_ref[...] = modulated(y.astype(F32), mod_ref[3:4, :], mod_ref[4:5, :]).astype(BF)


def kernel_own(h_ref, w_ref, b_ref, out_ref, *, size, frames):
    h = h_ref[...]
    mask = temporal_mask(h.shape[0], size, frames)
    bias = bias_column(b_ref)
    for i in range(w_ref.shape[0]):
        out_ref[i] = temporal_head(w_ref[i], bias[i * 3 * HD : (i + 1) * 3 * HD], h, mask)


def kernel_rest(h_ref, own_ref, *refs, size, frames, spaces):
    b_refs, w_refs, (out_ref, turn_ref) = refs[: spaces - 1], refs[spaces - 1 : -2], refs[-2:]
    space, core = coordinates()
    h = h_ref[...]
    rows = h.shape[0]
    mask = temporal_mask(rows, size, frames)
    heads = own_ref.shape[0]
    half = heads // 2
    for i in range(heads):
        turn_ref[space * heads + i] = own_ref[i]
    for n, w_ref in enumerate(w_refs):
        shift = n // 2 + 1
        bias = bias_column(b_refs[shift - 1])
        second = (core == 0) == (n % 2 == 1)
        within = jnp.where(second, half, 0)
        group = lax.rem(space - shift + spaces, spaces)
        bias = jnp.where(second, bias[half * 3 * HD :], bias[: half * 3 * HD])
        for i in range(half):
            o_t = temporal_head(w_ref[i], bias[i * 3 * HD : (i + 1) * 3 * HD], h, mask)
            turn_ref[group * heads + within + i] = o_t
    out_ref[...] = turn_ref[...].reshape(-1, rows).T.astype(BF)


def kernel_home(o_own_ref, x_ref, outbias_ref, mod_ref, *refs):
    space, core = coordinates()
    spaces = o_own_ref.shape[0]
    o_refs, pieces, out_ref = refs[: spaces - 1], refs[spaces - 1 : -1], refs[-1]
    parts = parts_of(lambda k: o_refs[k - 1][...] if k else o_own_ref[space], pieces, core)
    out_ref[...] = middle(flat(x_ref), parts, outbias_ref[...].reshape(1, -1), mod_ref[2:3, :])


def kernel_final(o_ref, y_ref, w_ref, outbias_ref, mod_ref, out_ref):
    final = mm(o_ref[...], w_ref[...]) + outbias_ref[...].reshape(1, -1)
    result = (y_ref[...].astype(F32) + mod_ref[5:6, :] * final).astype(BF)
    out_ref[...] = result.reshape(out_ref.shape)


def call(kernel, out_shape, count, flops, nbytes, scratch=(), in_any=(), params=PARAMS):
    return pl.pallas_call(
        kernel,
        out_shape=jax.ShapeDtypeStruct(out_shape, BF),
        in_specs=[ANY if i in in_any else VMEM for i in range(count)],
        out_specs=VMEM,
        scratch_shapes=list(scratch),
        compiler_params=params,
        cost_estimate=pl.CostEstimate(flops=int(flops), bytes_accessed=int(nbytes), transcendentals=0),
    )


def local(
    tokens,
    modulation,
    qkv_spatial,
    bias_spatial,
    out_spatial,
    outbias_spatial,
    qkv_temporal,
    bias_temporal,
    out_temporal,
    outbias_temporal,
):
    patches, frames, width = tokens.shape
    spaces, times = lax.axis_size("space"), lax.axis_size("tm")
    space = lax.axis_index("space")
    heads = qkv_spatial.shape[1] // (3 * HD)
    cols = heads * HD
    half = heads // 2
    size = patches // times
    rows = patches * frames

    def across(array, k):
        return lax.ppermute(array, "space", [(i, (i + k) % spaces) for i in range(spaces)])

    def beside(array):
        return lax.ppermute(array, "tm", [(i, i ^ 1) for i in range(times)])

    arrived = [across(tokens, k) for k in range(1, spaces)]

    w_spatial = qkv_spatial.T.reshape(heads, 3 * HD, width)
    w_temporal = qkv_temporal.T.reshape(heads, 3 * HD, width)
    own, my_heads, my_out = pl.pallas_call(
        kernel_qkv,
        out_shape=tuple(
            jax.ShapeDtypeStruct(a, BF)
            for a in ((heads, 3, HD, rows), (half, 3 * HD, width), (half * HD, width))
        ),
        in_specs=[VMEM] + [ANY] * 3 + [VMEM] * 2,
        out_specs=(VMEM, VMEM, VMEM),
        scratch_shapes=[pltpu.VMEM(w_spatial.shape, BF), pltpu.SemaphoreType.DMA((3,))],
        compiler_params=PARAMS,
        cost_estimate=pl.CostEstimate(
            flops=2 * rows * width * cols * 3, bytes_accessed=3 * 10**6, transcendentals=0
        ),
    )(tokens, w_spatial, w_temporal, out_spatial, modulation, bias_spatial)

    spread = lax.all_to_all(tokens.reshape(times, size, frames, width), "tm", 0, 0, tiled=True)

    other_bias = [across(bias_temporal, k) for k in range(1, spaces)]
    (my_out,) = after((my_out,), own)
    arrived = [after((a,), own, *other_bias)[0] for a in arrived]
    direct_out = [across(my_out, k) for k in range(1, spaces)]

    o_all = call(
        kernel_spatial,
        (spaces, rows, cols),
        4 + len(arrived),
        1e10,
        4e6,
        [
            pltpu.VMEM((spaces - 1, heads, 3, HD, rows), BF),
            pltpu.VMEM(own.shape, BF),
            pltpu.VMEM(w_spatial.shape, BF),
            pltpu.SemaphoreType.DMA((heads + 1,)),
        ],
        (0, 1),
        params=LARGE,
    )(own, w_spatial, modulation, bias_spatial, *arrived)

    (my_heads,) = after((my_heads,), o_all, spread, *direct_out)
    direct_heads = [across(my_heads, k) for k in range(1, spaces)]
    out_pieces = [out_spatial]
    for a in direct_out:
        out_pieces += [a, beside(after((a,), o_all)[0])]

    o_here = lax.all_to_all(
        after((o_all,), spread, *out_pieces)[0].reshape(spaces * times, frames * size, cols), ("space", "tm"), 0, 0, tiled=True
    ).reshape(spaces, rows, cols)
    other_heads = []
    for a in direct_heads:
        other_heads += [a, beside(after((a,), o_here)[0])]

    o_home = [
        across(lax.dynamic_index_in_dim(o_all, (space + k) % spaces, 0, keepdims=False), k)
        for k in range(1, spaces)
    ]

    y_home = call(
        kernel_home,
        (rows, width),
        4 + len(o_home) + len(out_pieces),
        2 * rows * width * cols * spaces,
        3e6,
        params=SMALL,
    )(o_all, tokens, outbias_spatial, modulation, *o_home, *out_pieces)
    x_here = spread.reshape(rows // frames, frames, width)
    h_here = call(
        kernel_between, (rows, width), 4 + len(out_pieces), 2 * rows * width * cols * spaces, 3e6, params=SMALL
    )(o_here, x_here, outbias_spatial, modulation, *out_pieces)
    o_own = pl.pallas_call(
        functools.partial(kernel_own, size=size, frames=frames),
        out_shape=jax.ShapeDtypeStruct((heads, HD, rows), F32),
        in_specs=[VMEM] * 3,
        out_specs=VMEM,
        compiler_params=SMALL,
        cost_estimate=pl.CostEstimate(
            flops=2 * rows * width * cols * 3, bytes_accessed=3 * 10**6, transcendentals=0
        ),
    )(h_here, w_temporal, bias_temporal)
    o_t = call(
        functools.partial(kernel_rest, size=size, frames=frames, spaces=spaces),
        (rows, spaces * cols),
        1 + spaces + len(other_heads),
        2 * rows * width * cols * 3 * (spaces - 1),
        5e6,
        [
            pltpu.VMEM((spaces * heads, HD, rows), F32),
        ],
        params=SMALL,
    )(h_here, o_own, *other_bias, *other_heads)
    o_t = o_t.reshape(times, frames * size, spaces * cols)
    o_final = lax.all_to_all(o_t, "tm", 0, 0, tiled=True).reshape(rows, spaces * cols)

    return call(
        kernel_final, (patches, frames, width), 5, 2 * rows * width * cols * spaces, 3e6, params=SMALL
    )(o_final, y_home, out_temporal, outbias_temporal, modulation)


def solution(mesh):
    return jax.shard_map(
        local,
        mesh=mesh,
        in_specs=(
            P("space", ("grp", "tm"), None),
            P("grp", None),
            P(None, "space"),
            P("space"),
            P("space", None),
            P(),
            P(None, "space"),
            P("space"),
            P(),
            P(),
        ),
        out_specs=P("space", ("grp", "tm"), None),
        check_vma=False,
    )
```

```python
import functools
import math

import jax
import jax.numpy as jnp
from jax import lax
from jax.experimental import pallas as pl
from jax.experimental.pallas import tpu as pltpu
from jax.sharding import PartitionSpec as P

HD = 72
WIN = 16
BF = jnp.bfloat16
F32 = jnp.float32
EXP2_SCALE = 1.0 / (math.sqrt(HD) * math.log(2.0))

VMEM = pl.BlockSpec(memory_space=pltpu.VMEM)
ANY = pl.BlockSpec(memory_space=pl.ANY)
LARGE = pltpu.CompilerParams(vmem_limit_bytes=62 * 1024 * 1024)
SMALL = pltpu.CompilerParams(vmem_limit_bytes=16 * 1024 * 1024)
PARAMS = pltpu.CompilerParams(vmem_limit_bytes=63 * 1024 * 1024)

NT = (((1,), (1,)), ((), ()))
TN = (((0,), (0,)), ((), ()))


def mm(a, b, dims=(((1,), (0,)), ((), ()))):
    return lax.dot_general(a, b, dims, preferred_element_type=F32)


def modulated(values, offset_vec, scaling):
    center = jnp.mean(values, axis=-1, keepdims=True)
    moved = values - center
    spread = jnp.mean(moved * moved, axis=-1, keepdims=True)
    return moved * lax.rsqrt(spread + 1e-06) * (1.0 + scaling) + offset_vec


def attend(q_t, k_t, v_t, mask=None):
    scores = mm(k_t, q_t, TN)
    if mask is not None:
        scores = jnp.where(mask, scores, F32(-1e30))
    highest = jnp.max(scores, axis=0, keepdims=True)
    expon = jnp.exp2((scores - highest) * F32(EXP2_SCALE))
    total = jnp.sum(expon, axis=0, keepdims=True)
    return mm(v_t, expon.astype(BF)) * (1.0 / total)


def after(arrays, *others):
    return lax.optimization_barrier((*arrays, *others))[: len(arrays)]


def flat(ref, *index):
    block = ref[index] if index else ref[...]
    return block.reshape(-1, block.shape[-1])


def column(rows):
    return lax.broadcasted_iota(jnp.int32, (rows, 1), 0)


def line(rows):
    return lax.broadcasted_iota(jnp.int32, (1, rows), 1)


def chosen(source, rows):
    return (source == line(rows)).astype(F32).astype(BF)


def by_frame_first(rows, frames):
    r = column(rows)
    return chosen(lax.rem(r, rows // frames) * frames + lax.div(r, rows // frames), rows)


def by_patch_first(rows, frames):
    r = column(rows)
    return chosen(lax.rem(r, frames) * (rows // frames) + lax.div(r, frames), rows)


def bias_column(b_ref):
    count = b_ref.shape[0]
    return jnp.broadcast_to(b_ref[...].reshape(1, count), (8, count)).T[:, 0:1]


def spatial_rows(x, mod_ref, frames):
    h = modulated(x.astype(F32), mod_ref[0:1, :], mod_ref[1:2, :]).astype(BF)
    return mm(by_frame_first(x.shape[0], frames), h).astype(BF)


def fetch(sources, targets, sems):
    copies = [pltpu.make_async_copy(a, b, sems.at[i]) for i, (a, b) in enumerate(zip(sources, targets))]
    for copy in copies:
        copy.start()
    return copies


def coordinates():
    return lax.axis_index("space"), lax.rem(lax.axis_index("tm"), 2)


def kernel_qkv(x_ref, w_hbm, w_other_hbm, out_w_hbm, mod_ref, b_ref, out_ref, heads_ref, half_ref, w_ref, sems):
    _, core = coordinates()
    half, rows = heads_ref.shape[0], half_ref.shape[0]
    copies = fetch(
        (
            w_hbm,
            out_w_hbm.at[pl.ds(pl.multiple_of(core * rows, rows), rows)],
            w_other_hbm.at[pl.ds(core * half, half)],
        ),
        (w_ref, half_ref, heads_ref),
        sems,
    )
    h = spatial_rows(flat(x_ref), mod_ref, x_ref.shape[1])
    bias = bias_column(b_ref)
    copies[0].wait()
    for i in range(w_ref.shape[0]):
        qkv = mm(w_ref[i], h, NT) + bias[i * 3 * HD : (i + 1) * 3 * HD]
        for c in range(3):
            out_ref[i, c] = qkv[c * HD : (c + 1) * HD].astype(BF)
    for copy in copies[1:]:
        copy.wait()


def kernel_spatial(own_hbm, w_hbm, mod_ref, b_ref, *refs):
    x_refs, (out_ref, part_ref, own_ref, w_ref, sems) = refs[:-5], refs[-5:]
    heads = w_ref.shape[0]
    copies = fetch(
        (*[w_hbm.at[i] for i in range(heads)], own_hbm),
        (*[w_ref.at[i] for i in range(heads)], own_ref),
        sems,
    )
    space, _ = coordinates()
    patches, frames, _ = x_refs[0].shape
    spaces = len(x_refs) + 1
    bias = bias_column(b_ref)
    rows = [spatial_rows(flat(x_ref), mod_ref, frames) for x_ref in x_refs]
    for i in range(heads):
        copies[i].wait()
        for j in range(spaces - 1):
            qkv = mm(w_ref[i], rows[j], NT) + bias[i * 3 * HD : (i + 1) * 3 * HD]
            for c in range(3):
                part_ref[j, i, c] = qkv[c * HD : (c + 1) * HD].astype(BF)
    copies[heads].wait()
    by_frame = []
    for f in range(frames):
        cols = slice(f * patches, (f + 1) * patches)
        done = []
        for i in range(heads):
            q_t, k_t, v_t = (
                jnp.concatenate(
                    [own_ref[i, c, :, cols]] + [part_ref[j, i, c, :, cols] for j in range(spaces - 1)],
                    axis=1,
                )
                for c in range(3)
            )
            done.append(attend(q_t, k_t, v_t))
        by_frame.append(jnp.concatenate(done, axis=0).astype(BF))
    back = by_patch_first(patches * frames, frames)
    for j in range(spaces):
        mine = jnp.concatenate([o[:, j * patches : (j + 1) * patches] for o in by_frame], axis=1)
        out_ref[lax.rem(space - j + spaces, spaces)] = mm(back, mine, NT).astype(BF)


def middle(tokens, parts, outbias, gate):
    summed = parts[0].astype(BF).astype(F32)
    for part in parts[1:]:
        summed = summed + part.astype(BF).astype(F32)
    return (tokens.astype(F32) + gate * (summed + outbias)).astype(BF)


def temporal_mask(rows, size, frames):
    def place(row):
        device, within = lax.div(row, frames * size), lax.rem(row, frames * size)
        return device * frames + lax.rem(within, frames), lax.div(within, frames)

    key_frame, key_patch = place(column(rows))
    query_frame, query_patch = place(line(rows))
    code_key = key_patch * 4 * WIN * rows + key_frame
    code_query = query_patch * 4 * WIN * rows + query_frame
    back = code_query - code_key
    return (back >= 0) & (back < WIN)


def temporal_head(w, b, h, mask):
    qkv = (mm(w, h, NT) + b).astype(BF)
    return attend(qkv[0:HD], qkv[HD : 2 * HD], qkv[2 * HD : 3 * HD], mask)


def parts_of(o, pieces, core):
    half = pieces[1].shape[0]
    parts = [mm(o(0), pieces[0][...])]
    for k in range(1, (len(pieces) + 1) // 2):
        first, second = pieces[2 * k - 1][...], pieces[2 * k][...]
        rows = jnp.concatenate([jnp.where(core == 0, first, second), jnp.where(core == 0, second, first)])
        parts.append(mm(o(k), rows))
    return parts


def kernel_between(o_ref, x_ref, outbias_ref, mod_ref, *refs):
    space, core = coordinates()
    pieces, h_ref = refs[:-1], refs[-1]
    spaces = o_ref.shape[0]
    parts = parts_of(lambda k: o_ref[lax.rem(space - k + spaces, spaces)], pieces, core)
    y = middle(flat(x_ref), parts, outbias_ref[...].reshape(1, -1), mod_ref[2:3, :])
    h_ref[...] = modulated(y.astype(F32), mod_ref[3:4, :], mod_ref[4:5, :]).astype(BF)


def kernel_own(h_ref, w_ref, b_ref, out_ref, *, size, frames):
    h = h_ref[...]
    mask = temporal_mask(h.shape[0], size, frames)
    bias = bias_column(b_ref)
    for i in range(w_ref.shape[0]):
        out_ref[i] = temporal_head(w_ref[i], bias[i * 3 * HD : (i + 1) * 3 * HD], h, mask)


def kernel_rest(h_ref, own_ref, *refs, size, frames, spaces):
    b_refs, w_refs, (out_ref, turn_ref) = refs[: spaces - 1], refs[spaces - 1 : -2], refs[-2:]
    space, core = coordinates()
    h = h_ref[...]
    rows = h.shape[0]
    mask = temporal_mask(rows, size, frames)
    heads = own_ref.shape[0]
    half = heads // 2
    for i in range(heads):
        turn_ref[space * heads + i] = own_ref[i]
    for n, w_ref in enumerate(w_refs):
        shift = n // 2 + 1
        bias = bias_column(b_refs[shift - 1])
        second = (core == 0) == (n % 2 == 1)
        within = jnp.where(second, half, 0)
        group = lax.rem(space - shift + spaces, spaces)
        bias = jnp.where(second, bias[half * 3 * HD :], bias[: half * 3 * HD])
        for i in range(half):
            o_t = temporal_head(w_ref[i], bias[i * 3 * HD : (i + 1) * 3 * HD], h, mask)
            turn_ref[group * heads + within + i] = o_t
    out_ref[...] = turn_ref[...].reshape(-1, rows).T.astype(BF)


def kernel_home(o_own_ref, x_ref, outbias_ref, mod_ref, *refs):
    space, core = coordinates()
    spaces = o_own_ref.shape[0]
    o_refs, pieces, out_ref = refs[: spaces - 1], refs[spaces - 1 : -1], refs[-1]
    parts = parts_of(lambda k: o_refs[k - 1][...] if k else o_own_ref[space], pieces, core)
    out_ref[...] = middle(flat(x_ref), parts, outbias_ref[...].reshape(1, -1), mod_ref[2:3, :])


def kernel_final(o_ref, y_ref, w_ref, outbias_ref, mod_ref, out_ref):
    final = mm(o_ref[...], w_ref[...]) + outbias_ref[...].reshape(1, -1)
    result = (y_ref[...].astype(F32) + mod_ref[5:6, :] * final).astype(BF)
    out_ref[...] = result.reshape(out_ref.shape)


def call(kernel, out_shape, count, flops, nbytes, scratch=(), in_any=(), params=PARAMS):
    return pl.pallas_call(
        kernel,
        out_shape=jax.ShapeDtypeStruct(out_shape, BF),
        in_specs=[ANY if i in in_any else VMEM for i in range(count)],
        out_specs=VMEM,
        scratch_shapes=list(scratch),
        compiler_params=params,
        cost_estimate=pl.CostEstimate(flops=int(flops), bytes_accessed=int(nbytes), transcendentals=0),
    )


def local(
    tokens,
    modulation,
    qkv_spatial,
    bias_spatial,
    out_spatial,
    outbias_spatial,
    qkv_temporal,
    bias_temporal,
    out_temporal,
    outbias_temporal,
):
    patches, frames, width = tokens.shape
    spaces, times = lax.axis_size("space"), lax.axis_size("tm")
    space = lax.axis_index("space")
    heads = qkv_spatial.shape[1] // (3 * HD)
    cols = heads * HD
    half = heads // 2
    size = patches // times
    rows = patches * frames

    def across(array, k):
        return lax.ppermute(array, "space", [(i, (i + k) % spaces) for i in range(spaces)])

    def beside(array):
        return lax.ppermute(array, "tm", [(i, i ^ 1) for i in range(times)])

    arrived = [across(tokens, k) for k in range(1, spaces)]

    w_spatial = qkv_spatial.T.reshape(heads, 3 * HD, width)
    w_temporal = qkv_temporal.T.reshape(heads, 3 * HD, width)
    own, my_heads, my_out = pl.pallas_call(
        kernel_qkv,
        out_shape=tuple(
            jax.ShapeDtypeStruct(a, BF)
            for a in ((heads, 3, HD, rows), (half, 3 * HD, width), (half * HD, width))
        ),
        in_specs=[VMEM] + [ANY] * 3 + [VMEM] * 2,
        out_specs=(VMEM, VMEM, VMEM),
        scratch_shapes=[pltpu.VMEM(w_spatial.shape, BF), pltpu.SemaphoreType.DMA((3,))],
        compiler_params=PARAMS,
        cost_estimate=pl.CostEstimate(
            flops=2 * rows * width * cols * 3, bytes_accessed=3 * 10**6, transcendentals=0
        ),
    )(tokens, w_spatial, w_temporal, out_spatial, modulation, bias_spatial)

    spread = lax.all_to_all(tokens.reshape(times, size, frames, width), "tm", 0, 0, tiled=True)

    other_bias = [across(bias_temporal, k) for k in range(1, spaces)]
    (my_out,) = after((my_out,), own)
    arrived = [after((a,), own, *other_bias)[0] for a in arrived]
    direct_out = [across(my_out, k) for k in range(1, spaces)]

    o_all = call(
        kernel_spatial,
        (spaces, rows, cols),
        4 + len(arrived),
        1e10,
        4e6,
        [
            pltpu.VMEM((spaces - 1, heads, 3, HD, rows), BF),
            pltpu.VMEM(own.shape, BF),
            pltpu.VMEM(w_spatial.shape, BF),
            pltpu.SemaphoreType.DMA((heads + 1,)),
        ],
        (0, 1),
        params=LARGE,
    )(own, w_spatial, modulation, bias_spatial, *arrived)

    (my_heads,) = after((my_heads,), o_all, spread, *direct_out)
    direct_heads = [across(my_heads, k) for k in range(1, spaces)]
    out_pieces = [out_spatial]
    for a in direct_out:
        out_pieces += [a, beside(after((a,), o_all)[0])]

    o_here = lax.all_to_all(
        after((o_all,), spread, *out_pieces)[0].reshape(spaces * times, frames * size, cols), ("space", "tm"), 0, 0, tiled=True
    ).reshape(spaces, rows, cols)
    other_heads = []
    for a in direct_heads:
        other_heads += [a, beside(after((a,), o_here)[0])]

    o_home = [
        across(lax.dynamic_index_in_dim(o_all, (space + k) % spaces, 0, keepdims=False), k)
        for k in range(1, spaces)
    ]

    y_home = call(
        kernel_home,
        (rows, width),
        4 + len(o_home) + len(out_pieces),
        2 * rows * width * cols * spaces,
        3e6,
        params=SMALL,
    )(o_all, tokens, outbias_spatial, modulation, *o_home, *out_pieces)
    x_here = spread.reshape(rows // frames, frames, width)
    h_here = call(
        kernel_between, (rows, width), 4 + len(out_pieces), 2 * rows * width * cols * spaces, 3e6, params=SMALL
    )(o_here, x_here, outbias_spatial, modulation, *out_pieces)
    o_own = pl.pallas_call(
        functools.partial(kernel_own, size=size, frames=frames),
        out_shape=jax.ShapeDtypeStruct((heads, HD, rows), F32),
        in_specs=[VMEM] * 3,
        out_specs=VMEM,
        compiler_params=SMALL,
        cost_estimate=pl.CostEstimate(
            flops=2 * rows * width * cols * 3, bytes_accessed=3 * 10**6, transcendentals=0
        ),
    )(h_here, w_temporal, bias_temporal)
    o_t = call(
        functools.partial(kernel_rest, size=size, frames=frames, spaces=spaces),
        (rows, spaces * cols),
        1 + spaces + len(other_heads),
        2 * rows * width * cols * 3 * (spaces - 1),
        5e6,
        [
            pltpu.VMEM((spaces * heads, HD, rows), F32),
        ],
        params=SMALL,
    )(h_here, o_own, *other_bias, *other_heads)
    o_t = o_t.reshape(times, frames * size, spaces * cols)
    o_final = lax.all_to_all(o_t, "tm", 0, 0, tiled=True).reshape(rows, spaces * cols)

    return call(
        kernel_final, (patches, frames, width), 5, 2 * rows * width * cols * spaces, 3e6
    )(o_final, y_home, out_temporal, outbias_temporal, modulation)


def solution(mesh):
    return jax.shard_map(
        local,
        mesh=mesh,
        in_specs=(
            P("space", ("grp", "tm"), None),
            P("grp", None),
            P(None, "space"),
            P("space"),
            P("space", None),
            P(),
            P(None, "space"),
            P("space"),
            P(),
            P(),
        ),
        out_specs=P("space", ("grp", "tm"), None),
        check_vma=False,
    )
```
